256 devices in a mesh: tp: 32 (over y_hi, z, core), dp: 8 (over x, y_lo).
Axes of the slice: x: 4, y: 4 (y_hi: 2, y_lo: 2; y = y_hi * 2 + y_lo), z: 8, core: 2. Of those that a mesh axis runs over, the one named last changes fastest.
Arguments:
- teacher_hidden: bfloat16 [512, 16384], P('tp', 'dp'), may hold values from -6 to 6
- teacher_gain: bfloat16 [16384], P('dp'), may hold values from 0.5 to 1.5
- teacher_head: bfloat16 [16384, 65536], P('dp', 'tp'), as said below
- student_hidden: bfloat16 [512, 4096], P(('tp', 'dp')), may hold values from -6 to 6
- student_gain: bfloat16 [4096], replicated, may hold values from 0.5 to 1.5
- student_head: bfloat16 [4096, 65536], P(None, ('tp', 'dp')), as said below
- token_ids: int32 [512], replicated, may hold values from 0 to 65535
Outputs:
- token_loss: float32 [512], replicated
- grad_hidden: bfloat16 [512, 4096], P(('tp', 'dp'))
- grad_gain: float32 [4096], replicated
- grad_head: bfloat16 [4096, 65536], P(None, ('tp', 'dp'))
The draws below stay inside these ranges and needn't reach their ends.
Inputs may be any that keep to these rules, and one draw needn't show every extreme that they name: `teacher_head`: entries of order 3 / sqrt(16384); some columns may be much larger. `student_head`: entries of order 3 / sqrt(4096); some columns may be much larger.
All inputs are finite; a program needn't handle non-finite values.
Results may differ from the reference program's by a relative error of at most 0.011.
Values may be sent and summed in bfloat16 or wider, within the bound.
A program may use at most 128 MiB of HBM per device.

```python
import math
import jax
import jax.numpy as jnp
import numpy as np
from jax import lax

D_T = 16384
D_S = 4096
V = 65536
TOKENS = 512


def draw_teacher_head(key, part):
    key = jax.random.fold_in(key, 11)
    key_base = jax.random.fold_in(key, 0)
    spread = 3.0 / D_T ** 0.5
    base = jnp.clip(jax.random.normal(key_base, (D_T, V), jnp.float32), -6.0, 6.0) * spread
    return base.astype(jnp.bfloat16)


def draw_student_head(key, part):
    key = jax.random.fold_in(key, 23)
    key_base = jax.random.fold_in(key, 0)
    spread = 3.0 / D_S ** 0.5
    base = jnp.clip(jax.random.normal(key_base, (D_S, V), jnp.float32), -6.0, 6.0) * spread
    return base.astype(jnp.bfloat16)


def touch_ends(entries, own_key, least, largest):
    shape = entries.shape
    index_at = [jax.random.randint(jax.random.fold_in(own_key, axis), (), 0, shape[axis]) for axis in range(len(shape))]
    entries = entries.at[tuple(index_at)].set(least)
    longest = shape.index(max(shape))
    index_at[longest] = (index_at[longest] + 1) % shape[longest]
    return entries.at[tuple(index_at)].set(largest)


def level_of(own_key, dims, cuts, least, high):
    def one(axis_at, parts):
        draws = jax.random.uniform(jax.random.fold_in(jax.random.fold_in(own_key, 6), axis_at), (parts,), jnp.float32, least / len(cuts), high / len(cuts))
        return jnp.repeat(jnp.exp(draws), dims[axis_at] // parts).reshape((-1,) + (1,) * (len(dims) - axis_at - 1))

    gain = one(*cuts[0])
    for cut in cuts[1:]:
        gain = gain * one(*cut)
    return gain


def cumulative_ranks(number_of, slope):
    weights = [(1 << 20) // math.isqrt(grade ** slope) + 1 for grade in range(1, number_of + 1)]
    deviation = 1 + sum(weights) // (1 << 30)
    return np.cumsum(np.array([max(1, weight // deviation) for weight in weights]))


def skewed_ids(own_key, shape, number_of, slope):
    table = cumulative_ranks(number_of, slope)
    pick = jax.random.randint(jax.random.fold_in(own_key, 1), shape, 0, int(table[number_of - 1]))
    standing = jnp.searchsorted(jnp.asarray(table, jnp.int32), pick, side="right")
    return jax.random.permutation(jax.random.fold_in(own_key, 2), number_of)[standing].astype(jnp.int32)


def gaussian(stream_key, extent, scale, limit, pieces=(), kind=jnp.bfloat16):
    values = jax.random.normal(stream_key, extent, jnp.float32) * scale
    if len(pieces) > 0:
        values = level_of(stream_key, extent, pieces, -0.22, 0.18) * values
    return jnp.clip(values, min=-limit, max=limit).astype(kind)


def setup_inputs(seed: int = 0) -> dict:
    arg_keys = jax.random.split(jax.random.key(seed), 8)
    teacher_hidden = gaussian(arg_keys[0], (TOKENS, D_T), 1.0, 6.0, ((0, 32), (1, 8)))
    teacher_gain = jnp.clip(1.0 + 0.1 * jax.random.normal(arg_keys[1], (D_T,), jnp.float32), 0.5, 1.5).astype(jnp.bfloat16)
    teacher_head = draw_teacher_head(jax.random.fold_in(arg_keys[7], 71), 0)
    student_hidden = gaussian(arg_keys[3], (TOKENS, D_S), 1.0, 6.0, ((0, 256),))
    student_gain = jnp.clip(1.0 + 0.1 * jax.random.normal(arg_keys[4], (D_S,), jnp.float32), 0.5, 1.5).astype(jnp.bfloat16)
    student_head = draw_student_head(jax.random.fold_in(arg_keys[7], 71), 0)
    token_ids = touch_ends(skewed_ids(arg_keys[6], (TOKENS,), V, 2), jax.random.fold_in(arg_keys[6], 3), 0, V - 1).astype(jnp.int32)
    return {"teacher_hidden": teacher_hidden, "teacher_gain": teacher_gain, "teacher_head": teacher_head, "student_hidden": student_hidden, "student_gain": student_gain, "student_head": student_head, "token_ids": token_ids}


epsilon = 1e-05
hard_weight = 0.5
loss_scale = 64.0

def reference(teacher_hidden, teacher_gain, teacher_head, student_hidden, student_gain, student_head, token_ids):
    teacher_wide = teacher_hidden.astype(jnp.float32)
    teacher_inv = lax.rsqrt(lax.optimization_barrier(jnp.sum(teacher_wide * teacher_wide, -1)) / D_T + epsilon)
    teacher_scaled = (teacher_wide * teacher_gain.astype(jnp.float32)).astype(jnp.bfloat16)
    teacher_logits = jnp.dot(teacher_scaled, teacher_head, preferred_element_type=jnp.float32) * teacher_inv[:, None]
    student_wide = student_hidden.astype(jnp.float32)
    student_inv = lax.rsqrt(lax.optimization_barrier(jnp.sum(student_wide * student_wide, -1)) / D_S + epsilon)
    student_normed = student_wide * student_inv[:, None]
    student_features = (student_normed * student_gain.astype(jnp.float32)).astype(jnp.bfloat16)
    student_logits = jnp.dot(student_features, student_head, preferred_element_type=jnp.float32)
    teacher_top = lax.optimization_barrier(jnp.max(teacher_logits, -1))
    student_top = lax.optimization_barrier(jnp.max(student_logits, -1))
    teacher_exp = jnp.exp(teacher_logits - teacher_top[:, None])
    student_exp = jnp.exp(student_logits - student_top[:, None])
    teacher_total = lax.optimization_barrier(jnp.sum(teacher_exp, -1))
    student_total = lax.optimization_barrier(jnp.sum(student_exp, -1))
    cross_term = lax.optimization_barrier(jnp.sum(teacher_exp * (teacher_logits - student_logits), -1))
    vocab_index = jnp.arange(V, dtype=jnp.int32)
    target_mask = vocab_index[None, :] == token_ids[:, None]
    target = lax.optimization_barrier(jnp.sum(jnp.where(target_mask, student_logits, 0.0), -1))
    teacher_lse = teacher_top + jnp.log(teacher_total)
    student_lse = student_top + jnp.log(student_total)
    token_loss = cross_term / teacher_total - teacher_lse + student_lse + hard_weight * (student_lse - target)
    teacher_prob = jnp.exp(teacher_logits - teacher_lse[:, None])
    student_prob = jnp.exp(student_logits - student_lse[:, None])
    onehot = target_mask.astype(jnp.float32)
    grad_logits = (loss_scale * (student_prob - teacher_prob + hard_weight * (student_prob - onehot))).astype(jnp.bfloat16)
    grad_head = lax.dot_general(student_features, grad_logits, (((0,), (0,)), ((), ())), preferred_element_type=jnp.float32).astype(jnp.bfloat16)
    grad_features = lax.dot_general(grad_logits, student_head, (((1,), (1,)), ((), ())), preferred_element_type=jnp.float32)
    grad_gain = lax.optimization_barrier(jnp.sum(grad_features * student_normed, 0))
    grad_normed = grad_features * student_gain.astype(jnp.float32)
    inner = lax.optimization_barrier(jnp.sum(grad_normed * student_normed, -1)) / D_S
    grad_hidden = (student_inv[:, None] * (grad_normed - student_normed * inner[:, None])).astype(jnp.bfloat16)
    return (token_loss, grad_hidden, grad_gain, grad_head)
```

```python
import functools

import jax
import jax.numpy as jnp
from jax import lax
from jax.experimental import pallas as pl
from jax.experimental.pallas import tpu as pltpu
from jax.sharding import PartitionSpec as P

D_T = 16384
D_S = 4096
TOKENS = 512
SLICE = 256

epsilon = 1e-05
hard_weight = 0.5
loss_scale = 64.0

MESH = pl.DeviceIdType.MESH
f32 = jnp.float32
bf16 = jnp.bfloat16
NT = (((1,), (1,)), ((), ()))

CHUNK_ROWS = (64, 128, 128, 128, 64)
CHUNK_AT = (0, 64, 192, 320, 448)
ORDER = (0, 2, 1, 3)
WIDE = 1024


class Sems:
    def __init__(self):
        self.count = 0

    def take(self, n):
        at = self.count
        self.count += n
        return at


def layout():
    s = Sems()
    base = {}
    for name, n in (
        ("load", 3),
        ("t_yh", 1), ("t_r", 4), ("t_l", 4), ("t_s", 8),
        ("s_yh", 1), ("s_r", 4), ("s_l", 4), ("s_s", 8),
        ("s0", 8), ("part", 40), ("sq", 8),
        ("st_c", 2), ("st_y", 4), ("st_x", 4), ("st_z", 8),
        ("ga_c", 2), ("ga_y", 4), ("ga_x", 4), ("ga_z", 8),
        ("core", 4), ("rs1", 16), ("rs2", 16), ("rs3", 8),
    ):
        base[name] = s.take(n)
    return base, s.count


BASE, N_SEMS = layout()


def kernel(
    th_ref, tg_ref, thead_hbm, sh_ref, sg_ref, sg8_ref, shead_hbm, ids_ref,
    loss_ref, ghead_hbm, ghid_ref, ggain_ref,
    head, w, h5, scaled, part, got, ssq, sqs, sqr,
    s0, s16, f5, t4, slog, stc, cols,
    st_c, st_y, st_x, st_z, ga_c, ga_y, ga_x, ga_z,
    g_s, gp, gh, own, cs, cr, rs, r1, s2, r2, z3, r3,
    ssem, rsem,
):
    tp = lax.axis_index("tp")
    dp = lax.axis_index("dp")
    c = tp % 2
    z = (tp // 2) % 8
    yh = tp // 16
    x = dp // 2
    yl = dp % 2
    y = yh * 2 + yl

    def dev(xx, yy, zz, cc):
        return ((yy // 2) * 16 + zz * 2 + cc, xx * 2 + yy % 2)

    def zmod(v):
        return (v + 16) % 8

    def peer(axis, j):
        if axis == "c":
            return dev(x, y, z, (c + j) % 2)
        if axis == "x":
            return dev((x + j) % 4, y, z, c)
        if axis == "y":
            return dev(x, (y + j) % 4, z, c)
        return dev(x, y, (z + j) % 8, c)

    size = {"c": 2, "x": 4, "y": 4, "z": 8}
    mine = {"c": c, "x": x, "y": y, "z": z}

    def rc(src, dst, name, i, device):
        at = BASE[name] + i
        return pltpu.make_async_remote_copy(
            src_ref=src, dst_ref=dst, send_sem=ssem.at[at], recv_sem=rsem.at[at],
            device_id=device, device_id_type=MESH,
        )

    def arrived(dst, name, i):
        rc(dst, dst, name, i, peer("c", 1)).wait_recv()

    load_head = pltpu.make_async_copy(thead_hbm, head, ssem.at[BASE["load"]])
    load_w = pltpu.make_async_copy(shead_hbm, w, ssem.at[BASE["load"] + 1])
    load_head.start()
    load_w.start()

    barrier = pltpu.get_barrier_semaphore()
    partners = [peer("c", 1)]
    partners += [peer("x", j) for j in range(1, 4)]
    partners += [peer("y", j) for j in range(1, 4)]
    partners += [dev((x + j) % 4, yh * 2 + 1 - yl, z, c) for j in range(1, 4)]
    partners += [peer("z", j) for j in range(1, 8)]
    for device in partners:
        pl.semaphore_signal(barrier, inc=1, device_id=device, device_id_type=MESH)

    h5[yh, z, c] = th_ref[...]
    s0[dp] = sh_ref[...]
    pl.semaphore_wait(barrier, len(partners))

    yh_peer = dev(x, (y + 2) % 4, z, c)
    sibling = peer("c", 1)
    right = peer("z", 1)
    left = peer("z", 7)

    def yh_copy(buf, name):
        own_block = buf.at[yh, z, c]
        return rc(own_block, own_block, name + "_yh", 0, yh_peer)

    def ring_copies(buf, name, s):
        if s < 3:
            r, l = buf.at[:, zmod(z - s), c], buf.at[:, zmod(z + s), c]
        else:
            r, l = buf.at[0, zmod(z - s), c], buf.at[1, zmod(z + s), c]
        return rc(r, r, name + "_r", s, right), rc(l, l, name + "_l", s, left)

    def ring_arrived(buf, name, s):
        if s < 3:
            r, l = buf.at[:, zmod(z - 1 - s), c], buf.at[:, zmod(z + 1 + s), c]
        else:
            r, l = buf.at[0, zmod(z + 4), c], buf.at[1, zmod(z + 4), c]
        arrived(r, name + "_r", s)
        arrived(l, name + "_l", s)

    def units(s):
        if s == 0:
            return [(0, z)]
        if s == 4:
            return [(7, zmod(z + 4))]
        return [(2 * s - 1, zmod(z - s)), (2 * s, zmod(z + s))]

    def sib_copies(buf, name, s):
        return [
            rc(buf.at[:, zz, c], buf.at[:, zz, c], name + "_s", k, sibling) for k, zz in units(s)
        ]

    def sib_arrived(buf, name, s):
        for k, zz in units(s):
            arrived(buf.at[:, zz, 1 - c], name + "_s", k)

    yh_copy(h5, "t").start()

    def s0_copy(j):
        return rc(s0.at[dp], s0.at[dp], "s0", j, (tp, (dp + j) % 8))

    for j in range(1, 8):
        s0_copy(j).start()

    arrived(h5.at[1 - yh, z, c], "t_yh", 0)
    for cp in ring_copies(h5, "t", 0):
        cp.start()
    for cp in sib_copies(h5, "t", 0):
        cp.start()

    for j in range(1, 8):
        arrived(s0.at[(dp + 8 - j) % 8], "s0", j)
    for d in range(8):
        s16[2 * d : 2 * d + 2, :] = s0[d]
    wide = s16[...]
    inv16 = lax.rsqrt(jnp.sum(wide * wide, -1, keepdims=True) / D_S + epsilon)
    f5[yh, z, c] = (wide * inv16 * sg_ref[...]).astype(bf16)
    yh_copy(f5, "s").start()

    tg = tg_ref[...]

    def part_copy(j, k):
        rows = pl.ds(CHUNK_AT[k], CHUNK_ROWS[k])
        return rc(
            part.at[j, rows], got.at[j - 1, rows], "part", j * 5 + k, (tp, (dp + j) % 8)
        )

    def teacher_chunk(k):
        for i, (_, zz) in enumerate(units(k)):
            for half in range(2):
                block = h5[half, zz].reshape(32, 2048).astype(f32)
                squares = block * block
                total = squares[:, 0:128]
                for lane in range(128, 2048, 128):
                    total = total + squares[:, lane : lane + 128]
                ssq[half, zz] = total
                at = 64 * i + 32 * half
                scaled[at : at + 32, :] = (block * tg).astype(bf16)
        m = CHUNK_ROWS[k]

        def product(j):
            d = (dp + j) % 8
            columns = pl.ds(pl.multiple_of(d * SLICE, SLICE), SLICE)
            part[j, CHUNK_AT[k] : CHUNK_AT[k] + m, :] = jnp.dot(
                scaled[0:m, :], head[:, columns], preferred_element_type=f32
            )

        def send(j, carry):
            product(j)
            part_copy(j, k).start()
            return carry

        lax.fori_loop(1, 8, send, 0)
        product(0)

    load_head.wait()
    for s in range(4):
        ring_arrived(h5, "t", s)
        if s < 3:
            for cp in ring_copies(h5, "t", s + 1):
                cp.start()
        for cp in sib_copies(h5, "t", s + 1):
            cp.start()
        if s == 2:
            arrived(f5.at[1 - yh, z, c], "s_yh", 0)
            for cp in ring_copies(f5, "s", 0):
                cp.start()
            for cp in sib_copies(f5, "s", 0):
                cp.start()
        sib_arrived(h5, "t", s)
        teacher_chunk(s)
    sib_arrived(h5, "t", 4)
    teacher_chunk(4)

    sums = jnp.sum(ssq[...].reshape(TOKENS, 128).T, 0, keepdims=True)
    sqs[...] = jnp.broadcast_to(sums, (8, TOKENS))

    def sq_copy(j):
        return rc(sqs, sqr.at[j - 1], "sq", j, (tp, (dp + j) % 8))

    for j in range(1, 8):
        sq_copy(j).start()

    for s in range(4):
        ring_arrived(f5, "s", s)
        if s < 3:
            for cp in ring_copies(f5, "s", s + 1):
                cp.start()
        for cp in sib_copies(f5, "s", s + 1):
            cp.start()
    for s in range(5):
        sib_arrived(f5, "s", s)

    load_w.wait()
    for half in range(2):
        for quarter in range(2):
            rows = f5[half, 4 * quarter : 4 * quarter + 4].reshape(128, D_S)
            at = half * 256 + quarter * 128
            slog[at : at + 128, :] = jnp.dot(rows, w[...], preferred_element_type=f32)
    ids = jnp.broadcast_to(ids_ref[...], (128, TOKENS)).T
    ids = jnp.concatenate([ids, ids], axis=1)
    first = (tp * 8 + dp) * SLICE
    target_mask = ids == first + lax.broadcasted_iota(jnp.int32, (TOKENS, SLICE), 1)
    student = slog[...]
    s_top = jnp.max(student, -1, keepdims=True)
    s_total = jnp.sum(jnp.exp(student - s_top), -1, keepdims=True)
    target = jnp.sum(jnp.where(target_mask, student, 0.0), -1, keepdims=True)
    lane = lax.broadcasted_iota(jnp.int32, (TOKENS, 128), 1)
    stc[...] = jnp.where(
        lane == 3, s_top, jnp.where(lane == 4, s_total, jnp.where(lane == 5, target, 0.0))
    )

    for j in range(1, 8):
        arrived(sqr.at[j - 1], "sq", j)
    square_total = sqs[...]
    for j in range(7):
        square_total = square_total + sqr[j]
    t_inv = lax.rsqrt(square_total / D_T + epsilon)
    t_inv = jnp.broadcast_to(t_inv[0:1, :], (128, TOKENS)).T
    t_inv = jnp.concatenate([t_inv, t_inv], axis=1)
    for k in range(5):
        for j in range(1, 8):
            rows = pl.ds(CHUNK_AT[k], CHUNK_ROWS[k])
            arrived(got.at[j - 1, rows], "part", j * 5 + k)
        for i, (_, zz) in enumerate(units(k)):
            at = CHUNK_AT[k] + 64 * i
            total = part[0, at : at + 64, :]
            for j in range(7):
                total = total + got[j, at : at + 64, :]
            t4[0, zz] = total[0:32]
            t4[1, zz] = total[32:64]
    teacher = t4[...].reshape(TOKENS, SLICE) * t_inv

    t_top = jnp.max(teacher, -1, keepdims=True)
    t_exp = jnp.exp(teacher - t_top)
    t_total = jnp.sum(t_exp, -1, keepdims=True)
    cross = jnp.sum(t_exp * (teacher - student), -1, keepdims=True)
    packed = jnp.where(
        lane == 0, t_top, jnp.where(lane == 1, t_total, jnp.where(lane == 2, cross, stc[...]))
    )
    stats = packed.T[0:8, :]

    def exchange(buf, name, axis, value):
        buf[mine[axis]] = value
        for j in range(1, size[axis]):
            exchange_copy(buf, name, axis, j).start()

    def exchange_copy(buf, name, axis, j):
        slot = buf.at[mine[axis]]
        return rc(slot, slot, name + "_" + axis, j, peer(axis, j))

    def exchanged(buf, name, axis):
        n = size[axis]
        for j in range(1, n):
            arrived(buf.at[(mine[axis] + n - j) % n], name + "_" + axis, j)
        return [buf[i] for i in range(n)]

    def merged(parts):
        t_m = functools.reduce(jnp.maximum, [p[0:1] for p in parts])
        s_m = functools.reduce(jnp.maximum, [p[3:4] for p in parts])
        t_s = c_s = s_s = tgt = 0.0
        for p in parts:
            t_f = jnp.exp(p[0:1] - t_m)
            s_f = jnp.exp(p[3:4] - s_m)
            t_s = t_s + p[1:2] * t_f
            c_s = c_s + p[2:3] * t_f
            s_s = s_s + p[4:5] * s_f
            tgt = tgt + p[5:6]
        row = lax.broadcasted_iota(jnp.int32, (8, TOKENS), 0)
        out = jnp.zeros((8, TOKENS), f32)
        for i, v in enumerate((t_m, t_s, c_s, s_m, s_s, tgt)):
            out = jnp.where(row == i, v, out)
        return out

    for axis, buf in (("c", st_c), ("y", st_y), ("x", st_x), ("z", st_z)):
        exchange(buf, "st", axis, stats)
        stats = merged(exchanged(buf, "st", axis))

    t_lse = stats[0:1] + jnp.log(stats[1:2])
    s_lse = stats[3:4] + jnp.log(stats[4:5])
    loss_ref[...] = (
        stats[2:3] / stats[1:2] - t_lse + s_lse + hard_weight * (s_lse - stats[5:6])
    )
    t_col = jnp.broadcast_to(t_lse, (128, TOKENS)).T
    s_col = jnp.broadcast_to(s_lse, (128, TOKENS)).T
    t_prob = jnp.exp(teacher - jnp.concatenate([t_col, t_col], axis=1))
    s_prob = jnp.exp(student - jnp.concatenate([s_col, s_col], axis=1))
    onehot = target_mask.astype(f32)
    g = (loss_scale * (s_prob - t_prob + hard_weight * (s_prob - onehot))).astype(bf16)
    g_s[...] = g

    p = lax.broadcasted_iota(jnp.int32, (TOKENS, TOKENS), 0)
    q = lax.broadcasted_iota(jnp.int32, (TOKENS, TOKENS), 1)
    source = (
        ((p >> 5) & 1) * 256
        + ((p >> 1) & 7) * 32
        + (p >> 8) * 16
        + ((p >> 6) & 3) * 4
        + ((p >> 4) & 1) * 2
        + (p & 1)
    )
    perm = jnp.where(q == source, 1.0, 0.0).astype(bf16)
    gp[...] = jnp.dot(perm, g, preferred_element_type=f32).astype(bf16)

    def core_copy(ch):
        return rc(cs.at[ch], cr.at[ch], "core", ch, sibling)

    other_rows = pl.ds(pl.multiple_of((1 - c) * 256, 256), 256)
    own_rows = pl.ds(pl.multiple_of(c * 256, 256), 256)
    for ch in ORDER:
        for tile in range(2):
            at = ch * WIDE + tile * 512
            cs[ch, :, tile * 512 : tile * 512 + 512] = lax.dot_general(
                gp[other_rows, :], w[at : at + 512, :], NT, preferred_element_type=f32
            ).astype(bf16)
        core_copy(ch).start()
    for ch in ORDER:
        for tile in range(2):
            at = ch * WIDE + tile * 512
            own[ch, :, tile * 512 : tile * 512 + 512] = lax.dot_general(
                gp[own_rows, :], w[at : at + 512, :], NT, preferred_element_type=f32
            )

    def rs1_copy(ch, j):
        if ch < 2:
            return rc(rs.at[ch, (x + j) % 4], r1.at[ch, j - 1], "rs1", ch * 4 + j, peer("x", j))
        return rc(rs.at[ch, :, (y + j) % 4], r1.at[ch, j - 1], "rs1", ch * 4 + j, peer("y", j))

    for ch in ORDER:
        arrived(cr.at[ch], "core", ch)
        both = own[ch] + cr[ch].astype(f32)
        rs[ch] = both.astype(bf16).reshape(4, 4, 16, WIDE)
        for j in range(1, 4):
            rs1_copy(ch, j).start()

    ones = jnp.ones((8, SLICE), bf16)

    def head_tile(i, carry):
        at = pl.ds(pl.multiple_of(i * 512, 512), 512)
        features = f5[:, :, :, :, at].reshape(TOKENS, 512)
        tile = jnp.dot(features.T, g_s[...], preferred_element_type=f32)
        gh[at, :] = tile.astype(bf16)
        product = tile * w[at, :].astype(f32)
        high = product.astype(bf16)
        low = (product - high.astype(f32)).astype(bf16)
        row = lax.dot_general(ones, high, NT, preferred_element_type=f32) + lax.dot_general(
            ones, low, NT, preferred_element_type=f32
        )
        cols[...] = jnp.where(
            lax.broadcasted_iota(jnp.int32, (8, 512), 0) == i, row, cols[...]
        )
        return carry

    cols[...] = jnp.zeros((8, 512), f32)
    lax.fori_loop(0, 8, head_tile, 0)
    store_head = pltpu.make_async_copy(gh, ghead_hbm, ssem.at[BASE["load"] + 2])
    store_head.start()
    gain = cols[...]
    for axis, buf in (("c", ga_c), ("x", ga_x)):
        exchange(buf, "ga", axis, gain)
        gain = functools.reduce(jnp.add, exchanged(buf, "ga", axis))
    exchange(ga_y, "ga", "y", gain)

    def rs2_copy(ch, j):
        if ch < 2:
            return rc(s2.at[ch, (y + j) % 4], r2.at[ch, j - 1], "rs2", ch * 4 + j, peer("y", j))
        return rc(s2.at[ch, (x + j) % 4], r2.at[ch, j - 1], "rs2", ch * 4 + j, peer("x", j))

    for ch in ORDER:
        for j in range(1, 4):
            arrived(r1.at[ch, j - 1], "rs1", ch * 4 + j)
        kept = rs[ch, x] if ch < 2 else rs[ch, :, y]
        total = kept.astype(f32)
        for j in range(3):
            total = total + r1[ch, j].astype(f32)
        s2[ch] = total.astype(bf16)
        for j in range(1, 4):
            rs2_copy(ch, j).start()

    gain = functools.reduce(jnp.add, exchanged(ga_y, "ga", "y"))
    exchange(ga_z, "ga", "z", gain)

    for ch in ORDER:
        for j in range(1, 4):
            arrived(r2.at[ch, j - 1], "rs2", ch * 4 + j)
        kept = s2[ch, y] if ch < 2 else s2[ch, x]
        total = kept.astype(f32)
        for j in range(3):
            total = total + r2[ch, j].astype(f32)
        for zz in range(8):
            z3[zz, :, ch * WIDE : ch * WIDE + WIDE] = total[2 * zz : 2 * zz + 2, :]

    def rs3_copy(j):
        return rc(z3.at[(z + j) % 8], r3.at[j - 1], "rs3", j, peer("z", j))

    for j in range(1, 8):
        rs3_copy(j).start()

    own_wide = sh_ref[...]
    own_inv = lax.rsqrt(jnp.sum(own_wide * own_wide, -1, keepdims=True) / D_S + epsilon)
    own_normed = own_wide * own_inv
    gain = functools.reduce(jnp.add, exchanged(ga_z, "ga", "z"))
    ggain_ref[...] = gain / sg8_ref[...]

    for j in range(1, 8):
        arrived(r3.at[j - 1], "rs3", j)
    grad_features = z3[z]
    for j in range(7):
        grad_features = grad_features + r3[j]
    grad_normed = grad_features * sg_ref[...]
    inner = jnp.sum(grad_normed * own_normed, -1, keepdims=True) / D_S
    ghid_ref[...] = own_inv * (grad_normed - own_normed * inner)

    for buf, name in ((h5, "t"), (f5, "s")):
        yh_copy(buf, name).wait_send()
        for s in range(4):
            for cp in ring_copies(buf, name, s):
                cp.wait_send()
        for s in range(5):
            for cp in sib_copies(buf, name, s):
                cp.wait_send()
    for j in range(1, 8):
        s0_copy(j).wait_send()
        sq_copy(j).wait_send()
        rs3_copy(j).wait_send()
        for k in range(5):
            part_copy(j, k).wait_send()
    for name, bufs in (("st", (st_c, st_y, st_x, st_z)), ("ga", (ga_c, ga_y, ga_x, ga_z))):
        for axis, buf in zip("cyxz", bufs):
            for j in range(1, size[axis]):
                exchange_copy(buf, name, axis, j).wait_send()
    for ch in range(4):
        core_copy(ch).wait_send()
        for j in range(1, 4):
            rs1_copy(ch, j).wait_send()
            rs2_copy(ch, j).wait_send()
    store_head.wait()


def shards(
    teacher_hidden,
    teacher_gain,
    teacher_head,
    student_hidden,
    student_gain,
    student_head,
    token_ids,
):
    vmem = pl.BlockSpec(memory_space=pltpu.VMEM)
    hbm = pl.BlockSpec(memory_space=pl.ANY)
    gain_wide = student_gain.astype(f32)
    row8 = (8, TOKENS)
    scratch = [
        ((2048, 2048), bf16), ((D_S, SLICE), bf16), ((2, 8, 2, 16, 2048), bf16),
        ((128, 2048), bf16), ((8, TOKENS, SLICE), f32), ((7, TOKENS, SLICE), f32),
        ((2, 8, 32, 128), f32), (row8, f32), ((7,) + row8, f32),
        ((8, 2, D_S), f32), ((16, D_S), f32), ((2, 8, 2, 16, D_S), bf16),
        ((2, 8, 32, SLICE), f32), ((TOKENS, SLICE), f32), ((TOKENS, 128), f32), ((8, 512), f32),
        ((2,) + row8, f32), ((4,) + row8, f32), ((4,) + row8, f32), ((8,) + row8, f32),
        ((2,) + row8, f32), ((4,) + row8, f32), ((4,) + row8, f32), ((8,) + row8, f32),
        ((TOKENS, SLICE), bf16), ((TOKENS, SLICE), bf16), ((D_S, SLICE), bf16),
        ((4, 256, WIDE), f32), ((4, 256, WIDE), bf16), ((4, 256, WIDE), bf16),
        ((4, 4, 4, 16, WIDE), bf16), ((4, 3, 4, 16, WIDE), bf16),
        ((4, 4, 16, WIDE), bf16), ((4, 3, 16, WIDE), bf16),
        ((8, 2, D_S), f32), ((7, 2, D_S), f32),
    ]
    loss, grad_head, grad_hidden, grad_gain = pl.pallas_call(
        kernel,
        out_shape=(
            jax.ShapeDtypeStruct((1, TOKENS), f32),
            jax.ShapeDtypeStruct((D_S, SLICE), bf16),
            jax.ShapeDtypeStruct((2, D_S), f32),
            jax.ShapeDtypeStruct((8, 512), f32),
        ),
        in_specs=[vmem, vmem, hbm, vmem, vmem, vmem, hbm, vmem],
        out_specs=(vmem, hbm, vmem, vmem),
        scratch_shapes=[pltpu.VMEM(shape, dtype) for shape, dtype in scratch]
        + [pltpu.SemaphoreType.DMA((N_SEMS,)), pltpu.SemaphoreType.DMA((N_SEMS,))],
        compiler_params=pltpu.CompilerParams(
            collective_id=0, has_side_effects=True, vmem_limit_bytes=56 * 1024 * 1024
        ),
        cost_estimate=pl.CostEstimate(
            flops=7_600_000_000, bytes_accessed=13_000_000, transcendentals=600_000
        ),
    )(
        teacher_hidden,
        teacher_gain.astype(f32).reshape(1, 2048),
        teacher_head,
        student_hidden.astype(f32),
        gain_wide.reshape(1, D_S),
        gain_wide.reshape(8, 512),
        student_head,
        token_ids.reshape(1, TOKENS),
    )
    return (
        loss.reshape(TOKENS),
        grad_hidden.astype(bf16),
        grad_gain.reshape(D_S),
        grad_head,
    )


def solution(mesh):
    in_specs = (
        P("tp", "dp"),
        P("dp"),
        P("dp", "tp"),
        P(("tp", "dp"), None),
        P(),
        P(None, ("tp", "dp")),
        P(),
    )
    out_specs = (P(), P(("tp", "dp"), None), P(), P(None, ("tp", "dp")))
    return jax.shard_map(shards, mesh=mesh, in_specs=in_specs, out_specs=out_specs, check_vma=False)
```

```python
import functools

import jax
import jax.numpy as jnp
from jax import lax
from jax.experimental import pallas as pl
from jax.experimental.pallas import tpu as pltpu
from jax.sharding import PartitionSpec as P

D_T = 16384
D_S = 4096
TOKENS = 512
SLICE = 256

epsilon = 1e-05
hard_weight = 0.5
loss_scale = 64.0

MESH = pl.DeviceIdType.MESH
f32 = jnp.float32
bf16 = jnp.bfloat16
NT = (((1,), (1,)), ((), ()))

CHUNK_ROWS = (32, 64, 64, 64, 32)
CHUNK_AT = (0, 32, 96, 160, 224)
ORDER = (0, 2, 1, 3)
WIDE = 1024


class Sems:
    def __init__(self):
        self.count = 0

    def take(self, n):
        at = self.count
        self.count += n
        return at


def layout():
    s = Sems()
    base = {}
    for name, n in (
        ("load", 3),
        ("t_yh", 1), ("t_r", 4), ("t_l", 4), ("t_s", 8),
        ("s_yh", 1), ("s_r", 8), ("s_l", 8), ("s_s", 8),
        ("s0", 8), ("ex", 50), ("sq", 8),
        ("st_cx", 8), ("st_y", 4), ("st_z", 8),
        ("ga_cx", 8), ("ga_y", 4), ("ga_z", 8),
        ("core", 4), ("q1", 8), ("q2", 8), ("rs2", 16), ("rs3", 8),
    ):
        base[name] = s.take(n)
    return base, s.count


BASE, N_SEMS = layout()


def kernel(
    th_ref, tg_ref, thead_hbm, sh_ref, sg_ref, shead_hbm, ids_ref,
    loss_ref, ghead_hbm, ghid_ref, ggain_ref,
    head, w, wt, h5, scaled, pa, pb, ya, xa1, xa2, xb1, xb2, yb, ssq, sqs, sqr,
    s0, s16, f5, t4, slog, stc, cols,
    st_cx, st_y, st_z, ga_cx, ga_y, ga_z,
    g_s, gp, perm, gh, own, cs, cr, rs, q1, q2, s2, r2, zf, zb, r3, unfolded,
    ssem, rsem,
):
    tp = lax.axis_index("tp")
    dp = lax.axis_index("dp")
    c = tp % 2
    z = (tp // 2) % 8
    yh = tp // 16
    x = dp // 2
    yl = dp % 2
    y = yh * 2 + yl

    def dev(xx, yy, zz, cc):
        return ((yy // 2) * 16 + zz * 2 + cc, xx * 2 + yy % 2)

    def zmod(v):
        return (v + 16) % 8

    def peer(axis, j):
        if axis == "c":
            return dev(x, y, z, (c + j) % 2)
        if axis == "x":
            return dev((x + j) % 4, y, z, c)
        if axis == "y":
            return dev(x, (y + j) % 4, z, c)
        if axis == "cx":
            at = (x * 2 + c + j) % 8
            return dev(at // 2, y, z, at % 2)
        return dev(x, y, (z + j) % 8, c)

    size = {"cx": 8, "y": 4, "z": 8}
    mine = {"cx": x * 2 + c, "y": y, "z": z}

    def rc(src, dst, name, i, device):
        at = BASE[name] + i
        return pltpu.make_async_remote_copy(
            src_ref=src, dst_ref=dst, send_sem=ssem.at[at], recv_sem=rsem.at[at],
            device_id=device, device_id_type=MESH,
        )

    def arrived(dst, name, i):
        rc(dst, dst, name, i, peer("c", 1)).wait_recv()

    load_head = pltpu.make_async_copy(thead_hbm, head, ssem.at[BASE["load"]])
    load_w = pltpu.make_async_copy(shead_hbm, w, ssem.at[BASE["load"] + 1])
    load_head.start()
    load_w.start()

    barrier = pltpu.get_barrier_semaphore()
    partners = [peer("c", 1)]
    partners += [dev((x + j) % 4, y, z, cc) for j in range(1, 4) for cc in range(2)]
    partners += [peer("y", j) for j in range(1, 4)]
    partners += [dev((x + j) % 4, yh * 2 + 1 - yl, z, c) for j in range(1, 4)]
    partners += [peer("z", j) for j in range(1, 8)]
    for device in partners:
        pl.semaphore_signal(barrier, inc=1, device_id=device, device_id_type=MESH)

    h5[yh, z, c] = th_ref[...]
    s0[dp] = sh_ref[...].astype(f32)
    pl.semaphore_wait(barrier, len(partners))

    yh_peer = dev(x, (y + 2) % 4, z, c)
    sibling = peer("c", 1)
    right = peer("z", 1)
    left = peer("z", 7)

    y_outer = dev(x, 3 - y, z, c)

    def yh_copy(buf, name):
        own_block = buf.at[yh, z, c]
        return rc(own_block, own_block, name + "_yh", 0, yh_peer if name == "t" else y_outer)

    def ring_copies(buf, name, s):
        if s < 3:
            r, l = buf.at[:, zmod(z - s), c], buf.at[:, zmod(z + s), c]
        else:
            r, l = buf.at[0, zmod(z - s), c], buf.at[1, zmod(z + s), c]
        return rc(r, r, name + "_r", s, right), rc(l, l, name + "_l", s, left)

    def ring_arrived(buf, name, s):
        if s < 3:
            r, l = buf.at[:, zmod(z - 1 - s), c], buf.at[:, zmod(z + 1 + s), c]
        else:
            r, l = buf.at[0, zmod(z + 4), c], buf.at[1, zmod(z + 4), c]
        arrived(r, name + "_r", s)
        arrived(l, name + "_l", s)

    def half_copies(s, half):
        r, l = f5.at[half, zmod(z - s), c], f5.at[half, zmod(z + s), c]
        copies = []
        if s < 3 or half == 0:
            copies.append(rc(r, r, "s_r", 2 * s + half, right))
        if s < 3 or half == 1:
            copies.append(rc(l, l, "s_l", 2 * s + half, left))
        return copies

    def half_arrived(s, half):
        if s < 3 or half == 0:
            arrived(f5.at[half, zmod(z - 1 - s), c], "s_r", 2 * s + half)
        if s < 3 or half == 1:
            arrived(f5.at[half, zmod(z + 1 + s), c], "s_l", 2 * s + half)

    def student_step(s, half):
        half_arrived(s, half)
        if s < 3:
            for cp in half_copies(s + 1, half):
                cp.start()
        if half == 1:
            for cp in sib_copies(f5, "s", s + 1):
                cp.start()

    def units(s):
        if s == 0:
            return [(0, z)]
        if s == 4:
            return [(7, zmod(z + 4))]
        return [(2 * s - 1, zmod(z - s)), (2 * s, zmod(z + s))]

    def sib_copies(buf, name, s):
        return [
            rc(buf.at[:, zz, c], buf.at[:, zz, c], name + "_s", k, sibling) for k, zz in units(s)
        ]

    def sib_arrived(buf, name, s):
        for k, zz in units(s):
            arrived(buf.at[:, zz, 1 - c], name + "_s", k)

    yh_copy(h5, "t").start()

    def s0_copy(j):
        return rc(s0.at[dp], s0.at[dp], "s0", j, (tp, (dp + j) % 8))

    for j in range(1, 8):
        s0_copy(j).start()

    arrived(h5.at[1 - yh, z, c], "t_yh", 0)
    for cp in ring_copies(h5, "t", 0):
        cp.start()
    for cp in sib_copies(h5, "t", 0):
        cp.start()

    for j in range(1, 8):
        arrived(s0.at[(dp + 8 - j) % 8], "s0", j)
    for d in range(8):
        s16[2 * d : 2 * d + 2, :] = s0[d]
    wide = s16[...]
    inv16 = lax.rsqrt(jnp.sum(wide * wide, -1, keepdims=True) / D_S + epsilon)
    gain_row = sg_ref[...].astype(f32).reshape(1, D_S)
    f5[yh, z, c] = (wide * inv16 * gain_row).astype(bf16)
    yh_copy(f5, "s").start()

    tg = tg_ref[...].astype(f32).reshape(1, 2048)

    x_right = peer("x", 1)
    x_left = peer("x", 3)
    y_pair = dev(x, yh * 2 + 1 - yl, z, c)

    def span(k, part):
        at, n = CHUNK_AT[k], CHUNK_ROWS[k]
        return {"all": pl.ds(at, n), "r": pl.ds(at, n // 2), "l": pl.ds(at + n // 2, n // 2)}[part]

    def ex_copies(k, step):
        every, rows_r, rows_l = span(k, "all"), span(k, "r"), span(k, "l")
        a_y = (pa.at[:, 1, every], ya.at[:, every], 0, y_pair)
        a_x1r = (pa.at[2, 0, rows_r], xa1.at[0, rows_r], 1, x_right)
        a_x1l = (pa.at[2, 0, rows_l], xa1.at[1, rows_l], 2, x_left)
        a_x2r = (pa.at[1, 0, every], xa2.at[0, every], 3, x_right)
        a_x2l = (pa.at[3, 0, every], xa2.at[1, every], 4, x_left)
        b_x1r = (pb.at[2, :, rows_r], xb1.at[0, :, rows_r], 5, x_right)
        b_x1l = (pb.at[2, :, rows_l], xb1.at[1, :, rows_l], 6, x_left)
        b_x2r = (pb.at[1, :, every], xb2.at[0, :, every], 7, x_right)
        b_x2l = (pb.at[3, :, every], xb2.at[1, :, every], 8, x_left)
        b_y = (pb.at[0, 1, every], yb.at[every], 9, y_pair)
        steps = (
            (a_y, b_x1r, b_x1l), (a_x1r, a_x1l, b_x2r, b_x2l), (a_x2r, a_x2l, b_y),
        )
        return [rc(src, dst, "ex", k * 10 + i, device) for src, dst, i, device in steps[step]]

    def ex_arrived(k, step):
        for cp in ex_copies(k, step):
            cp.wait_recv()

    def ex_send(k, step):
        for cp in ex_copies(k, step):
            cp.start()

    def ex_second(k):
        every, rows_r, rows_l = span(k, "all"), span(k, "r"), span(k, "l")
        ex_arrived(k, 0)
        pb[1, :, rows_r] += xb1[0, :, rows_r]
        pb[3, :, rows_l] += xb1[1, :, rows_l]
        pa[:, 0, every] += ya[:, every]
        ex_send(k, 1)

    def ex_third(k):
        every, rows_r, rows_l = span(k, "all"), span(k, "r"), span(k, "l")
        ex_arrived(k, 1)
        pa[1, 0, rows_r] += xa1[0, rows_r]
        pa[3, 0, rows_l] += xa1[1, rows_l]
        pb[0, :, every] += xb2[0, :, every] + xb2[1, :, every]
        ex_send(k, 2)

    def teacher_chunk(k):
        for i, (_, zz) in enumerate(units(k)):
            for half in range(2):
                block = h5[half, zz].reshape(32, 2048).astype(f32)
                squares = block * block
                total = squares[:, 0:128]
                for lane in range(128, 2048, 128):
                    total = total + squares[:, lane : lane + 128]
                ssq[half, zz] = total
                at = CHUNK_ROWS[k] * half + 32 * i
                scaled[at : at + 32, :] = (block * tg).astype(bf16)
        m = CHUNK_ROWS[k]

        def product(j, carry):
            xo, yo = j // 2, j % 2
            d = ((x + xo) % 4) * 2 + (yl + yo) % 2
            columns = pl.ds(pl.multiple_of(d * SLICE, SLICE), SLICE)
            both = jnp.dot(scaled[0 : 2 * m, :], head[:, columns], preferred_element_type=f32)
            pa[xo, yo, CHUNK_AT[k] : CHUNK_AT[k] + m, :] = both[0:m]
            pb[xo, yo, CHUNK_AT[k] : CHUNK_AT[k] + m, :] = both[m : 2 * m]
            return carry

        lax.fori_loop(0, 8, product, 0)
        ex_send(k, 0)

    load_w.wait()

    def turn(i, carry):
        at = pl.ds(pl.multiple_of(i * 512, 512), 512)
        wt[:, at] = w[at, :].T
        return carry

    lax.fori_loop(0, 8, turn, 0)
    load_head.wait()
    for s in range(4):
        ring_arrived(h5, "t", s)
        if s < 3:
            for cp in ring_copies(h5, "t", s + 1):
                cp.start()
        for cp in sib_copies(h5, "t", s + 1):
            cp.start()
        if s == 0:
            arrived(f5.at[1 - yh, z, c], "s_yh", 0)
            for half in range(2):
                for cp in half_copies(0, half):
                    cp.start()
            for cp in sib_copies(f5, "s", 0):
                cp.start()
        if s >= 2:
            student_step(0, s - 2)
        sib_arrived(h5, "t", s)
        teacher_chunk(s)
        if s >= 1:
            ex_second(s - 1)
        if s >= 2:
            ex_third(s - 2)
    student_step(1, 0)
    sib_arrived(h5, "t", 4)
    teacher_chunk(4)
    student_step(1, 1)

    sums = jnp.sum(ssq[...].reshape(TOKENS, 128).T, 0, keepdims=True)
    sqs[...] = jnp.broadcast_to(sums, (8, TOKENS))

    def sq_copy(j):
        return rc(sqs, sqr.at[j - 1], "sq", j, (tp, (dp + j) % 8))

    for j in range(1, 8):
        sq_copy(j).start()

    ex_second(3)
    ex_third(2)
    student_step(2, 0)
    ex_second(4)
    student_step(2, 1)
    ex_third(3)
    student_step(3, 0)
    ex_third(4)
    student_step(3, 1)
    for s in range(5):
        sib_arrived(f5, "s", s)

    p = lax.broadcasted_iota(jnp.int32, (TOKENS, TOKENS), 0)
    q = lax.broadcasted_iota(jnp.int32, (TOKENS, TOKENS), 1)
    source = (
        ((p >> 5) & 1) * 256
        + ((p >> 1) & 7) * 32
        + (p >> 8) * 16
        + ((p >> 6) & 3) * 4
        + ((p >> 4) & 1) * 2
        + (p & 1)
    )
    perm[...] = jnp.where(q == source, 1.0, 0.0).astype(bf16)

    for half in range(2):
        for quarter in range(2):
            rows = f5[half, 4 * quarter : 4 * quarter + 4].reshape(128, D_S)
            at = half * 256 + quarter * 128
            slog[at : at + 128, :] = jnp.dot(rows, w[...], preferred_element_type=f32)
    ids = jnp.broadcast_to(ids_ref[...], (128, TOKENS)).T
    ids = jnp.concatenate([ids, ids], axis=1)
    first = (tp * 8 + dp) * SLICE
    target_mask = ids == first + lax.broadcasted_iota(jnp.int32, (TOKENS, SLICE), 1)
    student = slog[...]
    s_top = jnp.max(student, -1, keepdims=True)
    s_total = jnp.sum(jnp.exp(student - s_top), -1, keepdims=True)
    target = jnp.sum(jnp.where(target_mask, student, 0.0), -1, keepdims=True)
    lane = lax.broadcasted_iota(jnp.int32, (TOKENS, 128), 1)
    stc[...] = jnp.where(
        lane == 3, s_top, jnp.where(lane == 4, s_total, jnp.where(lane == 5, target, 0.0))
    )

    for j in range(1, 8):
        arrived(sqr.at[j - 1], "sq", j)
    square_total = sqs[...]
    for j in range(7):
        square_total = square_total + sqr[j]
    t_inv = lax.rsqrt(square_total / D_T + epsilon)
    t_inv = jnp.broadcast_to(t_inv[0:1, :], (128, TOKENS)).T
    t_inv = jnp.concatenate([t_inv, t_inv], axis=1)
    for k in range(5):
        ex_arrived(k, 2)
        for i, (_, zz) in enumerate(units(k)):
            rows = pl.ds(CHUNK_AT[k] + 32 * i, 32)
            t4[0, zz] = pa[0, 0, rows] + xa2[0, rows] + xa2[1, rows]
            t4[1, zz] = pb[0, 0, rows] + yb[rows]
    teacher = t4[...].reshape(TOKENS, SLICE) * t_inv

    t_top = jnp.max(teacher, -1, keepdims=True)
    t_exp = jnp.exp(teacher - t_top)
    t_total = jnp.sum(t_exp, -1, keepdims=True)
    cross = jnp.sum(t_exp * (teacher - student), -1, keepdims=True)
    packed = jnp.where(
        lane == 0, t_top, jnp.where(lane == 1, t_total, jnp.where(lane == 2, cross, stc[...]))
    )
    stats = packed.T[0:8, :]

    def exchange(buf, name, axis, value):
        buf[mine[axis]] = value
        for j in range(1, size[axis]):
            exchange_copy(buf, name, axis, j).start()

    def exchange_copy(buf, name, axis, j):
        slot = buf.at[mine[axis]]
        return rc(slot, slot, name + "_" + axis, j, peer(axis, j))

    def exchanged(buf, name, axis):
        n = size[axis]
        for j in range(1, n):
            arrived(buf.at[(mine[axis] + n - j) % n], name + "_" + axis, j)
        return [buf[i] for i in range(n)]

    def merged(parts):
        t_m = functools.reduce(jnp.maximum, [p[0:1] for p in parts])
        s_m = functools.reduce(jnp.maximum, [p[3:4] for p in parts])
        t_s = c_s = s_s = tgt = 0.0
        for p in parts:
            t_f = jnp.exp(p[0:1] - t_m)
            s_f = jnp.exp(p[3:4] - s_m)
            t_s = t_s + p[1:2] * t_f
            c_s = c_s + p[2:3] * t_f
            s_s = s_s + p[4:5] * s_f
            tgt = tgt + p[5:6]
        row = lax.broadcasted_iota(jnp.int32, (8, TOKENS), 0)
        out = jnp.zeros((8, TOKENS), f32)
        for i, v in enumerate((t_m, t_s, c_s, s_m, s_s, tgt)):
            out = jnp.where(row == i, v, out)
        return out

    for axis, buf in (("cx", st_cx), ("y", st_y), ("z", st_z)):
        exchange(buf, "st", axis, stats)
        stats = merged(exchanged(buf, "st", axis))

    t_lse = stats[0:1] + jnp.log(stats[1:2])
    s_lse = stats[3:4] + jnp.log(stats[4:5])
    loss_ref[...] = (
        stats[2:3] / stats[1:2] - t_lse + s_lse + hard_weight * (s_lse - stats[5:6])
    )
    t_col = jnp.broadcast_to(t_lse, (128, TOKENS)).T
    s_col = jnp.broadcast_to(s_lse, (128, TOKENS)).T
    t_prob = jnp.exp(teacher - jnp.concatenate([t_col, t_col], axis=1))
    s_prob = jnp.exp(student - jnp.concatenate([s_col, s_col], axis=1))
    onehot = target_mask.astype(f32)
    g = (loss_scale * (s_prob - t_prob + hard_weight * (s_prob - onehot))).astype(bf16)
    g_s[...] = g

    gp[...] = jnp.dot(perm[...], g, preferred_element_type=f32).astype(bf16)

    def core_copy(ch):
        return rc(cs.at[ch], cr.at[ch], "core", ch, sibling)

    other_rows = pl.ds(pl.multiple_of((1 - c) * 256, 256), 256)
    own_rows = pl.ds(pl.multiple_of(c * 256, 256), 256)
    def product_of(rows, ch, tile):
        at = ch * WIDE + tile * 512
        return jnp.dot(gp[rows, :], wt[:, at : at + 512], preferred_element_type=f32)

    def other_part(ch):
        for tile in range(2):
            cs[ch, :, tile * 512 : tile * 512 + 512] = product_of(other_rows, ch, tile).astype(bf16)
        core_copy(ch).start()

    def own_part(ch):
        for tile in range(2):
            own[ch, :, tile * 512 : tile * 512 + 512] = product_of(own_rows, ch, tile)

    def shard(ch, o, part=slice(0, 4)):
        if ch < 2:
            return rs.at[ch, (x + o) % 4, part]
        return rs.at[ch, part, (y + o) % 4]

    y_right = peer("y", 1)
    y_left = peer("y", 3)

    def q1_copies(ch):
        r, l = (x_right, x_left) if ch < 2 else (y_right, y_left)
        return (
            rc(shard(ch, 2, slice(0, 2)), q1.at[ch, 0], "q1", ch * 2, r),
            rc(shard(ch, 2, slice(2, 4)), q1.at[ch, 1], "q1", ch * 2 + 1, l),
        )

    def q2_copies(ch):
        r, l = (x_right, x_left) if ch < 2 else (y_right, y_left)
        return (
            rc(shard(ch, 1), q2.at[ch, 0], "q2", ch * 2, r),
            rc(shard(ch, 3), q2.at[ch, 1], "q2", ch * 2 + 1, l),
        )

    other_part(ORDER[0])
    other_part(ORDER[1])
    for i, ch in enumerate(ORDER):
        own_part(ch)
        if i + 2 < 4:
            other_part(ORDER[i + 2])
        arrived(cr.at[ch], "core", ch)
        both = own[ch] + cr[ch].astype(f32)
        rs[ch] = both.astype(bf16).reshape(4, 4, 16, WIDE)
        for cp in q1_copies(ch):
            cp.start()
    for ch in ORDER:
        for cp in q1_copies(ch):
            cp.wait_recv()
        for o, part, way in ((1, slice(0, 2), 0), (3, slice(2, 4), 1)):
            ref = shard(ch, o, part)
            ref[...] = (ref[...].astype(f32) + q1[ch, way].astype(f32)).astype(bf16)
        for cp in q2_copies(ch):
            cp.start()

    ones = jnp.ones((8, SLICE), bf16)

    def head_tile(i, carry):
        at = pl.ds(pl.multiple_of(i * 512, 512), 512)
        features = f5[:, :, :, :, at].reshape(TOKENS, 512)
        tile = jnp.dot(features.T, g_s[...], preferred_element_type=f32)
        gh[at, :] = tile.astype(bf16)
        product = tile * w[at, :].astype(f32)
        high = product.astype(bf16)
        low = (product - high.astype(f32)).astype(bf16)
        row = lax.dot_general(ones, high, NT, preferred_element_type=f32) + lax.dot_general(
            ones, low, NT, preferred_element_type=f32
        )
        cols[...] = jnp.where(
            lax.broadcasted_iota(jnp.int32, (8, 512), 0) == i, row, cols[...]
        )
        return carry

    cols[...] = jnp.zeros((8, 512), f32)
    lax.fori_loop(0, 8, head_tile, 0)
    store_head = pltpu.make_async_copy(gh, ghead_hbm, ssem.at[BASE["load"] + 2])
    store_head.start()
    gain = cols[...]
    exchange(ga_cx, "ga", "cx", gain)

    def rs2_copy(ch, j):
        if ch < 2:
            return rc(s2.at[ch, (y + j) % 4], r2.at[ch, j - 1], "rs2", ch * 4 + j, peer("y", j))
        return rc(s2.at[ch, (x + j) % 4], r2.at[ch, j - 1], "rs2", ch * 4 + j, peer("x", j))

    for ch in ORDER:
        for cp in q2_copies(ch):
            cp.wait_recv()
        kept = shard(ch, 0)[...].astype(f32)
        total = kept + (q2[ch, 0].astype(f32) + q2[ch, 1].astype(f32))
        s2[ch] = total.astype(bf16)
        for j in range(1, 4):
            rs2_copy(ch, j).start()

    gain = functools.reduce(jnp.add, exchanged(ga_cx, "ga", "cx"))
    exchange(ga_y, "ga", "y", gain)

    for ch in ORDER:
        for j in range(1, 4):
            arrived(r2.at[ch, j - 1], "rs2", ch * 4 + j)
        kept = s2[ch, y] if ch < 2 else s2[ch, x]
        total = kept.astype(f32)
        for j in range(3):
            total = total + r2[ch, j].astype(f32)
        for zz in range(8):
            for half in range(2):
                at = 4 * ch + 2 * half
                zf[zz, at : at + 2, :] = total[2 * zz : 2 * zz + 2, 512 * half : 512 * half + 512]
    zb[...] = zf[...].astype(bf16)

    def rs3_copy(j):
        return rc(zb.at[(z + j) % 8], r3.at[j - 1], "rs3", j, peer("z", j))

    for j in range(1, 8):
        rs3_copy(j).start()

    gain = functools.reduce(jnp.add, exchanged(ga_y, "ga", "y"))
    exchange(ga_z, "ga", "z", gain)

    own_wide = sh_ref[...].astype(f32)
    own_inv = lax.rsqrt(jnp.sum(own_wide * own_wide, -1, keepdims=True) / D_S + epsilon)
    own_normed = own_wide * own_inv
    for j in range(1, 8):
        arrived(r3.at[j - 1], "rs3", j)
    folded = zf[z]
    for j in range(7):
        folded = folded + r3[j].astype(f32)
    for i in range(8):
        unfolded[:, 512 * i : 512 * i + 512] = folded[2 * i : 2 * i + 2, :]
    grad_normed = unfolded[...] * gain_row
    inner = jnp.sum(grad_normed * own_normed, -1, keepdims=True) / D_S
    ghid_ref[...] = own_inv * (grad_normed - own_normed * inner)

    gain = functools.reduce(jnp.add, exchanged(ga_z, "ga", "z"))
    row = lax.broadcasted_iota(jnp.int32, (8, 512), 0)
    gain_rows = jnp.ones((8, 512), f32)
    for i in range(8):
        gain_rows = jnp.where(row == i, gain_row[:, 512 * i : 512 * i + 512], gain_rows)
    ggain_ref[...] = gain / gain_rows

    for buf, name in ((h5, "t"), (f5, "s")):
        yh_copy(buf, name).wait_send()
        for s in range(4):
            copies = ring_copies(buf, name, s) if name == "t" else half_copies(s, 0) + half_copies(s, 1)
            for cp in copies:
                cp.wait_send()
        for s in range(5):
            for cp in sib_copies(buf, name, s):
                cp.wait_send()
    for j in range(1, 8):
        s0_copy(j).wait_send()
        sq_copy(j).wait_send()
        rs3_copy(j).wait_send()
    for k in range(5):
        for step in range(3):
            for cp in ex_copies(k, step):
                cp.wait_send()
    for name, bufs in (("st", (st_cx, st_y, st_z)), ("ga", (ga_cx, ga_y, ga_z))):
        for axis, buf in zip(("cx", "y", "z"), bufs):
            for j in range(1, size[axis]):
                exchange_copy(buf, name, axis, j).wait_send()
    for ch in range(4):
        core_copy(ch).wait_send()
        for cp in q1_copies(ch) + q2_copies(ch):
            cp.wait_send()
        for j in range(1, 4):
            rs2_copy(ch, j).wait_send()
    store_head.wait()


def finish(loss_ref, hidden_ref, gain_ref, head_ref, loss_out, hidden_out, gain_out, head_out):
    head_out[...] = head_ref[...]

    @pl.when(pl.program_id(0) == 0)
    def _():
        loss_out[...] = loss_ref[...]
        hidden_out[...] = hidden_ref[...].astype(bf16)
        for i in range(8):
            gain_out[:, 512 * i : 512 * i + 512] = gain_ref[i : i + 1, :]


def shards(
    teacher_hidden,
    teacher_gain,
    teacher_head,
    student_hidden,
    student_gain,
    student_head,
    token_ids,
):
    vmem = pl.BlockSpec(memory_space=pltpu.VMEM)
    hbm = pl.BlockSpec(memory_space=pl.ANY)
    block = pl.BlockSpec((1024, SLICE), lambda i: (i, 0))

    def whole(*shape):
        return pl.BlockSpec(shape, lambda i: (0, 0))

    row8 = (8, TOKENS)
    scratch = [
        ((2048, 2048), bf16), ((D_S, SLICE), bf16), ((SLICE, D_S), bf16), ((2, 8, 2, 16, 2048), bf16),
        ((128, 2048), bf16), ((4, 2, 256, SLICE), f32), ((4, 2, 256, SLICE), f32),
        ((4, 256, SLICE), f32), ((2, 256, SLICE), f32), ((2, 256, SLICE), f32),
        ((2, 2, 256, SLICE), f32), ((2, 2, 256, SLICE), f32), ((256, SLICE), f32),
        ((2, 8, 32, 128), f32), (row8, f32), ((7,) + row8, f32),
        ((8, 2, D_S), f32), ((16, D_S), f32), ((2, 8, 2, 16, D_S), bf16),
        ((2, 8, 32, SLICE), f32), ((TOKENS, SLICE), f32), ((TOKENS, 128), f32), ((8, 512), f32),
        ((8,) + row8, f32), ((4,) + row8, f32), ((8,) + row8, f32),
        ((8,) + row8, f32), ((4,) + row8, f32), ((8,) + row8, f32),
        ((TOKENS, SLICE), bf16), ((TOKENS, SLICE), bf16), ((TOKENS, TOKENS), bf16), ((D_S, SLICE), bf16),
        ((4, 256, WIDE), f32), ((4, 256, WIDE), bf16), ((4, 256, WIDE), bf16),
        ((4, 4, 4, 16, WIDE), bf16), ((4, 2, 2, 16, WIDE), bf16), ((4, 2, 4, 16, WIDE), bf16),
        ((4, 4, 16, WIDE), bf16), ((4, 3, 16, WIDE), bf16),
        ((8, 16, 512), f32), ((8, 16, 512), bf16), ((7, 16, 512), bf16), ((2, D_S), f32),
    ]
    loss, grad_head, grad_hidden, grad_gain = pl.pallas_call(
        kernel,
        out_shape=(
            jax.ShapeDtypeStruct((1, TOKENS), f32),
            jax.ShapeDtypeStruct((D_S, SLICE), bf16),
            jax.ShapeDtypeStruct((2, D_S), f32),
            jax.ShapeDtypeStruct((8, 512), f32),
        ),
        in_specs=[vmem, vmem, hbm, vmem, vmem, hbm, vmem],
        out_specs=(vmem, hbm, vmem, vmem),
        scratch_shapes=[pltpu.VMEM(shape, dtype) for shape, dtype in scratch]
        + [pltpu.SemaphoreType.DMA((N_SEMS,)), pltpu.SemaphoreType.DMA((N_SEMS,))],
        compiler_params=pltpu.CompilerParams(
            collective_id=0, has_side_effects=True, vmem_limit_bytes=56 * 1024 * 1024
        ),
        cost_estimate=pl.CostEstimate(
            flops=7_600_000_000, bytes_accessed=13_000_000, transcendentals=600_000
        ),
    )(
        teacher_hidden,
        teacher_gain,
        teacher_head,
        student_hidden,
        student_gain,
        student_head,
        token_ids.reshape(1, TOKENS),
    )
    loss, grad_hidden, grad_gain, grad_head = pl.pallas_call(
        finish,
        out_shape=(
            jax.ShapeDtypeStruct((1, TOKENS), f32),
            jax.ShapeDtypeStruct((2, D_S), bf16),
            jax.ShapeDtypeStruct((1, D_S), f32),
            jax.ShapeDtypeStruct((D_S, SLICE), bf16),
        ),
        grid=(4,),
        in_specs=[whole(1, TOKENS), whole(2, D_S), whole(8, 512), block],
        out_specs=(whole(1, TOKENS), whole(2, D_S), whole(1, D_S), block),
        compiler_params=pltpu.CompilerParams(vmem_limit_bytes=56 * 1024 * 1024),
    )(loss, grad_hidden, grad_gain, grad_head)
    return loss.reshape(TOKENS), grad_hidden, grad_gain.reshape(D_S), grad_head


def solution(mesh):
    in_specs = (
        P("tp", "dp"),
        P("dp"),
        P("dp", "tp"),
        P(("tp", "dp"), None),
        P(),
        P(None, ("tp", "dp")),
        P(),
    )
    out_specs = (P(), P(("tp", "dp"), None), P(), P(None, ("tp", "dp")))
    return jax.shard_map(shards, mesh=mesh, in_specs=in_specs, out_specs=out_specs, check_vma=False)
```

```python
import functools

import jax
import jax.numpy as jnp
from jax import lax
from jax.experimental import pallas as pl
from jax.experimental.pallas import tpu as pltpu
from jax.sharding import PartitionSpec as P

D_T = 16384
D_S = 4096
TOKENS = 512
SLICE = 256

epsilon = 1e-05
hard_weight = 0.5
loss_scale = 64.0

MESH = pl.DeviceIdType.MESH
f32 = jnp.float32
bf16 = jnp.bfloat16

CHUNK_ROWS = (32, 64, 64, 64, 32)
CHUNK_AT = (0, 32, 96, 160, 224)
ORDER = (0, 2, 1, 3)
WIDE = 1024


class Sems:
    def __init__(self):
        self.count = 0

    def take(self, n):
        at = self.count
        self.count += n
        return at


def layout():
    s = Sems()
    base = {}
    for name, n in (
        ("load", 3),
        ("t_yh", 1), ("t_r", 4), ("t_l", 4), ("t_s", 8),
        ("s_yh", 1), ("s_r", 8), ("s_l", 8), ("s_s", 8),
        ("s0", 8), ("ex", 50), ("sq", 8),
        ("st_cx", 8), ("st_y", 4), ("st_z", 8),
        ("ga_cx", 8), ("ga_y", 4), ("ga_z", 8),
        ("core", 4), ("q1", 8), ("q2", 8), ("rs2", 16), ("rs3", 8),
    ):
        base[name] = s.take(n)
    return base, s.count


BASE, N_SEMS = layout()


def kernel(
    th_ref, tg_ref, thead_hbm, sh_ref, sg_ref, shead_hbm, ids_ref,
    loss_ref, ghead_hbm, ghid_ref, ggain_ref,
    head, w, wt, h5, scaled, pa, pb, ya, xa1, xa2, xb1, xb2, yb, ssq, sqs, sqr,
    s0, s16, f5, t4, slog, stc, cols, idc,
    st_cx, st_y, st_z, ga_cx, ga_y, ga_z,
    gp, perm, gh, own, cs, cr, rs, q1, q2, s2, r2, zf, zb, r3, unfolded,
    ssem, rsem,
):
    tp = lax.axis_index("tp")
    dp = lax.axis_index("dp")
    c = tp % 2
    z = (tp // 2) % 8
    yh = tp // 16
    x = dp // 2
    yl = dp % 2
    y = yh * 2 + yl

    def dev(xx, yy, zz, cc):
        return ((yy // 2) * 16 + zz * 2 + cc, xx * 2 + yy % 2)

    def zmod(v):
        return (v + 16) % 8

    def peer(axis, j):
        if axis == "c":
            return dev(x, y, z, (c + j) % 2)
        if axis == "x":
            return dev((x + j) % 4, y, z, c)
        if axis == "y":
            return dev(x, (y + j) % 4, z, c)
        if axis == "cx":
            at = (x * 2 + c + j) % 8
            return dev(at // 2, y, z, at % 2)
        return dev(x, y, (z + j) % 8, c)

    size = {"cx": 8, "y": 4, "z": 8}
    mine = {"cx": x * 2 + c, "y": y, "z": z}

    def rc(src, dst, name, i, device):
        at = BASE[name] + i
        return pltpu.make_async_remote_copy(
            src_ref=src, dst_ref=dst, send_sem=ssem.at[at], recv_sem=rsem.at[at],
            device_id=device, device_id_type=MESH,
        )

    def arrived(dst, name, i):
        rc(dst, dst, name, i, peer("c", 1)).wait_recv()

    load_head = pltpu.make_async_copy(thead_hbm, head, ssem.at[BASE["load"]])
    load_w = pltpu.make_async_copy(shead_hbm, w, ssem.at[BASE["load"] + 1])
    load_w.start()
    load_head.start()

    barrier = pltpu.get_barrier_semaphore()
    partners = [peer("c", 1)]
    partners += [dev((x + j) % 4, y, z, cc) for j in range(1, 4) for cc in range(2)]
    partners += [peer("y", j) for j in range(1, 4)]
    partners += [dev((x + j) % 4, yh * 2 + 1 - yl, z, c) for j in range(1, 4)]
    partners += [peer("z", j) for j in range(1, 8)]
    for device in partners:
        pl.semaphore_signal(barrier, inc=1, device_id=device, device_id_type=MESH)

    h5[yh, z, c] = th_ref[...]
    s0[dp] = sh_ref[...].astype(f32)
    idc[...] = jnp.broadcast_to(ids_ref[...], (128, TOKENS)).T

    p = lax.broadcasted_iota(jnp.int32, (TOKENS, TOKENS), 0)
    q = lax.broadcasted_iota(jnp.int32, (TOKENS, TOKENS), 1)
    source = (
        ((p >> 5) & 1) * 256
        + ((p >> 1) & 7) * 32
        + (p >> 8) * 16
        + ((p >> 6) & 3) * 4
        + ((p >> 4) & 1) * 2
        + (p & 1)
    )
    perm[...] = jnp.where(q == source, 1.0, 0.0).astype(bf16)

    pl.semaphore_wait(barrier, len(partners))

    yh_peer = dev(x, (y + 2) % 4, z, c)
    sibling = peer("c", 1)
    right = peer("z", 1)
    left = peer("z", 7)

    y_outer = dev(x, 3 - y, z, c)

    def yh_copy(buf, name):
        own_block = buf.at[yh, z, c]
        return rc(own_block, own_block, name + "_yh", 0, yh_peer if name == "t" else y_outer)

    def ring_copies(buf, name, s):
        if s < 3:
            r, l = buf.at[:, zmod(z - s), c], buf.at[:, zmod(z + s), c]
        else:
            r, l = buf.at[0, zmod(z - s), c], buf.at[1, zmod(z + s), c]
        return rc(r, r, name + "_r", s, right), rc(l, l, name + "_l", s, left)

    def ring_arrived(buf, name, s):
        if s < 3:
            r, l = buf.at[:, zmod(z - 1 - s), c], buf.at[:, zmod(z + 1 + s), c]
        else:
            r, l = buf.at[0, zmod(z + 4), c], buf.at[1, zmod(z + 4), c]
        arrived(r, name + "_r", s)
        arrived(l, name + "_l", s)

    def half_copies(s, half):
        r, l = f5.at[half, zmod(z - s), c], f5.at[half, zmod(z + s), c]
        copies = []
        if s < 3 or half == 0:
            copies.append(rc(r, r, "s_r", 2 * s + half, right))
        if s < 3 or half == 1:
            copies.append(rc(l, l, "s_l", 2 * s + half, left))
        return copies

    def half_arrived(s, half):
        if s < 3 or half == 0:
            arrived(f5.at[half, zmod(z - 1 - s), c], "s_r", 2 * s + half)
        if s < 3 or half == 1:
            arrived(f5.at[half, zmod(z + 1 + s), c], "s_l", 2 * s + half)

    def student_step(s, half):
        half_arrived(s, half)
        if s < 3:
            for cp in half_copies(s + 1, half):
                cp.start()
        if half == 1:
            for cp in sib_copies(f5, "s", s + 1):
                cp.start()

    def units(s):
        if s == 0:
            return [(0, z)]
        if s == 4:
            return [(7, zmod(z + 4))]
        return [(2 * s - 1, zmod(z - s)), (2 * s, zmod(z + s))]

    def sib_copies(buf, name, s):
        return [
            rc(buf.at[:, zz, c], buf.at[:, zz, c], name + "_s", k, sibling) for k, zz in units(s)
        ]

    def sib_arrived(buf, name, s):
        for k, zz in units(s):
            arrived(buf.at[:, zz, 1 - c], name + "_s", k)

    yh_copy(h5, "t").start()

    def s0_copy(j):
        return rc(s0.at[dp], s0.at[dp], "s0", j, (tp, (dp + j) % 8))

    for j in range(1, 8):
        s0_copy(j).start()

    load_w.wait()

    def turn(i, carry):
        at = pl.ds(pl.multiple_of(i * 512, 512), 512)
        wt[:, at] = w[at, :].T
        return carry

    lax.fori_loop(0, 8, turn, 0)
    arrived(h5.at[1 - yh, z, c], "t_yh", 0)
    for cp in ring_copies(h5, "t", 0):
        cp.start()
    for cp in sib_copies(h5, "t", 0):
        cp.start()

    for j in range(1, 8):
        arrived(s0.at[(dp + 8 - j) % 8], "s0", j)
    for d in range(8):
        s16[2 * d : 2 * d + 2, :] = s0[d]
    wide = s16[...]
    inv16 = lax.rsqrt(jnp.sum(wide * wide, -1, keepdims=True) / D_S + epsilon)
    gain_row = sg_ref[...].astype(f32).reshape(1, D_S)
    f5[yh, z, c] = (wide * inv16 * gain_row).astype(bf16)
    yh_copy(f5, "s").start()

    tg = tg_ref[...].astype(f32).reshape(1, 2048)

    x_right = peer("x", 1)
    x_left = peer("x", 3)
    y_pair = dev(x, yh * 2 + 1 - yl, z, c)

    def span(k, part):
        at, n = CHUNK_AT[k], CHUNK_ROWS[k]
        return {"all": pl.ds(at, n), "r": pl.ds(at, n // 2), "l": pl.ds(at + n // 2, n // 2)}[part]

    def ex_copies(k, step, which="ab"):
        every, rows_r, rows_l = span(k, "all"), span(k, "r"), span(k, "l")
        a_y = (pa.at[:, 1, every], ya.at[:, every], 0, y_pair)
        a_x1r = (pa.at[2, 0, rows_r], xa1.at[0, rows_r], 1, x_right)
        a_x1l = (pa.at[2, 0, rows_l], xa1.at[1, rows_l], 2, x_left)
        a_x2r = (pa.at[1, 0, every], xa2.at[0, every], 3, x_right)
        a_x2l = (pa.at[3, 0, every], xa2.at[1, every], 4, x_left)
        b_x1r = (pb.at[2, :, rows_r], xb1.at[0, :, rows_r], 5, x_right)
        b_x1l = (pb.at[2, :, rows_l], xb1.at[1, :, rows_l], 6, x_left)
        b_x2r = (pb.at[1, :, every], xb2.at[0, :, every], 7, x_right)
        b_x2l = (pb.at[3, :, every], xb2.at[1, :, every], 8, x_left)
        b_y = (pb.at[0, 1, every], yb.at[every], 9, y_pair)
        steps = {
            "a": ((a_y,), (a_x1r, a_x1l), (a_x2r, a_x2l)),
            "b": ((b_x1r, b_x1l), (b_x2r, b_x2l), (b_y,)),
        }
        return [
            rc(src, dst, "ex", k * 10 + i, device)
            for part in which
            for src, dst, i, device in steps[part][step]
        ]

    def ex_arrived(k, step, which="ab"):
        for cp in ex_copies(k, step, which):
            cp.wait_recv()

    def ex_send(k, step, which):
        for cp in ex_copies(k, step, which):
            cp.start()

    def ex_second(k):
        every, rows_r, rows_l = span(k, "all"), span(k, "r"), span(k, "l")
        ex_arrived(k, 0, "b")
        pb[1, :, rows_r] += xb1[0, :, rows_r]
        pb[3, :, rows_l] += xb1[1, :, rows_l]
        ex_send(k, 1, "b")
        ex_arrived(k, 0, "a")
        pa[:, 0, every] += ya[:, every]
        ex_send(k, 1, "a")

    def ex_third(k):
        every, rows_r, rows_l = span(k, "all"), span(k, "r"), span(k, "l")
        ex_arrived(k, 1, "b")
        pb[0, :, every] += xb2[0, :, every] + xb2[1, :, every]
        ex_send(k, 2, "b")
        ex_arrived(k, 1, "a")
        pa[1, 0, rows_r] += xa1[0, rows_r]
        pa[3, 0, rows_l] += xa1[1, rows_l]
        ex_send(k, 2, "a")

    def teacher_chunk(k):
        for i, (_, zz) in enumerate(units(k)):
            for half in range(2):
                block = h5[half, zz].reshape(32, 2048).astype(f32)
                squares = block * block
                total = squares[:, 0:128]
                for lane in range(128, 2048, 128):
                    total = total + squares[:, lane : lane + 128]
                ssq[half, zz] = total
                at = CHUNK_ROWS[k] * half + 32 * i
                scaled[at : at + 32, :] = (block * tg).astype(bf16)
        m = CHUNK_ROWS[k]

        def product(xo, yo):
            d = ((x + xo) % 4) * 2 + (yl + yo) % 2
            columns = pl.ds(pl.multiple_of(d * SLICE, SLICE), SLICE)
            both = jnp.dot(scaled[0 : 2 * m, :], head[:, columns], preferred_element_type=f32)
            pa[xo, yo, CHUNK_AT[k] : CHUNK_AT[k] + m, :] = both[0:m]
            pb[xo, yo, CHUNK_AT[k] : CHUNK_AT[k] + m, :] = both[m : 2 * m]

        def other_y(xo, carry):
            product(xo, 1)
            return carry

        lax.fori_loop(0, 4, other_y, 0)
        ex_send(k, 0, "a")
        product(2, 0)
        ex_send(k, 0, "b")
        for xo in (1, 3, 0):
            product(xo, 0)

    load_head.wait()
    for s in range(4):
        ring_arrived(h5, "t", s)
        if s < 3:
            for cp in ring_copies(h5, "t", s + 1):
                cp.start()
        for cp in sib_copies(h5, "t", s + 1):
            cp.start()
        if s >= 2:
            student_step(0, s - 2)
        sib_arrived(h5, "t", s)
        teacher_chunk(s)
        if s == 0:
            arrived(f5.at[1 - yh, z, c], "s_yh", 0)
            for half in range(2):
                for cp in half_copies(0, half):
                    cp.start()
            for cp in sib_copies(f5, "s", 0):
                cp.start()
        if s >= 1:
            ex_second(s - 1)
        if s >= 2:
            ex_third(s - 2)
    student_step(1, 0)
    sib_arrived(h5, "t", 4)
    teacher_chunk(4)
    student_step(1, 1)

    sums = jnp.sum(ssq[...].reshape(TOKENS, 128).T, 0, keepdims=True)
    sqs[...] = jnp.broadcast_to(sums, (8, TOKENS))

    def sq_copy(j):
        return rc(sqs, sqr.at[j - 1], "sq", j, (tp, (dp + j) % 8))

    for j in range(1, 8):
        sq_copy(j).start()

    ex_second(3)
    ex_third(2)
    student_step(2, 0)
    ex_second(4)
    student_step(2, 1)
    ex_third(3)
    student_step(3, 0)
    ex_third(4)
    student_step(3, 1)
    for s in range(5):
        sib_arrived(f5, "s", s)

    for half in range(2):
        rows = f5[half].reshape(256, D_S)
        slog[half * 256 : half * 256 + 256, :] = jnp.dot(rows, w[...], preferred_element_type=f32)
    ids = jnp.concatenate([idc[...], idc[...]], axis=1)
    first = (tp * 8 + dp) * SLICE
    target_mask = ids == first + lax.broadcasted_iota(jnp.int32, (TOKENS, SLICE), 1)
    student = slog[...]
    s_top = jnp.max(student, -1, keepdims=True)
    s_total = jnp.sum(jnp.exp(student - s_top), -1, keepdims=True)
    target = jnp.sum(jnp.where(target_mask, student, 0.0), -1, keepdims=True)
    lane = lax.broadcasted_iota(jnp.int32, (TOKENS, 128), 1)
    stc[...] = jnp.where(
        lane == 3, s_top, jnp.where(lane == 4, s_total, jnp.where(lane == 5, target, 0.0))
    )

    for j in range(1, 8):
        arrived(sqr.at[j - 1], "sq", j)
    square_total = sqs[...]
    for j in range(7):
        square_total = square_total + sqr[j]
    t_inv = lax.rsqrt(square_total / D_T + epsilon)
    t_inv = jnp.broadcast_to(t_inv[0:1, :], (128, TOKENS)).T
    t_inv = jnp.concatenate([t_inv, t_inv], axis=1)
    for k in range(5):
        ex_arrived(k, 2)
        for i, (_, zz) in enumerate(units(k)):
            rows = pl.ds(CHUNK_AT[k] + 32 * i, 32)
            t4[0, zz] = pa[0, 0, rows] + xa2[0, rows] + xa2[1, rows]
            t4[1, zz] = pb[0, 0, rows] + yb[rows]
    teacher = t4[...].reshape(TOKENS, SLICE) * t_inv

    t_top = jnp.max(teacher, -1, keepdims=True)
    t_exp = jnp.exp(teacher - t_top)
    t_total = jnp.sum(t_exp, -1, keepdims=True)
    cross = jnp.sum(t_exp * (teacher - student), -1, keepdims=True)
    packed = jnp.where(
        lane == 0, t_top, jnp.where(lane == 1, t_total, jnp.where(lane == 2, cross, stc[...]))
    )
    stats = packed.T[0:8, :]

    def exchange(buf, name, axis, value):
        buf[mine[axis]] = value
        for j in range(1, size[axis]):
            exchange_copy(buf, name, axis, j).start()

    def exchange_copy(buf, name, axis, j):
        slot = buf.at[mine[axis]]
        return rc(slot, slot, name + "_" + axis, j, peer(axis, j))

    def exchanged(buf, name, axis):
        n = size[axis]
        for j in range(1, n):
            arrived(buf.at[(mine[axis] + n - j) % n], name + "_" + axis, j)
        return [buf[i] for i in range(n)]

    def merged(parts):
        t_m = functools.reduce(jnp.maximum, [p[0:1] for p in parts])
        s_m = functools.reduce(jnp.maximum, [p[3:4] for p in parts])
        t_s = c_s = s_s = tgt = 0.0
        for p in parts:
            t_f = jnp.exp(p[0:1] - t_m)
            s_f = jnp.exp(p[3:4] - s_m)
            t_s = t_s + p[1:2] * t_f
            c_s = c_s + p[2:3] * t_f
            s_s = s_s + p[4:5] * s_f
            tgt = tgt + p[5:6]
        row = lax.broadcasted_iota(jnp.int32, (8, TOKENS), 0)
        out = jnp.zeros((8, TOKENS), f32)
        for i, v in enumerate((t_m, t_s, c_s, s_m, s_s, tgt)):
            out = jnp.where(row == i, v, out)
        return out

    for axis, buf in (("cx", st_cx), ("y", st_y), ("z", st_z)):
        exchange(buf, "st", axis, stats)
        stats = merged(exchanged(buf, "st", axis))

    t_lse = stats[0:1] + jnp.log(stats[1:2])
    s_lse = stats[3:4] + jnp.log(stats[4:5])
    loss_ref[...] = (
        stats[2:3] / stats[1:2] - t_lse + s_lse + hard_weight * (s_lse - stats[5:6])
    )
    t_col = jnp.broadcast_to(t_lse, (128, TOKENS)).T
    s_col = jnp.broadcast_to(s_lse, (128, TOKENS)).T
    t_prob = jnp.exp(teacher - jnp.concatenate([t_col, t_col], axis=1))
    s_prob = jnp.exp(student - jnp.concatenate([s_col, s_col], axis=1))
    onehot = target_mask.astype(f32)
    g = (loss_scale * (s_prob - t_prob + hard_weight * (s_prob - onehot))).astype(bf16)

    gp[...] = jnp.dot(perm[...], g, preferred_element_type=f32).astype(bf16)

    def core_copy(ch):
        return rc(cs.at[ch], cr.at[ch], "core", ch, sibling)

    other_rows = pl.ds(pl.multiple_of((1 - c) * 256, 256), 256)
    own_rows = pl.ds(pl.multiple_of(c * 256, 256), 256)
    def product_of(rows, ch, tile):
        at = ch * WIDE + tile * 512
        return jnp.dot(gp[rows, :], wt[:, at : at + 512], preferred_element_type=f32)

    def other_part(ch):
        for tile in range(2):
            cs[ch, :, tile * 512 : tile * 512 + 512] = product_of(other_rows, ch, tile).astype(bf16)
        core_copy(ch).start()

    def own_part(ch):
        for tile in range(2):
            own[ch, :, tile * 512 : tile * 512 + 512] = product_of(own_rows, ch, tile)

    def shard(ch, o, part=slice(0, 4)):
        if ch < 2:
            return rs.at[ch, (x + o) % 4, part]
        return rs.at[ch, part, (y + o) % 4]

    y_right = peer("y", 1)
    y_left = peer("y", 3)

    def q1_copies(ch):
        r, l = (x_right, x_left) if ch < 2 else (y_right, y_left)
        return (
            rc(shard(ch, 2, slice(0, 2)), q1.at[ch, 0], "q1", ch * 2, r),
            rc(shard(ch, 2, slice(2, 4)), q1.at[ch, 1], "q1", ch * 2 + 1, l),
        )

    def q2_copies(ch):
        r, l = (x_right, x_left) if ch < 2 else (y_right, y_left)
        return (
            rc(shard(ch, 1), q2.at[ch, 0], "q2", ch * 2, r),
            rc(shard(ch, 3), q2.at[ch, 1], "q2", ch * 2 + 1, l),
        )

    other_part(ORDER[0])
    other_part(ORDER[1])
    for i, ch in enumerate(ORDER):
        own_part(ch)
        if i + 2 < 4:
            other_part(ORDER[i + 2])
        arrived(cr.at[ch], "core", ch)
        both = own[ch] + cr[ch].astype(f32)
        rs[ch] = both.astype(bf16).reshape(4, 4, 16, WIDE)
        for cp in q1_copies(ch):
            cp.start()
    for ch in ORDER:
        for cp in q1_copies(ch):
            cp.wait_recv()
        for o, part, way in ((1, slice(0, 2), 0), (3, slice(2, 4), 1)):
            ref = shard(ch, o, part)
            ref[...] = (ref[...].astype(f32) + q1[ch, way].astype(f32)).astype(bf16)
        for cp in q2_copies(ch):
            cp.start()

    turned = g.T

    def head_tile(i, carry):
        at = pl.ds(pl.multiple_of(i * 512, 512), 512)
        features = f5[:, :, :, :, at].reshape(TOKENS, 512)
        tile = jnp.dot(turned, features, preferred_element_type=f32)
        cols[pl.ds(i, 1), :] = jnp.sum(tile * wt[:, at].astype(f32), 0, keepdims=True)
        gh[at, :] = tile.astype(bf16).T
        return carry

    lax.fori_loop(0, 8, head_tile, 0)
    store_head = pltpu.make_async_copy(gh, ghead_hbm, ssem.at[BASE["load"] + 2])
    store_head.start()
    gain = cols[...]
    exchange(ga_cx, "ga", "cx", gain)

    def rs2_copy(ch, j):
        if ch < 2:
            return rc(s2.at[ch, (y + j) % 4], r2.at[ch, j - 1], "rs2", ch * 4 + j, peer("y", j))
        return rc(s2.at[ch, (x + j) % 4], r2.at[ch, j - 1], "rs2", ch * 4 + j, peer("x", j))

    for ch in ORDER:
        for cp in q2_copies(ch):
            cp.wait_recv()
        kept = shard(ch, 0)[...].astype(f32)
        total = kept + (q2[ch, 0].astype(f32) + q2[ch, 1].astype(f32))
        s2[ch] = total.astype(bf16)
        for j in range(1, 4):
            rs2_copy(ch, j).start()

    gain = functools.reduce(jnp.add, exchanged(ga_cx, "ga", "cx"))
    exchange(ga_y, "ga", "y", gain)

    for ch in ORDER:
        for j in range(1, 4):
            arrived(r2.at[ch, j - 1], "rs2", ch * 4 + j)
        kept = s2[ch, y] if ch < 2 else s2[ch, x]
        total = kept.astype(f32)
        for j in range(3):
            total = total + r2[ch, j].astype(f32)
        for zz in range(8):
            for half in range(2):
                at = 4 * ch + 2 * half
                zf[zz, at : at + 2, :] = total[2 * zz : 2 * zz + 2, 512 * half : 512 * half + 512]
    zb[...] = zf[...].astype(bf16)

    def rs3_copy(j):
        return rc(zb.at[(z + j) % 8], r3.at[j - 1], "rs3", j, peer("z", j))

    for j in range(1, 8):
        rs3_copy(j).start()

    gain = functools.reduce(jnp.add, exchanged(ga_y, "ga", "y"))
    exchange(ga_z, "ga", "z", gain)

    own_wide = sh_ref[...].astype(f32)
    own_inv = lax.rsqrt(jnp.sum(own_wide * own_wide, -1, keepdims=True) / D_S + epsilon)
    own_normed = own_wide * own_inv
    for j in range(1, 8):
        arrived(r3.at[j - 1], "rs3", j)
    folded = zf[z]
    for j in range(7):
        folded = folded + r3[j].astype(f32)
    for i in range(8):
        unfolded[:, 512 * i : 512 * i + 512] = folded[2 * i : 2 * i + 2, :]
    grad_normed = unfolded[...] * gain_row
    inner = jnp.sum(grad_normed * own_normed, -1, keepdims=True) / D_S
    ghid_ref[...] = own_inv * (grad_normed - own_normed * inner)

    gain = functools.reduce(jnp.add, exchanged(ga_z, "ga", "z"))
    row = lax.broadcasted_iota(jnp.int32, (8, 512), 0)
    gain_rows = jnp.ones((8, 512), f32)
    for i in range(8):
        gain_rows = jnp.where(row == i, gain_row[:, 512 * i : 512 * i + 512], gain_rows)
    ggain_ref[...] = gain / gain_rows

    for buf, name in ((h5, "t"), (f5, "s")):
        yh_copy(buf, name).wait_send()
        for s in range(4):
            copies = ring_copies(buf, name, s) if name == "t" else half_copies(s, 0) + half_copies(s, 1)
            for cp in copies:
                cp.wait_send()
        for s in range(5):
            for cp in sib_copies(buf, name, s):
                cp.wait_send()
    for j in range(1, 8):
        s0_copy(j).wait_send()
        sq_copy(j).wait_send()
        rs3_copy(j).wait_send()
    for k in range(5):
        for step in range(3):
            for cp in ex_copies(k, step):
                cp.wait_send()
    for name, bufs in (("st", (st_cx, st_y, st_z)), ("ga", (ga_cx, ga_y, ga_z))):
        for axis, buf in zip(("cx", "y", "z"), bufs):
            for j in range(1, size[axis]):
                exchange_copy(buf, name, axis, j).wait_send()
    for ch in range(4):
        core_copy(ch).wait_send()
        for cp in q1_copies(ch) + q2_copies(ch):
            cp.wait_send()
        for j in range(1, 4):
            rs2_copy(ch, j).wait_send()
    store_head.wait()


def finish(loss_ref, hidden_ref, gain_ref, head_ref, loss_out, hidden_out, gain_out, head_out):
    head_out[...] = head_ref[...]

    @pl.when(pl.program_id(0) == 0)
    def _():
        loss_out[...] = loss_ref[...]
        hidden_out[...] = hidden_ref[...].astype(bf16)
        for i in range(8):
            gain_out[:, 512 * i : 512 * i + 512] = gain_ref[i : i + 1, :]


def shards(
    teacher_hidden,
    teacher_gain,
    teacher_head,
    student_hidden,
    student_gain,
    student_head,
    token_ids,
):
    vmem = pl.BlockSpec(memory_space=pltpu.VMEM)
    hbm = pl.BlockSpec(memory_space=pl.ANY)
    block = pl.BlockSpec((2048, SLICE), lambda i: (i, 0))

    def whole(*shape):
        return pl.BlockSpec(shape, lambda i: (0, 0))

    row8 = (8, TOKENS)
    scratch = [
        ((2048, 2048), bf16), ((D_S, SLICE), bf16), ((SLICE, D_S), bf16), ((2, 8, 2, 16, 2048), bf16),
        ((128, 2048), bf16), ((4, 2, 256, SLICE), f32), ((4, 2, 256, SLICE), f32),
        ((4, 256, SLICE), f32), ((2, 256, SLICE), f32), ((2, 256, SLICE), f32),
        ((2, 2, 256, SLICE), f32), ((2, 2, 256, SLICE), f32), ((256, SLICE), f32),
        ((2, 8, 32, 128), f32), (row8, f32), ((7,) + row8, f32),
        ((8, 2, D_S), f32), ((16, D_S), f32), ((2, 8, 2, 16, D_S), bf16),
        ((2, 8, 32, SLICE), f32), ((TOKENS, SLICE), f32), ((TOKENS, 128), f32), ((8, 512), f32),
        ((TOKENS, 128), jnp.int32),
        ((8,) + row8, f32), ((4,) + row8, f32), ((8,) + row8, f32),
        ((8,) + row8, f32), ((4,) + row8, f32), ((8,) + row8, f32),
        ((TOKENS, SLICE), bf16), ((TOKENS, TOKENS), bf16), ((D_S, SLICE), bf16),
        ((4, 256, WIDE), f32), ((4, 256, WIDE), bf16), ((4, 256, WIDE), bf16),
        ((4, 4, 4, 16, WIDE), bf16), ((4, 2, 2, 16, WIDE), bf16), ((4, 2, 4, 16, WIDE), bf16),
        ((4, 4, 16, WIDE), bf16), ((4, 3, 16, WIDE), bf16),
        ((8, 16, 512), f32), ((8, 16, 512), bf16), ((7, 16, 512), bf16), ((2, D_S), f32),
    ]
    loss, grad_head, grad_hidden, grad_gain = pl.pallas_call(
        kernel,
        out_shape=(
            jax.ShapeDtypeStruct((1, TOKENS), f32),
            jax.ShapeDtypeStruct((D_S, SLICE), bf16),
            jax.ShapeDtypeStruct((2, D_S), f32),
            jax.ShapeDtypeStruct((8, 512), f32),
        ),
        in_specs=[vmem, vmem, hbm, vmem, vmem, hbm, vmem],
        out_specs=(vmem, hbm, vmem, vmem),
        scratch_shapes=[pltpu.VMEM(shape, dtype) for shape, dtype in scratch]
        + [pltpu.SemaphoreType.DMA((N_SEMS,)), pltpu.SemaphoreType.DMA((N_SEMS,))],
        compiler_params=pltpu.CompilerParams(
            collective_id=0, has_side_effects=True, vmem_limit_bytes=56 * 1024 * 1024
        ),
        cost_estimate=pl.CostEstimate(
            flops=7_600_000_000, bytes_accessed=13_000_000, transcendentals=600_000
        ),
    )(
        teacher_hidden,
        teacher_gain,
        teacher_head,
        student_hidden,
        student_gain,
        student_head,
        token_ids.reshape(1, TOKENS),
    )
    loss, grad_hidden, grad_gain, grad_head = pl.pallas_call(
        finish,
        out_shape=(
            jax.ShapeDtypeStruct((1, TOKENS), f32),
            jax.ShapeDtypeStruct((2, D_S), bf16),
            jax.ShapeDtypeStruct((1, D_S), f32),
            jax.ShapeDtypeStruct((D_S, SLICE), bf16),
        ),
        grid=(2,),
        in_specs=[whole(1, TOKENS), whole(2, D_S), whole(8, 512), block],
        out_specs=(whole(1, TOKENS), whole(2, D_S), whole(1, D_S), block),
        compiler_params=pltpu.CompilerParams(vmem_limit_bytes=56 * 1024 * 1024),
    )(loss, grad_hidden, grad_gain, grad_head)
    return loss.reshape(TOKENS), grad_hidden, grad_gain.reshape(D_S), grad_head


def solution(mesh):
    in_specs = (
        P("tp", "dp"),
        P("dp"),
        P("dp", "tp"),
        P(("tp", "dp"), None),
        P(),
        P(None, ("tp", "dp")),
        P(),
    )
    out_specs = (P(), P(("tp", "dp"), None), P(), P(None, ("tp", "dp")))
    return jax.shard_map(shards, mesh=mesh, in_specs=in_specs, out_specs=out_specs, check_vma=False)
```

```python
import functools

import jax
import jax.numpy as jnp
from jax import lax
from jax.experimental import pallas as pl
from jax.experimental.pallas import tpu as pltpu
from jax.sharding import PartitionSpec as P

D_T = 16384
D_S = 4096
TOKENS = 512
SLICE = 256

epsilon = 1e-05
hard_weight = 0.5
loss_scale = 64.0

MESH = pl.DeviceIdType.MESH
f32 = jnp.float32
bf16 = jnp.bfloat16

CHUNK_ROWS = (32, 64, 64, 64, 32)
CHUNK_AT = (0, 32, 96, 160, 224)
ORDER = (0, 2, 1, 3)
WIDE = 1024


class Sems:
    def __init__(self):
        self.count = 0

    def take(self, n):
        at = self.count
        self.count += n
        return at


def layout():
    s = Sems()
    base = {}
    for name, n in (
        ("load", 3),
        ("t_yh", 1), ("t_r", 4), ("t_l", 4), ("t_s", 8),
        ("s_yh", 1), ("s_r", 8), ("s_l", 8), ("s_s", 8),
        ("s0", 8), ("ex", 50), ("sq", 8),
        ("st_cx", 8), ("st_y", 4), ("st_z", 8),
        ("ga_cx", 8), ("ga_y", 4), ("ga_z", 8),
        ("wt", 1), ("gp", 1), ("q1", 8), ("q2", 8), ("rs2", 16), ("rs3", 8),
    ):
        base[name] = s.take(n)
    return base, s.count


BASE, N_SEMS = layout()


def kernel(
    th_ref, tg_ref, thead_hbm, sh_ref, sg_ref, shead_hbm, ids_ref,
    loss_ref, ghead_hbm, ghid_ref, ggain_ref,
    head, w, wt, h5, scaled, pa, pb, ya, xa1, xa2, xb1, xb2, yb, ssq, sqs, sqr,
    s0, s16, f5, t4, slog, cols,
    st_cx, st_y, st_z, ga_cx, ga_y, ga_z,
    gp, gr, perm, gh, rs, q1, q2, s2, r2, zf, zb, r3, unfolded,
    ssem, rsem,
):
    tp = lax.axis_index("tp")
    dp = lax.axis_index("dp")
    c = tp % 2
    z = (tp // 2) % 8
    yh = tp // 16
    x = dp // 2
    yl = dp % 2
    y = yh * 2 + yl

    def dev(xx, yy, zz, cc):
        return ((yy // 2) * 16 + zz * 2 + cc, xx * 2 + yy % 2)

    def zmod(v):
        return (v + 16) % 8

    def peer(axis, j):
        if axis == "c":
            return dev(x, y, z, (c + j) % 2)
        if axis == "x":
            return dev((x + j) % 4, y, z, c)
        if axis == "y":
            return dev(x, (y + j) % 4, z, c)
        if axis == "cx":
            at = (x * 2 + c + j) % 8
            return dev(at // 2, y, z, at % 2)
        return dev(x, y, (z + j) % 8, c)

    size = {"cx": 8, "y": 4, "z": 8}
    mine = {"cx": x * 2 + c, "y": y, "z": z}

    def rc(src, dst, name, i, device):
        at = BASE[name] + i
        return pltpu.make_async_remote_copy(
            src_ref=src, dst_ref=dst, send_sem=ssem.at[at], recv_sem=rsem.at[at],
            device_id=device, device_id_type=MESH,
        )

    def arrived(dst, name, i):
        rc(dst, dst, name, i, peer("c", 1)).wait_recv()

    load_head = pltpu.make_async_copy(thead_hbm, head, ssem.at[BASE["load"]])
    load_w = pltpu.make_async_copy(shead_hbm, w, ssem.at[BASE["load"] + 1])
    load_w.start()
    load_head.start()

    barrier = pltpu.get_barrier_semaphore()
    partners = [peer("c", 1)]
    partners += [dev((x + j) % 4, y, z, cc) for j in range(1, 4) for cc in range(2)]
    partners += [peer("y", j) for j in range(1, 4)]
    partners += [dev((x + j) % 4, yh * 2 + 1 - yl, z, c) for j in range(1, 4)]
    partners += [peer("z", j) for j in range(1, 8)]
    for device in partners:
        pl.semaphore_signal(barrier, inc=1, device_id=device, device_id_type=MESH)

    h5[yh, z, c] = th_ref[...]
    s0[dp] = sh_ref[...].astype(f32)

    p = lax.broadcasted_iota(jnp.int32, (TOKENS, TOKENS), 1)
    q = lax.broadcasted_iota(jnp.int32, (TOKENS, TOKENS), 0)
    source = (
        ((p >> 5) & 1) * 256
        + ((p >> 1) & 7) * 32
        + (p >> 8) * 16
        + ((p >> 6) & 3) * 4
        + ((p >> 4) & 1) * 2
        + (p & 1)
    )
    perm[...] = jnp.where(q == source, 1.0, 0.0).astype(bf16)

    pl.semaphore_wait(barrier, len(partners))

    yh_peer = dev(x, (y + 2) % 4, z, c)
    sibling = peer("c", 1)
    right = peer("z", 1)
    left = peer("z", 7)

    y_outer = dev(x, 3 - y, z, c)

    def yh_copy(buf, name):
        own_block = buf.at[yh, z, c]
        return rc(own_block, own_block, name + "_yh", 0, yh_peer if name == "t" else y_outer)

    def ring_copies(buf, name, s):
        if s < 3:
            r, l = buf.at[:, zmod(z - s), c], buf.at[:, zmod(z + s), c]
        else:
            r, l = buf.at[0, zmod(z - s), c], buf.at[1, zmod(z + s), c]
        return rc(r, r, name + "_r", s, right), rc(l, l, name + "_l", s, left)

    def ring_arrived(buf, name, s):
        if s < 3:
            r, l = buf.at[:, zmod(z - 1 - s), c], buf.at[:, zmod(z + 1 + s), c]
        else:
            r, l = buf.at[0, zmod(z + 4), c], buf.at[1, zmod(z + 4), c]
        arrived(r, name + "_r", s)
        arrived(l, name + "_l", s)

    def half_copies(s, half):
        r, l = f5.at[half, zmod(z - s), c], f5.at[half, zmod(z + s), c]
        copies = []
        if s < 3 or half == 0:
            copies.append(rc(r, r, "s_r", 2 * s + half, right))
        if s < 3 or half == 1:
            copies.append(rc(l, l, "s_l", 2 * s + half, left))
        return copies

    def half_arrived(s, half):
        if s < 3 or half == 0:
            arrived(f5.at[half, zmod(z - 1 - s), c], "s_r", 2 * s + half)
        if s < 3 or half == 1:
            arrived(f5.at[half, zmod(z + 1 + s), c], "s_l", 2 * s + half)

    def student_step(s, half):
        half_arrived(s, half)
        if s < 3:
            for cp in half_copies(s + 1, half):
                cp.start()
        if half == 1:
            for cp in sib_copies(f5, "s", s + 1):
                cp.start()

    def units(s):
        if s == 0:
            return [(0, z)]
        if s == 4:
            return [(7, zmod(z + 4))]
        return [(2 * s - 1, zmod(z - s)), (2 * s, zmod(z + s))]

    def sib_copies(buf, name, s):
        return [
            rc(buf.at[:, zz, c], buf.at[:, zz, c], name + "_s", k, sibling) for k, zz in units(s)
        ]

    def sib_arrived(buf, name, s):
        for k, zz in units(s):
            arrived(buf.at[:, zz, 1 - c], name + "_s", k)

    yh_copy(h5, "t").start()

    def s0_copy(j):
        return rc(s0.at[dp], s0.at[dp], "s0", j, (tp, (dp + j) % 8))

    for j in range(1, 8):
        s0_copy(j).start()

    load_w.wait()

    def turn(i, carry):
        at = pl.ds(pl.multiple_of(i * 512, 512), 512)
        wt[0:SLICE, at] = w[at, :].T
        return carry

    lax.fori_loop(0, 8, turn, 0)
    arrived(h5.at[1 - yh, z, c], "t_yh", 0)
    for cp in ring_copies(h5, "t", 0):
        cp.start()
    for cp in sib_copies(h5, "t", 0):
        cp.start()

    for j in range(1, 8):
        arrived(s0.at[(dp + 8 - j) % 8], "s0", j)
    for d in range(8):
        s16[2 * d : 2 * d + 2, :] = s0[d]
    wide = s16[...]
    inv16 = lax.rsqrt(jnp.sum(wide * wide, -1, keepdims=True) / D_S + epsilon)
    gain_row = sg_ref[...].astype(f32).reshape(1, D_S)
    f5[yh, z, c] = (wide * inv16 * gain_row).astype(bf16)
    yh_copy(f5, "s").start()

    tg = tg_ref[...].astype(f32).reshape(1, 2048)

    x_right = peer("x", 1)
    x_left = peer("x", 3)
    y_pair = dev(x, yh * 2 + 1 - yl, z, c)

    def span(k, part):
        at, n = CHUNK_AT[k], CHUNK_ROWS[k]
        return {"all": pl.ds(at, n), "r": pl.ds(at, n // 2), "l": pl.ds(at + n // 2, n // 2)}[part]

    def ex_copies(k, step, which="ab"):
        every, rows_r, rows_l = span(k, "all"), span(k, "r"), span(k, "l")
        a_y = (pa.at[:, 1, every], ya.at[:, every], 0, y_pair)
        a_x1r = (pa.at[2, 0, rows_r], xa1.at[0, rows_r], 1, x_right)
        a_x1l = (pa.at[2, 0, rows_l], xa1.at[1, rows_l], 2, x_left)
        a_x2r = (pa.at[1, 0, every], xa2.at[0, every], 3, x_right)
        a_x2l = (pa.at[3, 0, every], xa2.at[1, every], 4, x_left)
        b_x1r = (pb.at[2, :, rows_r], xb1.at[0, :, rows_r], 5, x_right)
        b_x1l = (pb.at[2, :, rows_l], xb1.at[1, :, rows_l], 6, x_left)
        b_x2r = (pb.at[1, :, every], xb2.at[0, :, every], 7, x_right)
        b_x2l = (pb.at[3, :, every], xb2.at[1, :, every], 8, x_left)
        b_y = (pb.at[0, 1, every], yb.at[every], 9, y_pair)
        steps = {
            "a": ((a_y,), (a_x1r, a_x1l), (a_x2r, a_x2l)),
            "b": ((b_x1r, b_x1l), (b_x2r, b_x2l), (b_y,)),
        }
        return [
            rc(src, dst, "ex", k * 10 + i, device)
            for part in which
            for src, dst, i, device in steps[part][step]
        ]

    def ex_arrived(k, step, which="ab"):
        for cp in ex_copies(k, step, which):
            cp.wait_recv()

    def ex_send(k, step, which):
        for cp in ex_copies(k, step, which):
            cp.start()

    def ex_second(k):
        every, rows_r, rows_l = span(k, "all"), span(k, "r"), span(k, "l")
        ex_arrived(k, 0, "b")
        pb[1, :, rows_r] += xb1[0, :, rows_r]
        pb[3, :, rows_l] += xb1[1, :, rows_l]
        ex_send(k, 1, "b")
        ex_arrived(k, 0, "a")
        pa[:, 0, every] += ya[:, every]
        ex_send(k, 1, "a")

    def ex_third(k):
        every, rows_r, rows_l = span(k, "all"), span(k, "r"), span(k, "l")
        ex_arrived(k, 1, "b")
        pb[0, :, every] += xb2[0, :, every] + xb2[1, :, every]
        ex_send(k, 2, "b")
        ex_arrived(k, 1, "a")
        pa[1, 0, rows_r] += xa1[0, rows_r]
        pa[3, 0, rows_l] += xa1[1, rows_l]
        ex_send(k, 2, "a")

    def teacher_chunk(k):
        for i, (_, zz) in enumerate(units(k)):
            for half in range(2):
                block = h5[half, zz].reshape(32, 2048).astype(f32)
                squares = block * block
                total = squares[:, 0:128]
                for lane in range(128, 2048, 128):
                    total = total + squares[:, lane : lane + 128]
                ssq[half, zz] = total
                at = CHUNK_ROWS[k] * half + 32 * i
                scaled[at : at + 32, :] = (block * tg).astype(bf16)
        m = CHUNK_ROWS[k]

        def product(xo, yo):
            d = ((x + xo) % 4) * 2 + (yl + yo) % 2
            columns = pl.ds(pl.multiple_of(d * SLICE, SLICE), SLICE)
            both = jnp.dot(scaled[0 : 2 * m, :], head[:, columns], preferred_element_type=f32)
            pa[xo, yo, CHUNK_AT[k] : CHUNK_AT[k] + m, :] = both[0:m]
            pb[xo, yo, CHUNK_AT[k] : CHUNK_AT[k] + m, :] = both[m : 2 * m]

        def other_y(xo, carry):
            product(xo, 1)
            return carry

        lax.fori_loop(0, 4, other_y, 0)
        ex_send(k, 0, "a")
        product(2, 0)
        ex_send(k, 0, "b")
        for xo in (1, 3, 0):
            product(xo, 0)

    load_head.wait()
    for s in range(4):
        ring_arrived(h5, "t", s)
        if s < 3:
            for cp in ring_copies(h5, "t", s + 1):
                cp.start()
        for cp in sib_copies(h5, "t", s + 1):
            cp.start()
        if s >= 2:
            student_step(0, s - 2)
        sib_arrived(h5, "t", s)
        teacher_chunk(s)
        if s == 0:
            arrived(f5.at[1 - yh, z, c], "s_yh", 0)
            for half in range(2):
                for cp in half_copies(0, half):
                    cp.start()
            for cp in sib_copies(f5, "s", 0):
                cp.start()
        if s >= 1:
            ex_second(s - 1)
        if s >= 2:
            ex_third(s - 2)
    student_step(1, 0)
    sib_arrived(h5, "t", 4)
    teacher_chunk(4)
    wt_copy = rc(wt.at[0:SLICE], wt.at[SLICE : 2 * SLICE], "wt", 0, sibling)
    wt_copy.start()
    student_step(1, 1)

    def fold(*rows):
        pieces = [v[:, 128 * i : 128 * i + 128] for v in rows for i in range(4)]
        row = lax.broadcasted_iota(jnp.int32, (8, 128), 0)
        out = jnp.zeros((8, 128), f32)
        for i, piece in enumerate(pieces):
            out = jnp.where(row == i, piece, out)
        return out

    def unfold(tile, first):
        return jnp.concatenate([tile[first + i : first + i + 1, :] for i in range(4)], axis=1)

    sqs[...] = fold(jnp.sum(ssq[...].reshape(TOKENS, 128).T, 0, keepdims=True))

    def sq_copy(j):
        return rc(sqs, sqr.at[j - 1], "sq", j, (tp, (dp + j) % 8))

    for j in range(1, 8):
        sq_copy(j).start()

    ex_second(3)
    ex_third(2)
    student_step(2, 0)
    ex_second(4)
    student_step(2, 1)
    ex_third(3)
    student_step(3, 0)
    ex_third(4)
    student_step(3, 1)
    for s in range(5):
        sib_arrived(f5, "s", s)

    for half in range(2):
        rows = f5[half].reshape(256, D_S)
        slog[:, half * 256 : half * 256 + 256] = jnp.dot(
            rows, w[...], preferred_element_type=f32
        ).T
    first = (tp * 8 + dp) * SLICE
    target_mask = ids_ref[...] == first + lax.broadcasted_iota(jnp.int32, (SLICE, TOKENS), 0)
    student = slog[...]
    s_top = jnp.max(student, 0, keepdims=True)
    s_total = jnp.sum(jnp.exp(student - s_top), 0, keepdims=True)
    target = jnp.sum(jnp.where(target_mask, student, 0.0), 0, keepdims=True)

    for j in range(1, 8):
        arrived(sqr.at[j - 1], "sq", j)
    square_total = sqs[...]
    for j in range(7):
        square_total = square_total + sqr[j]
    t_inv = unfold(lax.rsqrt(square_total / D_T + epsilon), 0)
    for k in range(5):
        ex_arrived(k, 2)
        for i, (_, zz) in enumerate(units(k)):
            rows = pl.ds(CHUNK_AT[k] + 32 * i, 32)
            t4[0, zz] = pa[0, 0, rows] + xa2[0, rows] + xa2[1, rows]
            t4[1, zz] = pb[0, 0, rows] + yb[rows]
    teacher = t4[...].reshape(TOKENS, SLICE).T * t_inv

    t_top = jnp.max(teacher, 0, keepdims=True)
    t_exp = jnp.exp(teacher - t_top)
    t_total = jnp.sum(t_exp, 0, keepdims=True)
    cross = jnp.sum(t_exp * (teacher - student), 0, keepdims=True)
    stats = (fold(t_top, s_top), fold(t_total, s_total), fold(cross, target))

    def exchange(buf, name, axis, value):
        if isinstance(value, tuple):
            for i, v in enumerate(value):
                buf[mine[axis], i] = v
        else:
            buf[mine[axis]] = value
        for j in range(1, size[axis]):
            exchange_copy(buf, name, axis, j).start()

    def exchange_copy(buf, name, axis, j):
        slot = buf.at[mine[axis]]
        return rc(slot, slot, name + "_" + axis, j, peer(axis, j))

    def exchanged(buf, name, axis):
        n = size[axis]
        for j in range(1, n):
            arrived(buf.at[(mine[axis] + n - j) % n], name + "_" + axis, j)
        return [buf[i] for i in range(n)]

    upper = lax.broadcasted_iota(jnp.int32, (8, 128), 0) < 4

    def merged(parts):
        top = functools.reduce(jnp.maximum, [p[0] for p in parts])
        total = other = 0.0
        for p in parts:
            factor = jnp.exp(p[0] - top)
            total = total + p[1] * factor
            other = other + p[2] * jnp.where(upper, factor, 1.0)
        return top, total, other

    for axis, buf in (("cx", st_cx), ("y", st_y), ("z", st_z)):
        exchange(buf, "st", axis, stats)
        stats = merged(exchanged(buf, "st", axis))

    top, total, other = stats
    lse = top + jnp.log(total)
    t_lse, s_lse = unfold(lse, 0), unfold(lse, 4)
    cross_mean, target = unfold(other / total, 0), unfold(other, 4)
    loss_ref[...] = cross_mean - t_lse + s_lse + hard_weight * (s_lse - target)
    t_prob = jnp.exp(teacher - t_lse)
    s_prob = jnp.exp(student - s_lse)
    onehot = target_mask.astype(f32)
    g = (loss_scale * (s_prob - t_prob + hard_weight * (s_prob - onehot))).astype(bf16)

    gp[...] = jnp.dot(g, perm[...], preferred_element_type=f32).astype(bf16).T

    other_rows = pl.ds(pl.multiple_of((1 - c) * 256, 256), 256)
    own_rows = pl.ds(pl.multiple_of(c * 256, 256), 256)
    gp_copy = rc(gp.at[other_rows], gr, "gp", 0, sibling)
    gp_copy.start()

    def shard(ch, o, part=slice(0, 4)):
        if ch < 2:
            return rs.at[ch, (x + o) % 4, part]
        return rs.at[ch, part, (y + o) % 4]

    y_right = peer("y", 1)
    y_left = peer("y", 3)

    def q1_copies(ch):
        r, l = (x_right, x_left) if ch < 2 else (y_right, y_left)
        return (
            rc(shard(ch, 2, slice(0, 2)), q1.at[ch, 0], "q1", ch * 2, r),
            rc(shard(ch, 2, slice(2, 4)), q1.at[ch, 1], "q1", ch * 2 + 1, l),
        )

    def q2_copies(ch):
        r, l = (x_right, x_left) if ch < 2 else (y_right, y_left)
        return (
            rc(shard(ch, 1), q2.at[ch, 0], "q2", ch * 2, r),
            rc(shard(ch, 3), q2.at[ch, 1], "q2", ch * 2 + 1, l),
        )

    arrived(wt.at[SLICE : 2 * SLICE], "wt", 0)
    arrived(gr, "gp", 0)
    both_slices = jnp.concatenate([gp[own_rows, :], gr[...]], axis=1)
    for ch in ORDER:
        for tile in range(2):
            at = ch * WIDE + tile * 512
            product = jnp.dot(both_slices, wt[:, at : at + 512], preferred_element_type=f32)
            rs[ch, :, :, :, tile * 512 : tile * 512 + 512] = product.astype(bf16).reshape(
                4, 4, 16, 512
            )
        for cp in q1_copies(ch):
            cp.start()
    for ch in ORDER:
        for cp in q1_copies(ch):
            cp.wait_recv()
        for o, part, way in ((1, slice(0, 2), 0), (3, slice(2, 4), 1)):
            ref = shard(ch, o, part)
            ref[...] = (ref[...].astype(f32) + q1[ch, way].astype(f32)).astype(bf16)
        for cp in q2_copies(ch):
            cp.start()

    def head_tile(i, carry):
        at = pl.ds(pl.multiple_of(i * 512, 512), 512)
        features = f5[:, :, :, :, at].reshape(TOKENS, 512)
        tile = jnp.dot(g, features, preferred_element_type=f32)
        cols[pl.ds(i, 1), :] = jnp.sum(tile * wt[0:SLICE, at].astype(f32), 0, keepdims=True)
        gh[at, :] = tile.astype(bf16).T
        return carry

    lax.fori_loop(0, 8, head_tile, 0)
    store_head = pltpu.make_async_copy(gh, ghead_hbm, ssem.at[BASE["load"] + 2])
    store_head.start()
    gain = cols[...]
    exchange(ga_cx, "ga", "cx", gain)

    def rs2_copy(ch, j):
        if ch < 2:
            return rc(s2.at[ch, (y + j) % 4], r2.at[ch, j - 1], "rs2", ch * 4 + j, peer("y", j))
        return rc(s2.at[ch, (x + j) % 4], r2.at[ch, j - 1], "rs2", ch * 4 + j, peer("x", j))

    for ch in ORDER:
        for cp in q2_copies(ch):
            cp.wait_recv()
        kept = shard(ch, 0)[...].astype(f32)
        total = kept + (q2[ch, 0].astype(f32) + q2[ch, 1].astype(f32))
        s2[ch] = total.astype(bf16)
        for j in range(1, 4):
            rs2_copy(ch, j).start()

    gain = functools.reduce(jnp.add, exchanged(ga_cx, "ga", "cx"))
    exchange(ga_y, "ga", "y", gain)

    for ch in ORDER:
        for j in range(1, 4):
            arrived(r2.at[ch, j - 1], "rs2", ch * 4 + j)
        kept = s2[ch, y] if ch < 2 else s2[ch, x]
        total = kept.astype(f32)
        for j in range(3):
            total = total + r2[ch, j].astype(f32)
        for zz in range(8):
            for half in range(2):
                at = 4 * ch + 2 * half
                zf[zz, at : at + 2, :] = total[2 * zz : 2 * zz + 2, 512 * half : 512 * half + 512]
    zb[...] = zf[...].astype(bf16)

    def rs3_copy(j):
        return rc(zb.at[(z + j) % 8], r3.at[j - 1], "rs3", j, peer("z", j))

    for j in range(1, 8):
        rs3_copy(j).start()

    gain = functools.reduce(jnp.add, exchanged(ga_y, "ga", "y"))
    exchange(ga_z, "ga", "z", gain)

    own_wide = sh_ref[...].astype(f32)
    own_inv = lax.rsqrt(jnp.sum(own_wide * own_wide, -1, keepdims=True) / D_S + epsilon)
    own_normed = own_wide * own_inv
    for j in range(1, 8):
        arrived(r3.at[j - 1], "rs3", j)
    folded = zf[z]
    for j in range(7):
        folded = folded + r3[j].astype(f32)
    for i in range(8):
        unfolded[:, 512 * i : 512 * i + 512] = folded[2 * i : 2 * i + 2, :]
    grad_normed = unfolded[...] * gain_row
    inner = jnp.sum(grad_normed * own_normed, -1, keepdims=True) / D_S
    ghid_ref[...] = own_inv * (grad_normed - own_normed * inner)

    gain = functools.reduce(jnp.add, exchanged(ga_z, "ga", "z"))
    row = lax.broadcasted_iota(jnp.int32, (8, 512), 0)
    gain_rows = jnp.ones((8, 512), f32)
    for i in range(8):
        gain_rows = jnp.where(row == i, gain_row[:, 512 * i : 512 * i + 512], gain_rows)
    ggain_ref[...] = gain / gain_rows

    for buf, name in ((h5, "t"), (f5, "s")):
        yh_copy(buf, name).wait_send()
        for s in range(4):
            copies = ring_copies(buf, name, s) if name == "t" else half_copies(s, 0) + half_copies(s, 1)
            for cp in copies:
                cp.wait_send()
        for s in range(5):
            for cp in sib_copies(buf, name, s):
                cp.wait_send()
    for j in range(1, 8):
        s0_copy(j).wait_send()
        sq_copy(j).wait_send()
        rs3_copy(j).wait_send()
    for k in range(5):
        for step in range(3):
            for cp in ex_copies(k, step):
                cp.wait_send()
    for name, bufs in (("st", (st_cx, st_y, st_z)), ("ga", (ga_cx, ga_y, ga_z))):
        for axis, buf in zip(("cx", "y", "z"), bufs):
            for j in range(1, size[axis]):
                exchange_copy(buf, name, axis, j).wait_send()
    for ch in range(4):
        for cp in q1_copies(ch) + q2_copies(ch):
            cp.wait_send()
        for j in range(1, 4):
            rs2_copy(ch, j).wait_send()
    wt_copy.wait_send()
    gp_copy.wait_send()
    store_head.wait()


def finish(loss_ref, hidden_ref, gain_ref, head_ref, loss_out, hidden_out, gain_out, head_out):
    head_out[...] = head_ref[...]

    @pl.when(pl.program_id(0) == 0)
    def _():
        loss_out[...] = loss_ref[...]
        hidden_out[...] = hidden_ref[...].astype(bf16)
        for i in range(8):
            gain_out[:, 512 * i : 512 * i + 512] = gain_ref[i : i + 1, :]


def shards(
    teacher_hidden,
    teacher_gain,
    teacher_head,
    student_hidden,
    student_gain,
    student_head,
    token_ids,
):
    vmem = pl.BlockSpec(memory_space=pltpu.VMEM)
    hbm = pl.BlockSpec(memory_space=pl.ANY)
    block = pl.BlockSpec((2048, SLICE), lambda i: (i, 0))

    def whole(*shape):
        return pl.BlockSpec(shape, lambda i: (0, 0))

    row8 = (8, TOKENS)
    scratch = [
        ((2048, 2048), bf16), ((D_S, SLICE), bf16), ((2 * SLICE, D_S), bf16), ((2, 8, 2, 16, 2048), bf16),
        ((128, 2048), bf16), ((4, 2, 256, SLICE), f32), ((4, 2, 256, SLICE), f32),
        ((4, 256, SLICE), f32), ((2, 256, SLICE), f32), ((2, 256, SLICE), f32),
        ((2, 2, 256, SLICE), f32), ((2, 2, 256, SLICE), f32), ((256, SLICE), f32),
        ((2, 8, 32, 128), f32), ((8, 128), f32), ((7, 8, 128), f32),
        ((8, 2, D_S), f32), ((16, D_S), f32), ((2, 8, 2, 16, D_S), bf16),
        ((2, 8, 32, SLICE), f32), ((SLICE, TOKENS), f32), ((8, 512), f32),
        ((8, 3, 8, 128), f32), ((4, 3, 8, 128), f32), ((8, 3, 8, 128), f32),
        ((8,) + row8, f32), ((4,) + row8, f32), ((8,) + row8, f32),
        ((TOKENS, SLICE), bf16), ((256, SLICE), bf16), ((TOKENS, TOKENS), bf16), ((D_S, SLICE), bf16),
        ((4, 4, 4, 16, WIDE), bf16), ((4, 2, 2, 16, WIDE), bf16), ((4, 2, 4, 16, WIDE), bf16),
        ((4, 4, 16, WIDE), bf16), ((4, 3, 16, WIDE), bf16),
        ((8, 16, 512), f32), ((8, 16, 512), bf16), ((7, 16, 512), bf16), ((2, D_S), f32),
    ]
    loss, grad_head, grad_hidden, grad_gain = pl.pallas_call(
        kernel,
        out_shape=(
            jax.ShapeDtypeStruct((1, TOKENS), f32),
            jax.ShapeDtypeStruct((D_S, SLICE), bf16),
            jax.ShapeDtypeStruct((2, D_S), f32),
            jax.ShapeDtypeStruct((8, 512), f32),
        ),
        in_specs=[vmem, vmem, hbm, vmem, vmem, hbm, vmem],
        out_specs=(vmem, hbm, vmem, vmem),
        scratch_shapes=[pltpu.VMEM(shape, dtype) for shape, dtype in scratch]
        + [pltpu.SemaphoreType.DMA((N_SEMS,)), pltpu.SemaphoreType.DMA((N_SEMS,))],
        compiler_params=pltpu.CompilerParams(
            collective_id=0, has_side_effects=True, vmem_limit_bytes=56 * 1024 * 1024
        ),
        cost_estimate=pl.CostEstimate(
            flops=7_600_000_000, bytes_accessed=13_000_000, transcendentals=600_000
        ),
    )(
        teacher_hidden,
        teacher_gain,
        teacher_head,
        student_hidden,
        student_gain,
        student_head,
        token_ids.reshape(1, TOKENS),
    )
    loss, grad_hidden, grad_gain, grad_head = pl.pallas_call(
        finish,
        out_shape=(
            jax.ShapeDtypeStruct((1, TOKENS), f32),
            jax.ShapeDtypeStruct((2, D_S), bf16),
            jax.ShapeDtypeStruct((1, D_S), f32),
            jax.ShapeDtypeStruct((D_S, SLICE), bf16),
        ),
        grid=(2,),
        in_specs=[whole(1, TOKENS), whole(2, D_S), whole(8, 512), block],
        out_specs=(whole(1, TOKENS), whole(2, D_S), whole(1, D_S), block),
        compiler_params=pltpu.CompilerParams(vmem_limit_bytes=56 * 1024 * 1024),
    )(loss, grad_hidden, grad_gain, grad_head)
    return loss.reshape(TOKENS), grad_hidden, grad_gain.reshape(D_S), grad_head


def solution(mesh):
    in_specs = (
        P("tp", "dp"),
        P("dp"),
        P("dp", "tp"),
        P(("tp", "dp"), None),
        P(),
        P(None, ("tp", "dp")),
        P(),
    )
    out_specs = (P(), P(("tp", "dp"), None), P(), P(None, ("tp", "dp")))
    return jax.shard_map(shards, mesh=mesh, in_specs=in_specs, out_specs=out_specs, check_vma=False)
```

```python
import functools

import jax
import jax.numpy as jnp
from jax import lax
from jax.experimental import pallas as pl
from jax.experimental.pallas import tpu as pltpu
from jax.sharding import PartitionSpec as P

D_T = 16384
D_S = 4096
TOKENS = 512
SLICE = 256

epsilon = 1e-05
hard_weight = 0.5
loss_scale = 64.0

MESH = pl.DeviceIdType.MESH
f32 = jnp.float32
bf16 = jnp.bfloat16

CHUNK_ROWS = (32, 64, 64, 64, 32)
CHUNK_AT = (0, 32, 96, 160, 224)
ORDER = (0, 2, 1, 3)
WIDE = 1024


FRONT = (
    ("tstep", 0), ("tchunk", 0), ("sstart",), ("tchunk", 1), ("b2", 0), ("tstep", 1),
    ("a2", 0), ("b2", 1), ("b3", 0), ("sstep", 0, 0), ("tchunk", 2), ("a2", 1), ("a3", 0),
    ("tstep", 2), ("sstep", 0, 1), ("b2", 2), ("sstep", 1, 0), ("tchunk", 3), ("a3", 1),
    ("a2", 2), ("tstep", 3), ("sstep", 1, 1), ("b2", 3), ("tchunk", 4), ("b3", 1), ("fin", 0),
    ("b3", 2), ("sstep", 2, 0), ("sq",), ("a3", 2), ("a2", 3), ("sstep", 2, 1), ("slog", 0),
    ("b2", 4), ("b3", 3), ("a2", 4), ("sstep", 3, 0), ("a3", 3), ("sstep", 3, 1), ("fin", 2),
    ("b3", 4), ("a3", 4), ("slog", 1), ("fin", 1), ("fin", 3), ("slog", 2), ("fin", 4),
)
PIECES = ((0, 1), (2,), (3, 4))


class Sems:
    def __init__(self):
        self.count = 0

    def take(self, n):
        at = self.count
        self.count += n
        return at


def layout():
    s = Sems()
    base = {}
    for name, n in (
        ("load", 3),
        ("t_yh", 1), ("t_r", 4), ("t_l", 4), ("t_s", 8),
        ("s_yh", 1), ("s_r", 8), ("s_l", 8), ("s_s", 8),
        ("s0", 8), ("ex", 50), ("sq", 8),
        ("st_cx", 8), ("st_y", 4), ("st_z", 8),
        ("ga_cx", 8), ("ga_y", 4), ("ga_z", 8),
        ("wt", 1), ("gp", 1), ("q1", 8), ("q2", 8), ("rs2", 16), ("rs3", 8),
    ):
        base[name] = s.take(n)
    return base, s.count


BASE, N_SEMS = layout()


def kernel(
    th_ref, tg_ref, thead_hbm, sh_ref, sg_ref, shead_hbm, ids_ref,
    loss_ref, ghead_hbm, ghid_ref, ggain_ref,
    head, w, wt, h5, scaled, pa, pb, ya, xa1, xa2, xb1, xb2, yb, ssq, sqs, sqr,
    s0, s16, f5, t4, s4, cols,
    st_cx, st_y, st_z, ga_cx, ga_y, ga_z,
    gp, gr, perm, gh, rs, q1, q2, s2, r2, zf, zb, r3, unfolded,
    ssem, rsem,
):
    tp = lax.axis_index("tp")
    dp = lax.axis_index("dp")
    c = tp % 2
    z = (tp // 2) % 8
    yh = tp // 16
    x = dp // 2
    yl = dp % 2
    y = yh * 2 + yl

    def dev(xx, yy, zz, cc):
        return ((yy // 2) * 16 + zz * 2 + cc, xx * 2 + yy % 2)

    def zmod(v):
        return (v + 16) % 8

    def peer(axis, j):
        if axis == "c":
            return dev(x, y, z, (c + j) % 2)
        if axis == "x":
            return dev((x + j) % 4, y, z, c)
        if axis == "y":
            return dev(x, (y + j) % 4, z, c)
        if axis == "cx":
            at = (x * 2 + c + j) % 8
            return dev(at // 2, y, z, at % 2)
        return dev(x, y, (z + j) % 8, c)

    size = {"cx": 8, "y": 4, "z": 8}
    mine = {"cx": x * 2 + c, "y": y, "z": z}

    def rc(src, dst, name, i, device):
        at = BASE[name] + i
        return pltpu.make_async_remote_copy(
            src_ref=src, dst_ref=dst, send_sem=ssem.at[at], recv_sem=rsem.at[at],
            device_id=device, device_id_type=MESH,
        )

    def arrived(dst, name, i):
        rc(dst, dst, name, i, peer("c", 1)).wait_recv()

    load_head = pltpu.make_async_copy(thead_hbm, head, ssem.at[BASE["load"]])
    load_w = pltpu.make_async_copy(shead_hbm, w, ssem.at[BASE["load"] + 1])
    load_w.start()
    load_head.start()

    barrier = pltpu.get_barrier_semaphore()
    partners = [peer("c", 1)]
    partners += [dev((x + j) % 4, y, z, cc) for j in range(1, 4) for cc in range(2)]
    partners += [peer("y", j) for j in range(1, 4)]
    partners += [dev((x + j) % 4, yh * 2 + 1 - yl, z, c) for j in range(1, 4)]
    partners += [peer("z", j) for j in range(1, 8)]
    for device in partners:
        pl.semaphore_signal(barrier, inc=1, device_id=device, device_id_type=MESH)

    h5[yh, z, c] = th_ref[...]
    s0[dp] = sh_ref[...].astype(f32)

    p = lax.broadcasted_iota(jnp.int32, (TOKENS, TOKENS), 1)
    q = lax.broadcasted_iota(jnp.int32, (TOKENS, TOKENS), 0)
    source = (
        ((p >> 5) & 1) * 256
        + ((p >> 1) & 7) * 32
        + (p >> 8) * 16
        + ((p >> 6) & 3) * 4
        + ((p >> 4) & 1) * 2
        + (p & 1)
    )
    perm[...] = jnp.where(q == source, 1.0, 0.0).astype(bf16)

    pl.semaphore_wait(barrier, len(partners))

    yh_peer = dev(x, (y + 2) % 4, z, c)
    sibling = peer("c", 1)
    right = peer("z", 1)
    left = peer("z", 7)

    y_outer = dev(x, 3 - y, z, c)

    def yh_copy(buf, name):
        own_block = buf.at[yh, z, c]
        return rc(own_block, own_block, name + "_yh", 0, yh_peer if name == "t" else y_outer)

    def ring_copies(buf, name, s):
        if s < 3:
            r, l = buf.at[:, zmod(z - s), c], buf.at[:, zmod(z + s), c]
        else:
            r, l = buf.at[0, zmod(z - s), c], buf.at[1, zmod(z + s), c]
        return rc(r, r, name + "_r", s, right), rc(l, l, name + "_l", s, left)

    def ring_arrived(buf, name, s):
        if s < 3:
            r, l = buf.at[:, zmod(z - 1 - s), c], buf.at[:, zmod(z + 1 + s), c]
        else:
            r, l = buf.at[0, zmod(z + 4), c], buf.at[1, zmod(z + 4), c]
        arrived(r, name + "_r", s)
        arrived(l, name + "_l", s)

    def half_copies(s, half):
        r, l = f5.at[half, zmod(z - s), c], f5.at[half, zmod(z + s), c]
        copies = []
        if s < 3 or half == 0:
            copies.append(rc(r, r, "s_r", 2 * s + half, right))
        if s < 3 or half == 1:
            copies.append(rc(l, l, "s_l", 2 * s + half, left))
        return copies

    def half_arrived(s, half):
        if s < 3 or half == 0:
            arrived(f5.at[half, zmod(z - 1 - s), c], "s_r", 2 * s + half)
        if s < 3 or half == 1:
            arrived(f5.at[half, zmod(z + 1 + s), c], "s_l", 2 * s + half)

    def student_step(s, half):
        half_arrived(s, half)
        if s < 3:
            for cp in half_copies(s + 1, half):
                cp.start()
        if half == 1:
            for cp in sib_copies(f5, "s", s + 1):
                cp.start()

    def units(s):
        if s == 0:
            return [(0, z)]
        if s == 4:
            return [(7, zmod(z + 4))]
        return [(2 * s - 1, zmod(z - s)), (2 * s, zmod(z + s))]

    def sib_copies(buf, name, s):
        return [
            rc(buf.at[:, zz, c], buf.at[:, zz, c], name + "_s", k, sibling) for k, zz in units(s)
        ]

    def sib_arrived(buf, name, s):
        for k, zz in units(s):
            arrived(buf.at[:, zz, 1 - c], name + "_s", k)

    yh_copy(h5, "t").start()

    def s0_copy(j):
        return rc(s0.at[dp], s0.at[dp], "s0", j, (tp, (dp + j) % 8))

    for j in range(1, 8):
        s0_copy(j).start()

    load_w.wait()

    def turn(i, carry):
        at = pl.ds(pl.multiple_of(i * 512, 512), 512)
        wt[0:SLICE, at] = w[at, :].T
        return carry

    lax.fori_loop(0, 8, turn, 0)
    arrived(h5.at[1 - yh, z, c], "t_yh", 0)
    for cp in ring_copies(h5, "t", 0):
        cp.start()
    for cp in sib_copies(h5, "t", 0):
        cp.start()

    for j in range(1, 8):
        arrived(s0.at[(dp + 8 - j) % 8], "s0", j)
    for d in range(8):
        s16[2 * d : 2 * d + 2, :] = s0[d]
    wide = s16[...]
    inv16 = lax.rsqrt(jnp.sum(wide * wide, -1, keepdims=True) / D_S + epsilon)
    gain_row = sg_ref[...].astype(f32).reshape(1, D_S)
    f5[yh, z, c] = (wide * inv16 * gain_row).astype(bf16)
    yh_copy(f5, "s").start()

    tg = tg_ref[...].astype(f32).reshape(1, 2048)

    x_right = peer("x", 1)
    x_left = peer("x", 3)
    y_pair = dev(x, yh * 2 + 1 - yl, z, c)

    def span(k, part):
        at, n = CHUNK_AT[k], CHUNK_ROWS[k]
        return {"all": pl.ds(at, n), "r": pl.ds(at, n // 2), "l": pl.ds(at + n // 2, n // 2)}[part]

    def ex_copies(k, step, which="ab"):
        every, rows_r, rows_l = span(k, "all"), span(k, "r"), span(k, "l")
        a_y = (pa.at[:, 1, every], ya.at[:, every], 0, y_pair)
        a_x1r = (pa.at[2, 0, rows_r], xa1.at[0, rows_r], 1, x_right)
        a_x1l = (pa.at[2, 0, rows_l], xa1.at[1, rows_l], 2, x_left)
        a_x2r = (pa.at[1, 0, every], xa2.at[0, every], 3, x_right)
        a_x2l = (pa.at[3, 0, every], xa2.at[1, every], 4, x_left)
        b_x1r = (pb.at[2, :, rows_r], xb1.at[0, :, rows_r], 5, x_right)
        b_x1l = (pb.at[2, :, rows_l], xb1.at[1, :, rows_l], 6, x_left)
        b_x2r = (pb.at[1, :, every], xb2.at[0, :, every], 7, x_right)
        b_x2l = (pb.at[3, :, every], xb2.at[1, :, every], 8, x_left)
        b_y = (pb.at[0, 1, every], yb.at[every], 9, y_pair)
        steps = {
            "a": ((a_y,), (a_x1r, a_x1l), (a_x2r, a_x2l)),
            "b": ((b_x1r, b_x1l), (b_x2r, b_x2l), (b_y,)),
        }
        return [
            rc(src, dst, "ex", k * 10 + i, device)
            for part in which
            for src, dst, i, device in steps[part][step]
        ]

    def ex_arrived(k, step, which="ab"):
        for cp in ex_copies(k, step, which):
            cp.wait_recv()

    def ex_send(k, step, which):
        for cp in ex_copies(k, step, which):
            cp.start()

    def b2(k):
        rows_r, rows_l = span(k, "r"), span(k, "l")
        ex_arrived(k, 0, "b")
        pb[1, :, rows_r] += xb1[0, :, rows_r]
        pb[3, :, rows_l] += xb1[1, :, rows_l]
        ex_send(k, 1, "b")

    def a2(k):
        every = span(k, "all")
        ex_arrived(k, 0, "a")
        pa[:, 0, every] += ya[:, every]
        ex_send(k, 1, "a")

    def b3(k):
        every = span(k, "all")
        ex_arrived(k, 1, "b")
        pb[0, :, every] += xb2[0, :, every] + xb2[1, :, every]
        ex_send(k, 2, "b")

    def a3(k):
        rows_r, rows_l = span(k, "r"), span(k, "l")
        ex_arrived(k, 1, "a")
        pa[1, 0, rows_r] += xa1[0, rows_r]
        pa[3, 0, rows_l] += xa1[1, rows_l]
        ex_send(k, 2, "a")

    def fin(k):
        ex_arrived(k, 2)
        for i, (_, zz) in enumerate(units(k)):
            rows = pl.ds(CHUNK_AT[k] + 32 * i, 32)
            t4[0, zz] = pa[0, 0, rows] + xa2[0, rows] + xa2[1, rows]
            t4[1, zz] = pb[0, 0, rows] + yb[rows]

    def teacher_chunk(k):
        for i, (_, zz) in enumerate(units(k)):
            for half in range(2):
                block = h5[half, zz].reshape(32, 2048).astype(f32)
                squares = block * block
                total = squares[:, 0:128]
                for lane in range(128, 2048, 128):
                    total = total + squares[:, lane : lane + 128]
                ssq[half, zz] = total
                at = CHUNK_ROWS[k] * half + 32 * i
                scaled[at : at + 32, :] = (block * tg).astype(bf16)
        m = CHUNK_ROWS[k]

        def product(xo, yo):
            d = ((x + xo) % 4) * 2 + (yl + yo) % 2
            columns = pl.ds(pl.multiple_of(d * SLICE, SLICE), SLICE)
            both = jnp.dot(scaled[0 : 2 * m, :], head[:, columns], preferred_element_type=f32)
            pa[xo, yo, CHUNK_AT[k] : CHUNK_AT[k] + m, :] = both[0:m]
            pb[xo, yo, CHUNK_AT[k] : CHUNK_AT[k] + m, :] = both[m : 2 * m]

        def other_y(xo, carry):
            product(xo, 1)
            return carry

        lax.fori_loop(0, 4, other_y, 0)
        ex_send(k, 0, "a")
        product(2, 0)
        ex_send(k, 0, "b")
        for xo in (1, 3, 0):
            product(xo, 0)

    load_head.wait()

    def tstep(s):
        ring_arrived(h5, "t", s)
        if s < 3:
            for cp in ring_copies(h5, "t", s + 1):
                cp.start()
        for cp in sib_copies(h5, "t", s + 1):
            cp.start()

    def tchunk(k):
        sib_arrived(h5, "t", k)
        teacher_chunk(k)

    def sstart():
        arrived(f5.at[1 - yh, z, c], "s_yh", 0)
        for half in range(2):
            for cp in half_copies(0, half):
                cp.start()
        for cp in sib_copies(f5, "s", 0):
            cp.start()

    def fold(*rows):
        pieces = [v[:, 128 * i : 128 * i + 128] for v in rows for i in range(4)]
        row = lax.broadcasted_iota(jnp.int32, (8, 128), 0)
        out = jnp.zeros((8, 128), f32)
        for i, piece in enumerate(pieces):
            out = jnp.where(row == i, piece, out)
        return out

    def unfold(tile, first):
        return jnp.concatenate([tile[first + i : first + i + 1, :] for i in range(4)], axis=1)

    def sq_copy(j):
        return rc(sqs, sqr.at[j - 1], "sq", j, (tp, (dp + j) % 8))

    wt_copy = rc(wt.at[0:SLICE], wt.at[SLICE : 2 * SLICE], "wt", 0, sibling)

    def sq():
        sqs[...] = fold(jnp.sum(ssq[...].reshape(TOKENS, 128).T, 0, keepdims=True))
        for j in range(1, 8):
            sq_copy(j).start()
        wt_copy.start()

    def slog(piece):
        blocks = []
        for s in PIECES[piece]:
            sib_arrived(f5, "s", s)
            blocks += [zz for _, zz in units(s)]
        rows = jnp.concatenate([f5[:, zz].reshape(64, D_S) for zz in blocks], axis=0)
        product = jnp.dot(rows, w[...], preferred_element_type=f32)
        for i, zz in enumerate(blocks):
            s4[0, zz] = product[64 * i : 64 * i + 32]
            s4[1, zz] = product[64 * i + 32 : 64 * i + 64]

    steps = {
        "tstep": tstep, "tchunk": tchunk, "sstart": sstart, "sstep": student_step,
        "b2": b2, "a2": a2, "b3": b3, "a3": a3, "sq": sq, "slog": slog, "fin": fin,
    }
    for step, *where in FRONT:
        steps[step](*where)

    first = (tp * 8 + dp) * SLICE
    target_mask = ids_ref[...] == first + lax.broadcasted_iota(jnp.int32, (SLICE, TOKENS), 0)
    student = s4[...].reshape(TOKENS, SLICE).T
    s_top = jnp.max(student, 0, keepdims=True)
    s_total = jnp.sum(jnp.exp(student - s_top), 0, keepdims=True)
    target = jnp.sum(jnp.where(target_mask, student, 0.0), 0, keepdims=True)

    for j in range(1, 8):
        arrived(sqr.at[j - 1], "sq", j)
    square_total = sqs[...]
    for j in range(7):
        square_total = square_total + sqr[j]
    t_inv = unfold(lax.rsqrt(square_total / D_T + epsilon), 0)
    teacher = t4[...].reshape(TOKENS, SLICE).T * t_inv

    t_top = jnp.max(teacher, 0, keepdims=True)
    t_exp = jnp.exp(teacher - t_top)
    t_total = jnp.sum(t_exp, 0, keepdims=True)
    cross = jnp.sum(t_exp * (teacher - student), 0, keepdims=True)
    stats = (fold(t_top, s_top), fold(t_total, s_total), fold(cross, target))

    def exchange(buf, name, axis, value):
        if isinstance(value, tuple):
            for i, v in enumerate(value):
                buf[mine[axis], i] = v
        else:
            buf[mine[axis]] = value
        for j in range(1, size[axis]):
            exchange_copy(buf, name, axis, j).start()

    def exchange_copy(buf, name, axis, j):
        slot = buf.at[mine[axis]]
        return rc(slot, slot, name + "_" + axis, j, peer(axis, j))

    def exchanged(buf, name, axis):
        n = size[axis]
        for j in range(1, n):
            arrived(buf.at[(mine[axis] + n - j) % n], name + "_" + axis, j)
        return [buf[i] for i in range(n)]

    upper = lax.broadcasted_iota(jnp.int32, (8, 128), 0) < 4

    def merged(parts):
        top = functools.reduce(jnp.maximum, [p[0] for p in parts])
        total = other = 0.0
        for p in parts:
            factor = jnp.exp(p[0] - top)
            total = total + p[1] * factor
            other = other + p[2] * jnp.where(upper, factor, 1.0)
        return top, total, other

    for axis, buf in (("cx", st_cx), ("y", st_y), ("z", st_z)):
        exchange(buf, "st", axis, stats)
        stats = merged(exchanged(buf, "st", axis))

    top, total, other = stats
    lse = top + jnp.log(total)
    t_lse, s_lse = unfold(lse, 0), unfold(lse, 4)
    cross_mean, target = unfold(other / total, 0), unfold(other, 4)
    loss_ref[...] = cross_mean - t_lse + s_lse + hard_weight * (s_lse - target)
    t_prob = jnp.exp(teacher - t_lse)
    s_prob = jnp.exp(student - s_lse)
    onehot = target_mask.astype(f32)
    g = (loss_scale * (s_prob - t_prob + hard_weight * (s_prob - onehot))).astype(bf16)

    gp[...] = jnp.dot(g, perm[...], preferred_element_type=f32).astype(bf16).T

    other_rows = pl.ds(pl.multiple_of((1 - c) * 256, 256), 256)
    own_rows = pl.ds(pl.multiple_of(c * 256, 256), 256)
    gp_copy = rc(gp.at[other_rows], gr, "gp", 0, sibling)
    gp_copy.start()

    def shard(ch, o, part=slice(0, 4)):
        if ch < 2:
            return rs.at[ch, (x + o) % 4, part]
        return rs.at[ch, part, (y + o) % 4]

    y_right = peer("y", 1)
    y_left = peer("y", 3)

    def q1_copies(ch):
        r, l = (x_right, x_left) if ch < 2 else (y_right, y_left)
        return (
            rc(shard(ch, 2, slice(0, 2)), q1.at[ch, 0], "q1", ch * 2, r),
            rc(shard(ch, 2, slice(2, 4)), q1.at[ch, 1], "q1", ch * 2 + 1, l),
        )

    def q2_copies(ch):
        r, l = (x_right, x_left) if ch < 2 else (y_right, y_left)
        return (
            rc(shard(ch, 1), q2.at[ch, 0], "q2", ch * 2, r),
            rc(shard(ch, 3), q2.at[ch, 1], "q2", ch * 2 + 1, l),
        )

    arrived(wt.at[SLICE : 2 * SLICE], "wt", 0)
    arrived(gr, "gp", 0)
    both_slices = jnp.concatenate([gp[own_rows, :], gr[...]], axis=1)
    for ch in ORDER:
        for tile in range(2):
            at = ch * WIDE + tile * 512
            product = jnp.dot(both_slices, wt[:, at : at + 512], preferred_element_type=f32)
            rs[ch, :, :, :, tile * 512 : tile * 512 + 512] = product.astype(bf16).reshape(
                4, 4, 16, 512
            )
        for cp in q1_copies(ch):
            cp.start()
    def head_tile(i, carry):
        at = pl.ds(pl.multiple_of(i * 512, 512), 512)
        features = f5[:, :, :, :, at].reshape(TOKENS, 512)
        tile = jnp.dot(g, features, preferred_element_type=f32)
        cols[pl.ds(i, 1), :] = jnp.sum(tile * wt[0:SLICE, at].astype(f32), 0, keepdims=True)
        gh[at, :] = tile.astype(bf16).T
        return carry

    lax.fori_loop(0, 2, head_tile, 0)
    for ch in ORDER:
        for cp in q1_copies(ch):
            cp.wait_recv()
        for o, part, way in ((1, slice(0, 2), 0), (3, slice(2, 4), 1)):
            ref = shard(ch, o, part)
            ref[...] = (ref[...].astype(f32) + q1[ch, way].astype(f32)).astype(bf16)
        for cp in q2_copies(ch):
            cp.start()

    def rs2_copy(ch, j):
        if ch < 2:
            return rc(s2.at[ch, (y + j) % 4], r2.at[ch, j - 1], "rs2", ch * 4 + j, peer("y", j))
        return rc(s2.at[ch, (x + j) % 4], r2.at[ch, j - 1], "rs2", ch * 4 + j, peer("x", j))

    lax.fori_loop(2, 6, head_tile, 0)
    for ch in ORDER:
        if ch == ORDER[2]:
            lax.fori_loop(6, 8, head_tile, 0)
            store_head = pltpu.make_async_copy(gh, ghead_hbm, ssem.at[BASE["load"] + 2])
            store_head.start()
            exchange(ga_cx, "ga", "cx", cols[...])
        for cp in q2_copies(ch):
            cp.wait_recv()
        kept = shard(ch, 0)[...].astype(f32)
        total = kept + (q2[ch, 0].astype(f32) + q2[ch, 1].astype(f32))
        s2[ch] = total.astype(bf16)
        for j in range(1, 4):
            rs2_copy(ch, j).start()

    gain = functools.reduce(jnp.add, exchanged(ga_cx, "ga", "cx"))
    exchange(ga_y, "ga", "y", gain)

    for ch in ORDER:
        for j in range(1, 4):
            arrived(r2.at[ch, j - 1], "rs2", ch * 4 + j)
        kept = s2[ch, y] if ch < 2 else s2[ch, x]
        total = kept.astype(f32)
        for j in range(3):
            total = total + r2[ch, j].astype(f32)
        for zz in range(8):
            for half in range(2):
                at = 4 * ch + 2 * half
                zf[zz, at : at + 2, :] = total[2 * zz : 2 * zz + 2, 512 * half : 512 * half + 512]
    zb[...] = zf[...].astype(bf16)

    def rs3_copy(j):
        return rc(zb.at[(z + j) % 8], r3.at[j - 1], "rs3", j, peer("z", j))

    for j in range(1, 8):
        rs3_copy(j).start()

    gain = functools.reduce(jnp.add, exchanged(ga_y, "ga", "y"))
    exchange(ga_z, "ga", "z", gain)

    own_wide = sh_ref[...].astype(f32)
    own_inv = lax.rsqrt(jnp.sum(own_wide * own_wide, -1, keepdims=True) / D_S + epsilon)
    own_normed = own_wide * own_inv
    for j in range(1, 8):
        arrived(r3.at[j - 1], "rs3", j)
    folded = zf[z]
    for j in range(7):
        folded = folded + r3[j].astype(f32)
    for i in range(8):
        unfolded[:, 512 * i : 512 * i + 512] = folded[2 * i : 2 * i + 2, :]
    grad_normed = unfolded[...] * gain_row
    inner = jnp.sum(grad_normed * own_normed, -1, keepdims=True) / D_S
    ghid_ref[...] = own_inv * (grad_normed - own_normed * inner)

    gain = functools.reduce(jnp.add, exchanged(ga_z, "ga", "z"))
    row = lax.broadcasted_iota(jnp.int32, (8, 512), 0)
    gain_rows = jnp.ones((8, 512), f32)
    for i in range(8):
        gain_rows = jnp.where(row == i, gain_row[:, 512 * i : 512 * i + 512], gain_rows)
    ggain_ref[...] = gain / gain_rows

    for buf, name in ((h5, "t"), (f5, "s")):
        yh_copy(buf, name).wait_send()
        for s in range(4):
            copies = ring_copies(buf, name, s) if name == "t" else half_copies(s, 0) + half_copies(s, 1)
            for cp in copies:
                cp.wait_send()
        for s in range(5):
            for cp in sib_copies(buf, name, s):
                cp.wait_send()
    for j in range(1, 8):
        s0_copy(j).wait_send()
        sq_copy(j).wait_send()
        rs3_copy(j).wait_send()
    for k in range(5):
        for step in range(3):
            for cp in ex_copies(k, step):
                cp.wait_send()
    for name, bufs in (("st", (st_cx, st_y, st_z)), ("ga", (ga_cx, ga_y, ga_z))):
        for axis, buf in zip(("cx", "y", "z"), bufs):
            for j in range(1, size[axis]):
                exchange_copy(buf, name, axis, j).wait_send()
    for ch in range(4):
        for cp in q1_copies(ch) + q2_copies(ch):
            cp.wait_send()
        for j in range(1, 4):
            rs2_copy(ch, j).wait_send()
    wt_copy.wait_send()
    gp_copy.wait_send()
    store_head.wait()


def finish(loss_ref, hidden_ref, gain_ref, head_ref, loss_out, hidden_out, gain_out, head_out):
    head_out[...] = head_ref[...]

    @pl.when(pl.program_id(0) == 0)
    def _():
        loss_out[...] = loss_ref[...]
        hidden_out[...] = hidden_ref[...].astype(bf16)
        for i in range(8):
            gain_out[:, 512 * i : 512 * i + 512] = gain_ref[i : i + 1, :]


def shards(
    teacher_hidden,
    teacher_gain,
    teacher_head,
    student_hidden,
    student_gain,
    student_head,
    token_ids,
):
    vmem = pl.BlockSpec(memory_space=pltpu.VMEM)
    hbm = pl.BlockSpec(memory_space=pl.ANY)
    block = pl.BlockSpec((2048, SLICE), lambda i: (i, 0))

    def whole(*shape):
        return pl.BlockSpec(shape, lambda i: (0, 0))

    row8 = (8, TOKENS)
    scratch = [
        ((2048, 2048), bf16), ((D_S, SLICE), bf16), ((2 * SLICE, D_S), bf16), ((2, 8, 2, 16, 2048), bf16),
        ((128, 2048), bf16), ((4, 2, 256, SLICE), f32), ((4, 2, 256, SLICE), f32),
        ((4, 256, SLICE), f32), ((2, 256, SLICE), f32), ((2, 256, SLICE), f32),
        ((2, 2, 256, SLICE), f32), ((2, 2, 256, SLICE), f32), ((256, SLICE), f32),
        ((2, 8, 32, 128), f32), ((8, 128), f32), ((7, 8, 128), f32),
        ((8, 2, D_S), f32), ((16, D_S), f32), ((2, 8, 2, 16, D_S), bf16),
        ((2, 8, 32, SLICE), f32), ((2, 8, 32, SLICE), f32), ((8, 512), f32),
        ((8, 3, 8, 128), f32), ((4, 3, 8, 128), f32), ((8, 3, 8, 128), f32),
        ((8,) + row8, f32), ((4,) + row8, f32), ((8,) + row8, f32),
        ((TOKENS, SLICE), bf16), ((256, SLICE), bf16), ((TOKENS, TOKENS), bf16), ((D_S, SLICE), bf16),
        ((4, 4, 4, 16, WIDE), bf16), ((4, 2, 2, 16, WIDE), bf16), ((4, 2, 4, 16, WIDE), bf16),
        ((4, 4, 16, WIDE), bf16), ((4, 3, 16, WIDE), bf16),
        ((8, 16, 512), f32), ((8, 16, 512), bf16), ((7, 16, 512), bf16), ((2, D_S), f32),
    ]
    loss, grad_head, grad_hidden, grad_gain = pl.pallas_call(
        kernel,
        out_shape=(
            jax.ShapeDtypeStruct((1, TOKENS), f32),
            jax.ShapeDtypeStruct((D_S, SLICE), bf16),
            jax.ShapeDtypeStruct((2, D_S), f32),
            jax.ShapeDtypeStruct((8, 512), f32),
        ),
        in_specs=[vmem, vmem, hbm, vmem, vmem, hbm, vmem],
        out_specs=(vmem, hbm, vmem, vmem),
        scratch_shapes=[pltpu.VMEM(shape, dtype) for shape, dtype in scratch]
        + [pltpu.SemaphoreType.DMA((N_SEMS,)), pltpu.SemaphoreType.DMA((N_SEMS,))],
        compiler_params=pltpu.CompilerParams(
            collective_id=0, has_side_effects=True, vmem_limit_bytes=56 * 1024 * 1024
        ),
        cost_estimate=pl.CostEstimate(
            flops=7_600_000_000, bytes_accessed=13_000_000, transcendentals=600_000
        ),
    )(
        teacher_hidden,
        teacher_gain,
        teacher_head,
        student_hidden,
        student_gain,
        student_head,
        token_ids.reshape(1, TOKENS),
    )
    loss, grad_hidden, grad_gain, grad_head = pl.pallas_call(
        finish,
        out_shape=(
            jax.ShapeDtypeStruct((1, TOKENS), f32),
            jax.ShapeDtypeStruct((2, D_S), bf16),
            jax.ShapeDtypeStruct((1, D_S), f32),
            jax.ShapeDtypeStruct((D_S, SLICE), bf16),
        ),
        grid=(2,),
        in_specs=[whole(1, TOKENS), whole(2, D_S), whole(8, 512), block],
        out_specs=(whole(1, TOKENS), whole(2, D_S), whole(1, D_S), block),
        compiler_params=pltpu.CompilerParams(vmem_limit_bytes=56 * 1024 * 1024),
    )(loss, grad_hidden, grad_gain, grad_head)
    return loss.reshape(TOKENS), grad_hidden, grad_gain.reshape(D_S), grad_head


def solution(mesh):
    in_specs = (
        P("tp", "dp"),
        P("dp"),
        P("dp", "tp"),
        P(("tp", "dp"), None),
        P(),
        P(None, ("tp", "dp")),
        P(),
    )
    out_specs = (P(), P(("tp", "dp"), None), P(), P(None, ("tp", "dp")))
    return jax.shard_map(shards, mesh=mesh, in_specs=in_specs, out_specs=out_specs, check_vma=False)
```

```python
import functools

import jax
import jax.numpy as jnp
from jax import lax
from jax.experimental import pallas as pl
from jax.experimental.pallas import tpu as pltpu
from jax.sharding import PartitionSpec as P

D_T = 16384
D_S = 4096
TOKENS = 512
SLICE = 256

epsilon = 1e-05
hard_weight = 0.5
loss_scale = 64.0

MESH = pl.DeviceIdType.MESH
f32 = jnp.float32
bf16 = jnp.bfloat16

CHUNK_ROWS = (32, 64, 64, 64, 32)
CHUNK_AT = (0, 32, 96, 160, 224)
ORDER = (0, 2, 1, 3)
WIDE = 1024


FRONT = (
    ("tstep", 0), ("tchunk", 0), ("sstart",), ("tchunk", 1), ("b2", 0), ("tstep", 1),
    ("a2", 0), ("b2", 1), ("b3", 0), ("sstep", 0, 0), ("tchunk", 2), ("a2", 1), ("a3", 0),
    ("tstep", 2), ("sstep", 0, 1), ("b2", 2), ("sstep", 1, 0), ("tchunk", 3), ("a3", 1),
    ("a2", 2), ("tstep", 3), ("sstep", 1, 1), ("b2", 3), ("tchunk", 4), ("b3", 1), ("fin", 0),
    ("b3", 2), ("sstep", 2, 0), ("sq",), ("a3", 2), ("a2", 3), ("sstep", 2, 1), ("slog", 0),
    ("b2", 4), ("b3", 3), ("a2", 4), ("sstep", 3, 0), ("a3", 3), ("sstep", 3, 1), ("fin", 2),
    ("b3", 4), ("a3", 4), ("slog", 1), ("fin", 1), ("fin", 3), ("slog", 2), ("fin", 4),
)
PIECES = ((0, 1), (2,), (3, 4))


class Sems:
    def __init__(self):
        self.count = 0

    def take(self, n):
        at = self.count
        self.count += n
        return at


def layout():
    s = Sems()
    base = {}
    for name, n in (
        ("load", 3),
        ("t_yh", 1), ("t_r", 4), ("t_l", 4), ("t_s", 8),
        ("s_yh", 1), ("s_r", 8), ("s_l", 8), ("s_s", 8),
        ("s0", 8), ("ex", 50), ("sq", 8),
        ("st_cx", 8), ("st_y", 4), ("st_z", 8),
        ("ga_cx", 8), ("ga_y", 4), ("ga_z", 8),
        ("wt", 1), ("gp", 1), ("q1", 8), ("q2", 8), ("rs2", 16), ("rs3", 8),
    ):
        base[name] = s.take(n)
    return base, s.count


BASE, N_SEMS = layout()


def kernel(
    th_ref, tg_ref, thead_hbm, sh_ref, sg_ref, shead_hbm, ids_ref,
    loss_ref, ghead_hbm, ghid_ref, ggain_ref,
    head, w, wt, h5, scaled, pa, pb, ya, xa1, xa2, xb1, xb2, yb, ssq, sqs, sqr,
    s0, s16, f5, t4, s4, cols,
    st_cx, st_y, st_z, ga_cx, ga_y, ga_z,
    gp, gr, perm, gh, rs, q1, q2, s2, r2, zf, zb, r3, unfolded,
    ssem, rsem,
):
    tp = lax.axis_index("tp")
    dp = lax.axis_index("dp")
    c = lax.rem(tp, 2)
    z = lax.rem(lax.div(tp, 2), 8)
    yh = lax.div(tp, 16)
    x = lax.div(dp, 2)
    yl = lax.rem(dp, 2)
    y = yh * 2 + yl

    def dev(xx, yy, zz, cc):
        return (lax.div(yy, 2) * 16 + zz * 2 + cc, xx * 2 + lax.rem(yy, 2))

    def zmod(v):
        return lax.rem(v + 16, 8)

    def peer(axis, j):
        if axis == "c":
            return dev(x, y, z, lax.rem(c + j, 2))
        if axis == "x":
            return dev(lax.rem(x + j, 4), y, z, c)
        if axis == "y":
            return dev(x, lax.rem(y + j, 4), z, c)
        if axis == "cx":
            at = lax.rem(x * 2 + c + j, 8)
            return dev(lax.div(at, 2), y, z, lax.rem(at, 2))
        return dev(x, y, lax.rem(z + j, 8), c)

    size = {"cx": 8, "y": 4, "z": 8}
    mine = {"cx": x * 2 + c, "y": y, "z": z}

    def rc(src, dst, name, i, device):
        at = BASE[name] + i
        return pltpu.make_async_remote_copy(
            src_ref=src, dst_ref=dst, send_sem=ssem.at[at], recv_sem=rsem.at[at],
            device_id=device, device_id_type=MESH,
        )

    def arrived(dst, name, i):
        rc(dst, dst, name, i, peer("c", 1)).wait_recv()

    load_head = pltpu.make_async_copy(thead_hbm, head, ssem.at[BASE["load"]])
    load_w = pltpu.make_async_copy(shead_hbm, w, ssem.at[BASE["load"] + 1])
    load_w.start()
    load_head.start()

    barrier = pltpu.get_barrier_semaphore()
    partners = [peer("c", 1)]
    partners += [dev((x + j) % 4, y, z, cc) for j in range(1, 4) for cc in range(2)]
    partners += [peer("y", j) for j in range(1, 4)]
    partners += [dev((x + j) % 4, yh * 2 + 1 - yl, z, c) for j in range(1, 4)]
    partners += [peer("z", j) for j in range(1, 8)]
    for device in partners:
        pl.semaphore_signal(barrier, inc=1, device_id=device, device_id_type=MESH)

    h5[yh, z, c] = th_ref[...]
    s0[dp] = sh_ref[...].astype(f32)

    p = lax.broadcasted_iota(jnp.int32, (TOKENS, TOKENS), 1)
    q = lax.broadcasted_iota(jnp.int32, (TOKENS, TOKENS), 0)
    source = (
        ((p >> 5) & 1) * 256
        + ((p >> 1) & 7) * 32
        + (p >> 8) * 16
        + ((p >> 6) & 3) * 4
        + ((p >> 4) & 1) * 2
        + (p & 1)
    )
    perm[...] = jnp.where(q == source, 1.0, 0.0).astype(bf16)

    pl.semaphore_wait(barrier, len(partners))

    yh_peer = dev(x, (y + 2) % 4, z, c)
    sibling = peer("c", 1)
    right = peer("z", 1)
    left = peer("z", 7)

    y_outer = dev(x, 3 - y, z, c)

    def yh_copy(buf, name):
        own_block = buf.at[yh, z, c]
        return rc(own_block, own_block, name + "_yh", 0, yh_peer if name == "t" else y_outer)

    def ring_copies(buf, name, s):
        if s < 3:
            r, l = buf.at[:, zmod(z - s), c], buf.at[:, zmod(z + s), c]
        else:
            r, l = buf.at[0, zmod(z - s), c], buf.at[1, zmod(z + s), c]
        return rc(r, r, name + "_r", s, right), rc(l, l, name + "_l", s, left)

    def ring_arrived(buf, name, s):
        if s < 3:
            r, l = buf.at[:, zmod(z - 1 - s), c], buf.at[:, zmod(z + 1 + s), c]
        else:
            r, l = buf.at[0, zmod(z + 4), c], buf.at[1, zmod(z + 4), c]
        arrived(r, name + "_r", s)
        arrived(l, name + "_l", s)

    def half_copies(s, half):
        r, l = f5.at[half, zmod(z - s), c], f5.at[half, zmod(z + s), c]
        copies = []
        if s < 3 or half == 0:
            copies.append(rc(r, r, "s_r", 2 * s + half, right))
        if s < 3 or half == 1:
            copies.append(rc(l, l, "s_l", 2 * s + half, left))
        return copies

    def half_arrived(s, half):
        if s < 3 or half == 0:
            arrived(f5.at[half, zmod(z - 1 - s), c], "s_r", 2 * s + half)
        if s < 3 or half == 1:
            arrived(f5.at[half, zmod(z + 1 + s), c], "s_l", 2 * s + half)

    def student_step(s, half):
        half_arrived(s, half)
        if s < 3:
            for cp in half_copies(s + 1, half):
                cp.start()
        if half == 1:
            for cp in sib_copies(f5, "s", s + 1):
                cp.start()

    def units(s):
        if s == 0:
            return [(0, z)]
        if s == 4:
            return [(7, zmod(z + 4))]
        return [(2 * s - 1, zmod(z - s)), (2 * s, zmod(z + s))]

    def sib_copies(buf, name, s):
        return [
            rc(buf.at[:, zz, c], buf.at[:, zz, c], name + "_s", k, sibling) for k, zz in units(s)
        ]

    def sib_arrived(buf, name, s):
        for k, zz in units(s):
            arrived(buf.at[:, zz, 1 - c], name + "_s", k)

    yh_copy(h5, "t").start()

    def s0_copy(j):
        return rc(s0.at[dp], s0.at[dp], "s0", j, (tp, lax.rem(dp + j, 8)))

    for j in range(1, 8):
        s0_copy(j).start()

    load_w.wait()

    def turn(i, carry):
        at = pl.ds(pl.multiple_of(i * 512, 512), 512)
        wt[0:SLICE, at] = w[at, :].T
        return carry

    lax.fori_loop(0, 8, turn, 0)
    arrived(h5.at[1 - yh, z, c], "t_yh", 0)
    for cp in ring_copies(h5, "t", 0):
        cp.start()
    for cp in sib_copies(h5, "t", 0):
        cp.start()

    for j in range(1, 8):
        arrived(s0.at[lax.rem(dp + 8 - j, 8)], "s0", j)
    for d in range(8):
        s16[2 * d : 2 * d + 2, :] = s0[d]
    wide = s16[...]
    inv16 = lax.rsqrt(jnp.sum(wide * wide, -1, keepdims=True) / D_S + epsilon)
    gain_row = sg_ref[...].astype(f32).reshape(1, D_S)
    f5[yh, z, c] = (wide * inv16 * gain_row).astype(bf16)
    yh_copy(f5, "s").start()

    tg = tg_ref[...].astype(f32).reshape(1, 2048)

    x_right = peer("x", 1)
    x_left = peer("x", 3)
    y_pair = dev(x, yh * 2 + 1 - yl, z, c)

    def span(k, part):
        at, n = CHUNK_AT[k], CHUNK_ROWS[k]
        return {"all": pl.ds(at, n), "r": pl.ds(at, n // 2), "l": pl.ds(at + n // 2, n // 2)}[part]

    def ex_copies(k, step, which="ab"):
        every, rows_r, rows_l = span(k, "all"), span(k, "r"), span(k, "l")
        a_y = (pa.at[:, 1, every], ya.at[:, every], 0, y_pair)
        a_x1r = (pa.at[2, 0, rows_r], xa1.at[0, rows_r], 1, x_right)
        a_x1l = (pa.at[2, 0, rows_l], xa1.at[1, rows_l], 2, x_left)
        a_x2r = (pa.at[1, 0, every], xa2.at[0, every], 3, x_right)
        a_x2l = (pa.at[3, 0, every], xa2.at[1, every], 4, x_left)
        b_x1r = (pb.at[2, :, rows_r], xb1.at[0, :, rows_r], 5, x_right)
        b_x1l = (pb.at[2, :, rows_l], xb1.at[1, :, rows_l], 6, x_left)
        b_x2r = (pb.at[1, :, every], xb2.at[0, :, every], 7, x_right)
        b_x2l = (pb.at[3, :, every], xb2.at[1, :, every], 8, x_left)
        b_y = (pb.at[0, 1, every], yb.at[every], 9, y_pair)
        steps = {
            "a": ((a_y,), (a_x1r, a_x1l), (a_x2r, a_x2l)),
            "b": ((b_x1r, b_x1l), (b_x2r, b_x2l), (b_y,)),
        }
        return [
            rc(src, dst, "ex", k * 10 + i, device)
            for part in which
            for src, dst, i, device in steps[part][step]
        ]

    def ex_arrived(k, step, which="ab"):
        for cp in ex_copies(k, step, which):
            cp.wait_recv()

    def ex_send(k, step, which):
        for cp in ex_copies(k, step, which):
            cp.start()

    def b2(k):
        rows_r, rows_l = span(k, "r"), span(k, "l")
        ex_arrived(k, 0, "b")
        pb[1, :, rows_r] += xb1[0, :, rows_r]
        pb[3, :, rows_l] += xb1[1, :, rows_l]
        ex_send(k, 1, "b")

    def a2(k):
        every = span(k, "all")
        ex_arrived(k, 0, "a")
        pa[:, 0, every] += ya[:, every]
        ex_send(k, 1, "a")

    def b3(k):
        every = span(k, "all")
        ex_arrived(k, 1, "b")
        pb[0, :, every] += xb2[0, :, every] + xb2[1, :, every]
        ex_send(k, 2, "b")

    def a3(k):
        rows_r, rows_l = span(k, "r"), span(k, "l")
        ex_arrived(k, 1, "a")
        pa[1, 0, rows_r] += xa1[0, rows_r]
        pa[3, 0, rows_l] += xa1[1, rows_l]
        ex_send(k, 2, "a")

    def fin(k):
        ex_arrived(k, 2)
        for i, (_, zz) in enumerate(units(k)):
            rows = pl.ds(CHUNK_AT[k] + 32 * i, 32)
            t4[0, zz] = pa[0, 0, rows] + xa2[0, rows] + xa2[1, rows]
            t4[1, zz] = pb[0, 0, rows] + yb[rows]

    def teacher_chunk(k):
        for i, (_, zz) in enumerate(units(k)):
            for half in range(2):
                block = h5[half, zz].reshape(32, 2048).astype(f32)
                squares = block * block
                total = squares[:, 0:128]
                for lane in range(128, 2048, 128):
                    total = total + squares[:, lane : lane + 128]
                ssq[half, zz] = total
                at = CHUNK_ROWS[k] * half + 32 * i
                scaled[at : at + 32, :] = (block * tg).astype(bf16)
        m = CHUNK_ROWS[k]

        def product(xo, yo):
            d = lax.rem(x + xo, 4) * 2 + lax.rem(yl + yo, 2)
            columns = pl.ds(pl.multiple_of(d * SLICE, SLICE), SLICE)
            both = jnp.dot(scaled[0 : 2 * m, :], head[:, columns], preferred_element_type=f32)
            pa[xo, yo, CHUNK_AT[k] : CHUNK_AT[k] + m, :] = both[0:m]
            pb[xo, yo, CHUNK_AT[k] : CHUNK_AT[k] + m, :] = both[m : 2 * m]

        def other_y(xo, carry):
            product(xo, 1)
            return carry

        lax.fori_loop(0, 4, other_y, 0)
        ex_send(k, 0, "a")
        product(2, 0)
        ex_send(k, 0, "b")
        for xo in (1, 3, 0):
            product(xo, 0)

    load_head.wait()

    def tstep(s):
        ring_arrived(h5, "t", s)
        if s < 3:
            for cp in ring_copies(h5, "t", s + 1):
                cp.start()
        for cp in sib_copies(h5, "t", s + 1):
            cp.start()

    def tchunk(k):
        sib_arrived(h5, "t", k)
        teacher_chunk(k)

    def sstart():
        arrived(f5.at[1 - yh, z, c], "s_yh", 0)
        for half in range(2):
            for cp in half_copies(0, half):
                cp.start()
        for cp in sib_copies(f5, "s", 0):
            cp.start()

    def fold(*rows):
        pieces = [v[:, 128 * i : 128 * i + 128] for v in rows for i in range(4)]
        row = lax.broadcasted_iota(jnp.int32, (8, 128), 0)
        out = jnp.zeros((8, 128), f32)
        for i, piece in enumerate(pieces):
            out = jnp.where(row == i, piece, out)
        return out

    def unfold(tile, first):
        return jnp.concatenate([tile[first + i : first + i + 1, :] for i in range(4)], axis=1)

    def sq_copy(j):
        return rc(sqs, sqr.at[j - 1], "sq", j, (tp, lax.rem(dp + j, 8)))

    wt_copy = rc(wt.at[0:SLICE], wt.at[SLICE : 2 * SLICE], "wt", 0, sibling)

    def sq():
        sqs[...] = fold(jnp.sum(ssq[...].reshape(TOKENS, 128).T, 0, keepdims=True))
        for j in range(1, 8):
            sq_copy(j).start()
        wt_copy.start()

    def slog(piece):
        blocks = []
        for s in PIECES[piece]:
            sib_arrived(f5, "s", s)
            blocks += [zz for _, zz in units(s)]
        rows = jnp.concatenate([f5[:, zz].reshape(64, D_S) for zz in blocks], axis=0)
        product = jnp.dot(rows, w[...], preferred_element_type=f32)
        for i, zz in enumerate(blocks):
            s4[0, zz] = product[64 * i : 64 * i + 32]
            s4[1, zz] = product[64 * i + 32 : 64 * i + 64]

    steps = {
        "tstep": tstep, "tchunk": tchunk, "sstart": sstart, "sstep": student_step,
        "b2": b2, "a2": a2, "b3": b3, "a3": a3, "sq": sq, "slog": slog, "fin": fin,
    }
    for step, *where in FRONT:
        steps[step](*where)

    first = (tp * 8 + dp) * SLICE
    target_mask = ids_ref[...] == first + lax.broadcasted_iota(jnp.int32, (SLICE, TOKENS), 0)
    student = s4[...].reshape(TOKENS, SLICE).T
    s_top = jnp.max(student, 0, keepdims=True)
    s_total = jnp.sum(jnp.exp(student - s_top), 0, keepdims=True)
    target = jnp.sum(jnp.where(target_mask, student, 0.0), 0, keepdims=True)

    for j in range(1, 8):
        arrived(sqr.at[j - 1], "sq", j)
    square_total = sqs[...]
    for j in range(7):
        square_total = square_total + sqr[j]
    t_inv = unfold(lax.rsqrt(square_total / D_T + epsilon), 0)
    teacher = t4[...].reshape(TOKENS, SLICE).T * t_inv

    t_top = jnp.max(teacher, 0, keepdims=True)
    t_exp = jnp.exp(teacher - t_top)
    t_total = jnp.sum(t_exp, 0, keepdims=True)
    cross = jnp.sum(t_exp * (teacher - student), 0, keepdims=True)
    stats = (fold(t_top, s_top), fold(t_total, s_total), fold(cross, target))

    def exchange(buf, name, axis, value):
        if isinstance(value, tuple):
            for i, v in enumerate(value):
                buf[mine[axis], i] = v
        else:
            buf[mine[axis]] = value
        for j in range(1, size[axis]):
            exchange_copy(buf, name, axis, j).start()

    def exchange_copy(buf, name, axis, j):
        slot = buf.at[mine[axis]]
        return rc(slot, slot, name + "_" + axis, j, peer(axis, j))

    def exchanged(buf, name, axis):
        n = size[axis]
        for j in range(1, n):
            arrived(buf.at[lax.rem(mine[axis] + n - j, n)], name + "_" + axis, j)
        return [buf[i] for i in range(n)]

    upper = lax.broadcasted_iota(jnp.int32, (8, 128), 0) < 4

    def merged(parts):
        top = functools.reduce(jnp.maximum, [p[0] for p in parts])
        total = other = 0.0
        for p in parts:
            factor = jnp.exp(p[0] - top)
            total = total + p[1] * factor
            other = other + p[2] * jnp.where(upper, factor, 1.0)
        return top, total, other

    def front_left():
        for buf, name in ((h5, "t"), (f5, "s")):
            yh_copy(buf, name).wait_send()
            for s in range(4):
                copies = ring_copies(buf, name, s) if name == "t" else half_copies(s, 0) + half_copies(s, 1)
                for cp in copies:
                    cp.wait_send()
            for s in range(5):
                for cp in sib_copies(buf, name, s):
                    cp.wait_send()
        wt_copy.wait_send()

    def exchange_left():
        for j in range(1, 8):
            s0_copy(j).wait_send()
            sq_copy(j).wait_send()
        for k in range(5):
            for step in range(3):
                for cp in ex_copies(k, step):
                    cp.wait_send()

    for axis, buf in (("cx", st_cx), ("y", st_y), ("z", st_z)):
        exchange(buf, "st", axis, stats)
        if axis == "cx":
            front_left()
        if axis == "z":
            exchange_left()
        stats = merged(exchanged(buf, "st", axis))

    top, total, other = stats
    lse = top + jnp.log(total)
    t_lse, s_lse = unfold(lse, 0), unfold(lse, 4)
    cross_mean, target = unfold(other / total, 0), unfold(other, 4)
    loss_ref[...] = cross_mean - t_lse + s_lse + hard_weight * (s_lse - target)
    t_prob = jnp.exp(teacher - t_lse)
    s_prob = jnp.exp(student - s_lse)
    onehot = target_mask.astype(f32)
    g = (loss_scale * (s_prob - t_prob + hard_weight * (s_prob - onehot))).astype(bf16)

    gp[...] = jnp.dot(g, perm[...], preferred_element_type=f32).astype(bf16).T

    other_rows = pl.ds(pl.multiple_of((1 - c) * 256, 256), 256)
    own_rows = pl.ds(pl.multiple_of(c * 256, 256), 256)
    gp_copy = rc(gp.at[other_rows], gr, "gp", 0, sibling)
    gp_copy.start()
    first_own = [
        jnp.dot(gp[own_rows, :], wt[0:SLICE, at : at + 512], preferred_element_type=f32)
        for at in (ORDER[0] * WIDE, ORDER[0] * WIDE + 512)
    ]
    for axis, buf in (("cx", st_cx), ("y", st_y), ("z", st_z)):
        for j in range(1, size[axis]):
            exchange_copy(buf, "st", axis, j).wait_send()

    def shard(ch, o, part=slice(0, 4)):
        if ch < 2:
            return rs.at[ch, lax.rem(x + o, 4), part]
        return rs.at[ch, part, lax.rem(y + o, 4)]

    y_right = peer("y", 1)
    y_left = peer("y", 3)

    def q1_copies(ch):
        r, l = (x_right, x_left) if ch < 2 else (y_right, y_left)
        return (
            rc(shard(ch, 2, slice(0, 2)), q1.at[ch, 0], "q1", ch * 2, r),
            rc(shard(ch, 2, slice(2, 4)), q1.at[ch, 1], "q1", ch * 2 + 1, l),
        )

    def q2_copies(ch):
        r, l = (x_right, x_left) if ch < 2 else (y_right, y_left)
        return (
            rc(shard(ch, 1), q2.at[ch, 0], "q2", ch * 2, r),
            rc(shard(ch, 3), q2.at[ch, 1], "q2", ch * 2 + 1, l),
        )

    arrived(wt.at[SLICE : 2 * SLICE], "wt", 0)
    arrived(gr, "gp", 0)
    both_slices = jnp.concatenate([gp[own_rows, :], gr[...]], axis=1)
    for ch in ORDER:
        for tile in range(2):
            at = ch * WIDE + tile * 512
            if ch == ORDER[0]:
                product = first_own[tile] + jnp.dot(
                    gr[...], wt[SLICE : 2 * SLICE, at : at + 512], preferred_element_type=f32
                )
            else:
                product = jnp.dot(both_slices, wt[:, at : at + 512], preferred_element_type=f32)
            rs[ch, :, :, :, tile * 512 : tile * 512 + 512] = product.astype(bf16).reshape(
                4, 4, 16, 512
            )
        for cp in q1_copies(ch):
            cp.start()
    def head_tile(i, carry):
        at = pl.ds(pl.multiple_of(i * 512, 512), 512)
        features = f5[:, :, :, :, at].reshape(TOKENS, 512)
        tile = jnp.dot(g, features, preferred_element_type=f32)
        cols[pl.ds(i, 1), :] = jnp.sum(tile * wt[0:SLICE, at].astype(f32), 0, keepdims=True)
        gh[at, :] = tile.astype(bf16).T
        return carry

    lax.fori_loop(0, 2, head_tile, 0)
    for ch in ORDER:
        for cp in q1_copies(ch):
            cp.wait_recv()
        for o, part, way in ((1, slice(0, 2), 0), (3, slice(2, 4), 1)):
            ref = shard(ch, o, part)
            ref[...] = (ref[...].astype(f32) + q1[ch, way].astype(f32)).astype(bf16)
        for cp in q2_copies(ch):
            cp.start()

    def rs2_copy(ch, j):
        if ch < 2:
            return rc(s2.at[ch, lax.rem(y + j, 4)], r2.at[ch, j - 1], "rs2", ch * 4 + j, peer("y", j))
        return rc(s2.at[ch, lax.rem(x + j, 4)], r2.at[ch, j - 1], "rs2", ch * 4 + j, peer("x", j))

    lax.fori_loop(2, 6, head_tile, 0)
    for ch in ORDER:
        if ch == ORDER[2]:
            lax.fori_loop(6, 8, head_tile, 0)
            store_head = pltpu.make_async_copy(gh, ghead_hbm, ssem.at[BASE["load"] + 2])
            store_head.start()
            exchange(ga_z, "ga", "z", cols[...])
        for cp in q2_copies(ch):
            cp.wait_recv()
        kept = shard(ch, 0)[...].astype(f32)
        total = kept + (q2[ch, 0].astype(f32) + q2[ch, 1].astype(f32))
        s2[ch] = total.astype(bf16)
        for j in range(1, 4):
            rs2_copy(ch, j).start()

    gain = functools.reduce(jnp.add, exchanged(ga_z, "ga", "z"))
    exchange(ga_cx, "ga", "cx", gain)

    for ch in ORDER:
        for j in range(1, 4):
            arrived(r2.at[ch, j - 1], "rs2", ch * 4 + j)
        kept = s2[ch, y] if ch < 2 else s2[ch, x]
        total = kept.astype(f32)
        for j in range(3):
            total = total + r2[ch, j].astype(f32)
        for zz in range(8):
            for half in range(2):
                at = 4 * ch + 2 * half
                zf[zz, at : at + 2, :] = total[2 * zz : 2 * zz + 2, 512 * half : 512 * half + 512]
    zb[...] = zf[...].astype(bf16)

    def rs3_copy(j):
        return rc(zb.at[lax.rem(z + j, 8)], r3.at[j - 1], "rs3", j, peer("z", j))

    for j in range(1, 8):
        rs3_copy(j).start()

    gain = functools.reduce(jnp.add, exchanged(ga_cx, "ga", "cx"))
    exchange(ga_y, "ga", "y", gain)

    def gains_left(*axes):
        for axis, buf in (("cx", ga_cx), ("y", ga_y), ("z", ga_z)):
            if axis in axes:
                for j in range(1, size[axis]):
                    exchange_copy(buf, "ga", axis, j).wait_send()

    gains_left("z", "cx")
    gp_copy.wait_send()
    for ch in range(4):
        for cp in q1_copies(ch) + q2_copies(ch):
            cp.wait_send()
        for j in range(1, 4):
            rs2_copy(ch, j).wait_send()

    own_wide = sh_ref[...].astype(f32)
    own_inv = lax.rsqrt(jnp.sum(own_wide * own_wide, -1, keepdims=True) / D_S + epsilon)
    own_normed = own_wide * own_inv
    for j in range(1, 8):
        arrived(r3.at[j - 1], "rs3", j)
    folded = zf[z]
    for j in range(7):
        folded = folded + r3[j].astype(f32)
    for i in range(8):
        unfolded[:, 512 * i : 512 * i + 512] = folded[2 * i : 2 * i + 2, :]
    grad_normed = unfolded[...] * gain_row
    inner = jnp.sum(grad_normed * own_normed, -1, keepdims=True) / D_S
    ghid_ref[...] = own_inv * (grad_normed - own_normed * inner)

    gain = functools.reduce(jnp.add, exchanged(ga_y, "ga", "y"))
    row = lax.broadcasted_iota(jnp.int32, (8, 512), 0)
    gain_rows = jnp.ones((8, 512), f32)
    for i in range(8):
        gain_rows = jnp.where(row == i, gain_row[:, 512 * i : 512 * i + 512], gain_rows)
    ggain_ref[...] = gain / gain_rows

    gains_left("y")
    for j in range(1, 8):
        rs3_copy(j).wait_send()
    store_head.wait()


def finish(loss_ref, hidden_ref, gain_ref, head_ref, loss_out, hidden_out, gain_out, head_out):
    head_out[...] = head_ref[...]

    @pl.when(pl.program_id(0) == 0)
    def _():
        loss_out[...] = loss_ref[...]
        hidden_out[...] = hidden_ref[...].astype(bf16)
        for i in range(8):
            gain_out[:, 512 * i : 512 * i + 512] = gain_ref[i : i + 1, :]


def shards(
    teacher_hidden,
    teacher_gain,
    teacher_head,
    student_hidden,
    student_gain,
    student_head,
    token_ids,
):
    vmem = pl.BlockSpec(memory_space=pltpu.VMEM)
    hbm = pl.BlockSpec(memory_space=pl.ANY)
    block = pl.BlockSpec((2048, SLICE), lambda i: (i, 0))

    def whole(*shape):
        return pl.BlockSpec(shape, lambda i: (0, 0))

    row8 = (8, TOKENS)
    scratch = [
        ((2048, 2048), bf16), ((D_S, SLICE), bf16), ((2 * SLICE, D_S), bf16), ((2, 8, 2, 16, 2048), bf16),
        ((128, 2048), bf16), ((4, 2, 256, SLICE), f32), ((4, 2, 256, SLICE), f32),
        ((4, 256, SLICE), f32), ((2, 256, SLICE), f32), ((2, 256, SLICE), f32),
        ((2, 2, 256, SLICE), f32), ((2, 2, 256, SLICE), f32), ((256, SLICE), f32),
        ((2, 8, 32, 128), f32), ((8, 128), f32), ((7, 8, 128), f32),
        ((8, 2, D_S), f32), ((16, D_S), f32), ((2, 8, 2, 16, D_S), bf16),
        ((2, 8, 32, SLICE), f32), ((2, 8, 32, SLICE), f32), ((8, 512), f32),
        ((8, 3, 8, 128), f32), ((4, 3, 8, 128), f32), ((8, 3, 8, 128), f32),
        ((8,) + row8, f32), ((4,) + row8, f32), ((8,) + row8, f32),
        ((TOKENS, SLICE), bf16), ((256, SLICE), bf16), ((TOKENS, TOKENS), bf16), ((D_S, SLICE), bf16),
        ((4, 4, 4, 16, WIDE), bf16), ((4, 2, 2, 16, WIDE), bf16), ((4, 2, 4, 16, WIDE), bf16),
        ((4, 4, 16, WIDE), bf16), ((4, 3, 16, WIDE), bf16),
        ((8, 16, 512), f32), ((8, 16, 512), bf16), ((7, 16, 512), bf16), ((2, D_S), f32),
    ]
    loss, grad_head, grad_hidden, grad_gain = pl.pallas_call(
        kernel,
        out_shape=(
            jax.ShapeDtypeStruct((1, TOKENS), f32),
            jax.ShapeDtypeStruct((D_S, SLICE), bf16),
            jax.ShapeDtypeStruct((2, D_S), f32),
            jax.ShapeDtypeStruct((8, 512), f32),
        ),
        in_specs=[vmem, vmem, hbm, vmem, vmem, hbm, vmem],
        out_specs=(vmem, hbm, vmem, vmem),
        scratch_shapes=[pltpu.VMEM(shape, dtype) for shape, dtype in scratch]
        + [pltpu.SemaphoreType.DMA((N_SEMS,)), pltpu.SemaphoreType.DMA((N_SEMS,))],
        compiler_params=pltpu.CompilerParams(
            collective_id=0, has_side_effects=True, vmem_limit_bytes=56 * 1024 * 1024
        ),
        cost_estimate=pl.CostEstimate(
            flops=7_600_000_000, bytes_accessed=13_000_000, transcendentals=600_000
        ),
    )(
        teacher_hidden,
        teacher_gain,
        teacher_head,
        student_hidden,
        student_gain,
        student_head,
        token_ids.reshape(1, TOKENS),
    )
    loss, grad_hidden, grad_gain, grad_head = pl.pallas_call(
        finish,
        out_shape=(
            jax.ShapeDtypeStruct((1, TOKENS), f32),
            jax.ShapeDtypeStruct((2, D_S), bf16),
            jax.ShapeDtypeStruct((1, D_S), f32),
            jax.ShapeDtypeStruct((D_S, SLICE), bf16),
        ),
        grid=(2,),
        in_specs=[whole(1, TOKENS), whole(2, D_S), whole(8, 512), block],
        out_specs=(whole(1, TOKENS), whole(2, D_S), whole(1, D_S), block),
        compiler_params=pltpu.CompilerParams(vmem_limit_bytes=56 * 1024 * 1024),
    )(loss, grad_hidden, grad_gain, grad_head)
    return loss.reshape(TOKENS), grad_hidden, grad_gain.reshape(D_S), grad_head


def solution(mesh):
    in_specs = (
        P("tp", "dp"),
        P("dp"),
        P("dp", "tp"),
        P(("tp", "dp"), None),
        P(),
        P(None, ("tp", "dp")),
        P(),
    )
    out_specs = (P(), P(("tp", "dp"), None), P(), P(None, ("tp", "dp")))
    return jax.shard_map(shards, mesh=mesh, in_specs=in_specs, out_specs=out_specs, check_vma=False)
```

```python
import functools

import jax
import jax.numpy as jnp
from jax import lax
from jax.experimental import pallas as pl
from jax.experimental.pallas import tpu as pltpu
from jax.sharding import PartitionSpec as P

D_T = 16384
D_S = 4096
TOKENS = 512
SLICE = 256

epsilon = 1e-05
hard_weight = 0.5
loss_scale = 64.0

MESH = pl.DeviceIdType.MESH
f32 = jnp.float32
bf16 = jnp.bfloat16

CHUNK_ROWS = (32, 64, 64, 64, 32)
CHUNK_AT = (0, 32, 96, 160, 224)
ORDER = (0, 2, 1, 3)
WIDE = 1024


FRONT = (
    ("turn",), ("th", 0, 0), ("t0",), ("th", 1, 0), ("feat",), ("th", 0, 1), ("tchunk", 0),
    ("th", 1, 1), ("th", 2, 0), ("sstart",), ("tchunk", 1), ("th", 2, 1), ("b2", 0), ("a2", 0),
    ("tchunk", 2), ("b2", 1), ("sstep", 0, 0), ("th", 3, 0), ("tchunk", 3), ("th", 3, 1),
    ("sstep", 0, 1), ("b3", 0), ("a3", 0), ("b2", 2), ("a2", 1), ("sstep", 1, 0),
    ("tchunk", 4), ("sstep", 1, 1), ("b2", 3), ("a2", 2), ("sstep", 2, 0), ("b3", 1),
    ("a3", 1), ("a2", 3), ("sstep", 2, 1), ("b3", 2), ("fin", 0), ("b2", 4), ("slog", 0),
    ("a3", 2), ("a2", 4), ("a3", 3), ("sstep", 3, 0), ("b3", 3), ("b3", 4), ("sstep", 3, 1),
    ("sq",), ("fin", 1), ("a3", 4), ("slog", 1), ("fin", 2), ("fin", 3), ("slog", 2),
    ("fin", 4),
)
PIECES = ((0, 1), (2,), (3, 4))


class Sems:
    def __init__(self):
        self.count = 0

    def take(self, n):
        at = self.count
        self.count += n
        return at


def layout():
    s = Sems()
    base = {}
    for name, n in (
        ("load", 3),
        ("t_yh", 1), ("t_r", 8), ("t_l", 8), ("t_s", 8),
        ("s_yh", 1), ("s_r", 8), ("s_l", 8), ("s_s", 8),
        ("s0", 8), ("ex", 50), ("sq", 8),
        ("st_cx", 8), ("st_y", 4), ("st_z", 8),
        ("ga_cx", 8), ("ga_y", 4), ("ga_z", 8),
        ("wt", 1), ("gp", 1), ("q1", 8), ("q2", 8), ("rs2", 16), ("rs3", 8),
    ):
        base[name] = s.take(n)
    return base, s.count


BASE, N_SEMS = layout()


def kernel(
    th_ref, tg_ref, thead_hbm, sh_ref, sg_ref, shead_hbm, ids_ref,
    loss_ref, ghead_hbm, ghid_ref, ggain_ref,
    head, w, wt, h5, scaled, pa, pb, ya, xa1, xa2, xb1, xb2, yb, ssq, sqs, sqr,
    s0, s16, f5, t4, s4, cols,
    st_cx, st_y, st_z, ga_cx, ga_y, ga_z,
    gp, gr, perm, gh, rs, q1, q2, s2, r2, zf, zb, r3, unfolded,
    ssem, rsem,
):
    tp = lax.axis_index("tp")
    dp = lax.axis_index("dp")
    c = lax.rem(tp, 2)
    z = lax.rem(lax.div(tp, 2), 8)
    yh = lax.div(tp, 16)
    x = lax.div(dp, 2)
    yl = lax.rem(dp, 2)
    y = yh * 2 + yl

    def dev(xx, yy, zz, cc):
        return (lax.div(yy, 2) * 16 + zz * 2 + cc, xx * 2 + lax.rem(yy, 2))

    def zmod(v):
        return lax.rem(v + 16, 8)

    def peer(axis, j):
        if axis == "c":
            return dev(x, y, z, lax.rem(c + j, 2))
        if axis == "x":
            return dev(lax.rem(x + j, 4), y, z, c)
        if axis == "y":
            return dev(x, lax.rem(y + j, 4), z, c)
        if axis == "cx":
            at = lax.rem(x * 2 + c + j, 8)
            return dev(lax.div(at, 2), y, z, lax.rem(at, 2))
        return dev(x, y, lax.rem(z + j, 8), c)

    size = {"cx": 8, "y": 4, "z": 8}
    mine = {"cx": x * 2 + c, "y": y, "z": z}

    def rc(src, dst, name, i, device):
        at = BASE[name] + i
        return pltpu.make_async_remote_copy(
            src_ref=src, dst_ref=dst, send_sem=ssem.at[at], recv_sem=rsem.at[at],
            device_id=device, device_id_type=MESH,
        )

    def arrived(dst, name, i):
        rc(dst, dst, name, i, peer("c", 1)).wait_recv()

    load_head = pltpu.make_async_copy(thead_hbm, head, ssem.at[BASE["load"]])
    load_w = pltpu.make_async_copy(shead_hbm, w, ssem.at[BASE["load"] + 1])
    load_w.start()
    load_head.start()

    barrier = pltpu.get_barrier_semaphore()
    partners = [peer("c", 1)]
    partners += [dev((x + j) % 4, y, z, cc) for j in range(1, 4) for cc in range(2)]
    partners += [peer("y", j) for j in range(1, 4)]
    partners += [dev((x + j) % 4, yh * 2 + 1 - yl, z, c) for j in range(1, 4)]
    partners += [peer("z", j) for j in range(1, 8)]
    for device in partners:
        pl.semaphore_signal(barrier, inc=1, device_id=device, device_id_type=MESH)

    h5[yh, z, c] = th_ref[...]
    s0[dp] = sh_ref[...].astype(f32)

    p = lax.broadcasted_iota(jnp.int32, (TOKENS, TOKENS), 1)
    q = lax.broadcasted_iota(jnp.int32, (TOKENS, TOKENS), 0)
    source = (
        ((p >> 5) & 1) * 256
        + ((p >> 1) & 7) * 32
        + (p >> 8) * 16
        + ((p >> 6) & 3) * 4
        + ((p >> 4) & 1) * 2
        + (p & 1)
    )
    perm[...] = jnp.where(q == source, 1.0, 0.0).astype(bf16)

    pl.semaphore_wait(barrier, len(partners))

    yh_peer = dev(x, (y + 2) % 4, z, c)
    sibling = peer("c", 1)
    right = peer("z", 1)
    left = peer("z", 7)

    y_outer = dev(x, 3 - y, z, c)

    def yh_copy(buf, name):
        own_block = buf.at[yh, z, c]
        return rc(own_block, own_block, name + "_yh", 0, yh_peer if name == "t" else y_outer)

    def half_copies(buf, name, s, half):
        of = yh if half == 0 else 1 - yh
        r, l = buf.at[of, zmod(z - s), c], buf.at[of, zmod(z + s), c]
        copies = []
        if s < 3 or half == 0:
            copies.append(rc(r, r, name + "_r", 2 * s + half, right))
        if s < 3 or half == 1:
            copies.append(rc(l, l, name + "_l", 2 * s + half, left))
        return copies

    def half_arrived(buf, name, s, half):
        of = yh if half == 0 else 1 - yh
        if s < 3 or half == 0:
            arrived(buf.at[of, zmod(z - 1 - s), c], name + "_r", 2 * s + half)
        if s < 3 or half == 1:
            arrived(buf.at[of, zmod(z + 1 + s), c], name + "_l", 2 * s + half)

    def ring_send(buf, name, s, half):
        for cp in half_copies(buf, name, s, half):
            cp.start()

    def ring_step(buf, name, s, half):
        half_arrived(buf, name, s, half)
        if s < 3:
            ring_send(buf, name, s + 1, half)
        if half == 1:
            for cp in sib_copies(buf, name, s + 1):
                cp.start()

    def units(s):
        if s == 0:
            return [(0, z)]
        if s == 4:
            return [(7, zmod(z + 4))]
        return [(2 * s - 1, zmod(z - s)), (2 * s, zmod(z + s))]

    def sib_copies(buf, name, s):
        return [
            rc(buf.at[:, zz, c], buf.at[:, zz, c], name + "_s", k, sibling) for k, zz in units(s)
        ]

    def sib_arrived(buf, name, s):
        for k, zz in units(s):
            arrived(buf.at[:, zz, 1 - c], name + "_s", k)

    yh_copy(h5, "t").start()
    ring_send(h5, "t", 0, 0)

    def s0_copy(j):
        return rc(s0.at[dp], s0.at[dp], "s0", j, (tp, lax.rem(dp + j, 8)))

    for j in range(1, 8):
        s0_copy(j).start()

    def turn():
        load_w.wait()

        def tile(i, carry):
            at = pl.ds(pl.multiple_of(i * 512, 512), 512)
            wt[0:SLICE, at] = w[at, :].T
            return carry

        lax.fori_loop(0, 8, tile, 0)

    def t0():
        arrived(h5.at[1 - yh, z, c], "t_yh", 0)
        ring_send(h5, "t", 0, 1)
        for cp in sib_copies(h5, "t", 0):
            cp.start()

    gain_row = sg_ref[...].astype(f32).reshape(1, D_S)

    def feat():
        for j in range(1, 8):
            arrived(s0.at[lax.rem(dp + 8 - j, 8)], "s0", j)
        for d in range(8):
            s16[2 * d : 2 * d + 2, :] = s0[d]
        wide = s16[...]
        inv16 = lax.rsqrt(jnp.sum(wide * wide, -1, keepdims=True) / D_S + epsilon)
        f5[yh, z, c] = (wide * inv16 * gain_row).astype(bf16)
        yh_copy(f5, "s").start()

    tg = tg_ref[...].astype(f32).reshape(1, 2048)

    x_right = peer("x", 1)
    x_left = peer("x", 3)
    y_pair = dev(x, yh * 2 + 1 - yl, z, c)

    def span(k, part):
        at, n = CHUNK_AT[k], CHUNK_ROWS[k]
        return {"all": pl.ds(at, n), "r": pl.ds(at, n // 2), "l": pl.ds(at + n // 2, n // 2)}[part]

    def ex_copies(k, step, which="ab"):
        every, rows_r, rows_l = span(k, "all"), span(k, "r"), span(k, "l")
        a_y = (pa.at[:, 1, every], ya.at[:, every], 0, y_pair)
        a_x1r = (pa.at[2, 0, rows_r], xa1.at[0, rows_r], 1, x_right)
        a_x1l = (pa.at[2, 0, rows_l], xa1.at[1, rows_l], 2, x_left)
        a_x2r = (pa.at[1, 0, every], xa2.at[0, every], 3, x_right)
        a_x2l = (pa.at[3, 0, every], xa2.at[1, every], 4, x_left)
        b_x1r = (pb.at[2, :, rows_r], xb1.at[0, :, rows_r], 5, x_right)
        b_x1l = (pb.at[2, :, rows_l], xb1.at[1, :, rows_l], 6, x_left)
        b_x2r = (pb.at[1, :, every], xb2.at[0, :, every], 7, x_right)
        b_x2l = (pb.at[3, :, every], xb2.at[1, :, every], 8, x_left)
        b_y = (pb.at[0, 1, every], yb.at[every], 9, y_pair)
        steps = {
            "a": ((a_y,), (a_x1r, a_x1l), (a_x2r, a_x2l)),
            "b": ((b_x1r, b_x1l), (b_x2r, b_x2l), (b_y,)),
        }
        return [
            rc(src, dst, "ex", k * 10 + i, device)
            for part in which
            for src, dst, i, device in steps[part][step]
        ]

    def ex_arrived(k, step, which="ab"):
        for cp in ex_copies(k, step, which):
            cp.wait_recv()

    def ex_send(k, step, which):
        for cp in ex_copies(k, step, which):
            cp.start()

    def b2(k):
        rows_r, rows_l = span(k, "r"), span(k, "l")
        ex_arrived(k, 0, "b")
        pb[1, :, rows_r] += xb1[0, :, rows_r]
        pb[3, :, rows_l] += xb1[1, :, rows_l]
        ex_send(k, 1, "b")

    def a2(k):
        every = span(k, "all")
        ex_arrived(k, 0, "a")
        pa[:, 0, every] += ya[:, every]
        ex_send(k, 1, "a")

    def b3(k):
        every = span(k, "all")
        ex_arrived(k, 1, "b")
        pb[0, :, every] += xb2[0, :, every] + xb2[1, :, every]
        ex_send(k, 2, "b")

    def a3(k):
        rows_r, rows_l = span(k, "r"), span(k, "l")
        ex_arrived(k, 1, "a")
        pa[1, 0, rows_r] += xa1[0, rows_r]
        pa[3, 0, rows_l] += xa1[1, rows_l]
        ex_send(k, 2, "a")

    def fin(k):
        ex_arrived(k, 2)
        for i, (_, zz) in enumerate(units(k)):
            rows = pl.ds(CHUNK_AT[k] + 32 * i, 32)
            t4[0, zz] = pa[0, 0, rows] + xa2[0, rows] + xa2[1, rows]
            t4[1, zz] = pb[0, 0, rows] + yb[rows]

    def teacher_chunk(k):
        for i, (_, zz) in enumerate(units(k)):
            for half in range(2):
                block = h5[half, zz].reshape(32, 2048).astype(f32)
                squares = block * block
                total = squares[:, 0:128]
                for lane in range(128, 2048, 128):
                    total = total + squares[:, lane : lane + 128]
                ssq[half, zz] = total
                at = CHUNK_ROWS[k] * half + 32 * i
                scaled[at : at + 32, :] = (block * tg).astype(bf16)
        m = CHUNK_ROWS[k]

        def product(xo, yo):
            d = lax.rem(x + xo, 4) * 2 + lax.rem(yl + yo, 2)
            columns = pl.ds(pl.multiple_of(d * SLICE, SLICE), SLICE)
            both = jnp.dot(scaled[0 : 2 * m, :], head[:, columns], preferred_element_type=f32)
            pa[xo, yo, CHUNK_AT[k] : CHUNK_AT[k] + m, :] = both[0:m]
            pb[xo, yo, CHUNK_AT[k] : CHUNK_AT[k] + m, :] = both[m : 2 * m]

        def other_y(xo, carry):
            product(xo, 1)
            return carry

        lax.fori_loop(0, 4, other_y, 0)
        ex_send(k, 0, "a")
        product(2, 0)
        ex_send(k, 0, "b")
        for xo in (1, 3, 0):
            product(xo, 0)

    def tchunk(k):
        if k == 0:
            load_head.wait()
        sib_arrived(h5, "t", k)
        teacher_chunk(k)

    def sstart():
        arrived(f5.at[1 - yh, z, c], "s_yh", 0)
        ring_send(f5, "s", 0, 0)
        ring_send(f5, "s", 0, 1)
        for cp in sib_copies(f5, "s", 0):
            cp.start()

    def fold(*rows):
        pieces = [v[:, 128 * i : 128 * i + 128] for v in rows for i in range(4)]
        row = lax.broadcasted_iota(jnp.int32, (8, 128), 0)
        out = jnp.zeros((8, 128), f32)
        for i, piece in enumerate(pieces):
            out = jnp.where(row == i, piece, out)
        return out

    def unfold(tile, first):
        return jnp.concatenate([tile[first + i : first + i + 1, :] for i in range(4)], axis=1)

    def sq_copy(j):
        return rc(sqs, sqr.at[j - 1], "sq", j, (tp, lax.rem(dp + j, 8)))

    wt_copy = rc(wt.at[0:SLICE], wt.at[SLICE : 2 * SLICE], "wt", 0, sibling)

    def sq():
        sqs[...] = fold(jnp.sum(ssq[...].reshape(TOKENS, 128).T, 0, keepdims=True))
        for j in range(1, 8):
            sq_copy(j).start()
        wt_copy.start()

    def slog(piece):
        blocks = []
        for s in PIECES[piece]:
            sib_arrived(f5, "s", s)
            blocks += [zz for _, zz in units(s)]
        rows = jnp.concatenate([f5[:, zz].reshape(64, D_S) for zz in blocks], axis=0)
        product = jnp.dot(rows, w[...], preferred_element_type=f32)
        for i, zz in enumerate(blocks):
            s4[0, zz] = product[64 * i : 64 * i + 32]
            s4[1, zz] = product[64 * i + 32 : 64 * i + 64]

    steps = {
        "turn": turn, "t0": t0, "feat": feat, "tchunk": tchunk, "sstart": sstart,
        "th": functools.partial(ring_step, h5, "t"), "sstep": functools.partial(ring_step, f5, "s"),
        "b2": b2, "a2": a2, "b3": b3, "a3": a3, "sq": sq, "slog": slog, "fin": fin,
    }
    for step, *where in FRONT:
        steps[step](*where)

    first = (tp * 8 + dp) * SLICE
    target_mask = ids_ref[...] == first + lax.broadcasted_iota(jnp.int32, (SLICE, TOKENS), 0)
    student = s4[...].reshape(TOKENS, SLICE).T
    s_top = jnp.max(student, 0, keepdims=True)
    s_total = jnp.sum(jnp.exp(student - s_top), 0, keepdims=True)
    target = jnp.sum(jnp.where(target_mask, student, 0.0), 0, keepdims=True)

    for j in range(1, 8):
        arrived(sqr.at[j - 1], "sq", j)
    square_total = sqs[...]
    for j in range(7):
        square_total = square_total + sqr[j]
    t_inv = unfold(lax.rsqrt(square_total / D_T + epsilon), 0)
    teacher = t4[...].reshape(TOKENS, SLICE).T * t_inv

    t_top = jnp.max(teacher, 0, keepdims=True)
    t_exp = jnp.exp(teacher - t_top)
    t_total = jnp.sum(t_exp, 0, keepdims=True)
    cross = jnp.sum(t_exp * (teacher - student), 0, keepdims=True)
    stats = (fold(t_top, s_top), fold(t_total, s_total), fold(cross, target))

    def exchange(buf, name, axis, value):
        if isinstance(value, tuple):
            for i, v in enumerate(value):
                buf[mine[axis], i] = v
        else:
            buf[mine[axis]] = value
        for j in range(1, size[axis]):
            exchange_copy(buf, name, axis, j).start()

    def exchange_copy(buf, name, axis, j):
        slot = buf.at[mine[axis]]
        return rc(slot, slot, name + "_" + axis, j, peer(axis, j))

    def exchanged(buf, name, axis):
        n = size[axis]
        for j in range(1, n):
            arrived(buf.at[lax.rem(mine[axis] + n - j, n)], name + "_" + axis, j)
        return [buf[i] for i in range(n)]

    upper = lax.broadcasted_iota(jnp.int32, (8, 128), 0) < 4

    def merged(parts):
        top = functools.reduce(jnp.maximum, [p[0] for p in parts])
        total = other = 0.0
        for p in parts:
            factor = jnp.exp(p[0] - top)
            total = total + p[1] * factor
            other = other + p[2] * jnp.where(upper, factor, 1.0)
        return top, total, other

    def front_left():
        for buf, name in ((h5, "t"), (f5, "s")):
            yh_copy(buf, name).wait_send()
            for s in range(4):
                for cp in half_copies(buf, name, s, 0) + half_copies(buf, name, s, 1):
                    cp.wait_send()
            for s in range(5):
                for cp in sib_copies(buf, name, s):
                    cp.wait_send()
        wt_copy.wait_send()

    def exchange_left():
        for j in range(1, 8):
            s0_copy(j).wait_send()
            sq_copy(j).wait_send()
        for k in range(5):
            for step in range(3):
                for cp in ex_copies(k, step):
                    cp.wait_send()

    for axis, buf in (("cx", st_cx), ("y", st_y), ("z", st_z)):
        exchange(buf, "st", axis, stats)
        if axis == "cx":
            front_left()
        if axis == "z":
            exchange_left()
        stats = merged(exchanged(buf, "st", axis))

    top, total, other = stats
    lse = top + jnp.log(total)
    t_lse, s_lse = unfold(lse, 0), unfold(lse, 4)
    cross_mean, target = unfold(other / total, 0), unfold(other, 4)
    loss_ref[...] = cross_mean - t_lse + s_lse + hard_weight * (s_lse - target)
    t_prob = jnp.exp(teacher - t_lse)
    s_prob = jnp.exp(student - s_lse)
    onehot = target_mask.astype(f32)
    g = (loss_scale * (s_prob - t_prob + hard_weight * (s_prob - onehot))).astype(bf16)

    gp[...] = jnp.dot(g, perm[...], preferred_element_type=f32).astype(bf16).T

    other_rows = pl.ds(pl.multiple_of((1 - c) * 256, 256), 256)
    own_rows = pl.ds(pl.multiple_of(c * 256, 256), 256)
    gp_copy = rc(gp.at[other_rows], gr, "gp", 0, sibling)
    gp_copy.start()
    first_own = [
        jnp.dot(gp[own_rows, :], wt[0:SLICE, at : at + 512], preferred_element_type=f32)
        for at in (ORDER[0] * WIDE, ORDER[0] * WIDE + 512)
    ]
    for axis, buf in (("cx", st_cx), ("y", st_y), ("z", st_z)):
        for j in range(1, size[axis]):
            exchange_copy(buf, "st", axis, j).wait_send()

    def shard(ch, o, part=slice(0, 4)):
        if ch < 2:
            return rs.at[ch, lax.rem(x + o, 4), part]
        return rs.at[ch, part, lax.rem(y + o, 4)]

    y_right = peer("y", 1)
    y_left = peer("y", 3)

    def q1_copies(ch):
        r, l = (x_right, x_left) if ch < 2 else (y_right, y_left)
        return (
            rc(shard(ch, 2, slice(0, 2)), q1.at[ch, 0], "q1", ch * 2, r),
            rc(shard(ch, 2, slice(2, 4)), q1.at[ch, 1], "q1", ch * 2 + 1, l),
        )

    def q2_copies(ch):
        r, l = (x_right, x_left) if ch < 2 else (y_right, y_left)
        return (
            rc(shard(ch, 1), q2.at[ch, 0], "q2", ch * 2, r),
            rc(shard(ch, 3), q2.at[ch, 1], "q2", ch * 2 + 1, l),
        )

    arrived(wt.at[SLICE : 2 * SLICE], "wt", 0)
    arrived(gr, "gp", 0)
    both_slices = jnp.concatenate([gp[own_rows, :], gr[...]], axis=1)
    for ch in ORDER:
        for tile in range(2):
            at = ch * WIDE + tile * 512
            if ch == ORDER[0]:
                product = first_own[tile] + jnp.dot(
                    gr[...], wt[SLICE : 2 * SLICE, at : at + 512], preferred_element_type=f32
                )
            else:
                product = jnp.dot(both_slices, wt[:, at : at + 512], preferred_element_type=f32)
            rs[ch, :, :, :, tile * 512 : tile * 512 + 512] = product.astype(bf16).reshape(
                4, 4, 16, 512
            )
        for cp in q1_copies(ch):
            cp.start()
    def head_tile(i, carry):
        at = pl.ds(pl.multiple_of(i * 512, 512), 512)
        features = f5[:, :, :, :, at].reshape(TOKENS, 512)
        tile = jnp.dot(g, features, preferred_element_type=f32)
        cols[pl.ds(i, 1), :] = jnp.sum(tile * wt[0:SLICE, at].astype(f32), 0, keepdims=True)
        gh[at, :] = tile.astype(bf16).T
        return carry

    lax.fori_loop(0, 2, head_tile, 0)
    for ch in ORDER:
        for cp in q1_copies(ch):
            cp.wait_recv()
        for o, part, way in ((1, slice(0, 2), 0), (3, slice(2, 4), 1)):
            ref = shard(ch, o, part)
            ref[...] = (ref[...].astype(f32) + q1[ch, way].astype(f32)).astype(bf16)
        for cp in q2_copies(ch):
            cp.start()

    def rs2_copy(ch, j):
        if ch < 2:
            return rc(s2.at[ch, lax.rem(y + j, 4)], r2.at[ch, j - 1], "rs2", ch * 4 + j, peer("y", j))
        return rc(s2.at[ch, lax.rem(x + j, 4)], r2.at[ch, j - 1], "rs2", ch * 4 + j, peer("x", j))

    lax.fori_loop(2, 6, head_tile, 0)
    for ch in ORDER:
        if ch == ORDER[2]:
            lax.fori_loop(6, 8, head_tile, 0)
            store_head = pltpu.make_async_copy(gh, ghead_hbm, ssem.at[BASE["load"] + 2])
            store_head.start()
            exchange(ga_z, "ga", "z", cols[...])
        for cp in q2_copies(ch):
            cp.wait_recv()
        kept = shard(ch, 0)[...].astype(f32)
        total = kept + (q2[ch, 0].astype(f32) + q2[ch, 1].astype(f32))
        s2[ch] = total.astype(bf16)
        for j in range(1, 4):
            rs2_copy(ch, j).start()

    gain = functools.reduce(jnp.add, exchanged(ga_z, "ga", "z"))
    exchange(ga_cx, "ga", "cx", gain)

    for ch in ORDER:
        for j in range(1, 4):
            arrived(r2.at[ch, j - 1], "rs2", ch * 4 + j)
        kept = s2[ch, y] if ch < 2 else s2[ch, x]
        total = kept.astype(f32)
        for j in range(3):
            total = total + r2[ch, j].astype(f32)
        for zz in range(8):
            for half in range(2):
                at = 4 * ch + 2 * half
                zf[zz, at : at + 2, :] = total[2 * zz : 2 * zz + 2, 512 * half : 512 * half + 512]
    zb[...] = zf[...].astype(bf16)

    def rs3_copy(j):
        return rc(zb.at[lax.rem(z + j, 8)], r3.at[j - 1], "rs3", j, peer("z", j))

    for j in range(1, 8):
        rs3_copy(j).start()

    gain = functools.reduce(jnp.add, exchanged(ga_cx, "ga", "cx"))
    exchange(ga_y, "ga", "y", gain)

    def gains_left(*axes):
        for axis, buf in (("cx", ga_cx), ("y", ga_y), ("z", ga_z)):
            if axis in axes:
                for j in range(1, size[axis]):
                    exchange_copy(buf, "ga", axis, j).wait_send()

    gains_left("z", "cx")
    gp_copy.wait_send()
    for ch in range(4):
        for cp in q1_copies(ch) + q2_copies(ch):
            cp.wait_send()
        for j in range(1, 4):
            rs2_copy(ch, j).wait_send()

    own_wide = sh_ref[...].astype(f32)
    own_inv = lax.rsqrt(jnp.sum(own_wide * own_wide, -1, keepdims=True) / D_S + epsilon)
    own_normed = own_wide * own_inv
    for j in range(1, 8):
        arrived(r3.at[j - 1], "rs3", j)
    folded = zf[z]
    for j in range(7):
        folded = folded + r3[j].astype(f32)
    for i in range(8):
        unfolded[:, 512 * i : 512 * i + 512] = folded[2 * i : 2 * i + 2, :]
    grad_normed = unfolded[...] * gain_row
    inner = jnp.sum(grad_normed * own_normed, -1, keepdims=True) / D_S
    ghid_ref[...] = own_inv * (grad_normed - own_normed * inner)

    gain = functools.reduce(jnp.add, exchanged(ga_y, "ga", "y"))
    row = lax.broadcasted_iota(jnp.int32, (8, 512), 0)
    gain_rows = jnp.ones((8, 512), f32)
    for i in range(8):
        gain_rows = jnp.where(row == i, gain_row[:, 512 * i : 512 * i + 512], gain_rows)
    ggain_ref[...] = gain / gain_rows

    gains_left("y")
    for j in range(1, 8):
        rs3_copy(j).wait_send()
    store_head.wait()


def finish(loss_ref, hidden_ref, gain_ref, head_ref, loss_out, hidden_out, gain_out, head_out):
    head_out[...] = head_ref[...]

    @pl.when(pl.program_id(0) == 0)
    def _():
        loss_out[...] = loss_ref[...]
        hidden_out[...] = hidden_ref[...].astype(bf16)
        for i in range(8):
            gain_out[:, 512 * i : 512 * i + 512] = gain_ref[i : i + 1, :]


def shards(
    teacher_hidden,
    teacher_gain,
    teacher_head,
    student_hidden,
    student_gain,
    student_head,
    token_ids,
):
    vmem = pl.BlockSpec(memory_space=pltpu.VMEM)
    hbm = pl.BlockSpec(memory_space=pl.ANY)
    block = pl.BlockSpec((2048, SLICE), lambda i: (i, 0))

    def whole(*shape):
        return pl.BlockSpec(shape, lambda i: (0, 0))

    row8 = (8, TOKENS)
    scratch = [
        ((2048, 2048), bf16), ((D_S, SLICE), bf16), ((2 * SLICE, D_S), bf16), ((2, 8, 2, 16, 2048), bf16),
        ((128, 2048), bf16), ((4, 2, 256, SLICE), f32), ((4, 2, 256, SLICE), f32),
        ((4, 256, SLICE), f32), ((2, 256, SLICE), f32), ((2, 256, SLICE), f32),
        ((2, 2, 256, SLICE), f32), ((2, 2, 256, SLICE), f32), ((256, SLICE), f32),
        ((2, 8, 32, 128), f32), ((8, 128), f32), ((7, 8, 128), f32),
        ((8, 2, D_S), f32), ((16, D_S), f32), ((2, 8, 2, 16, D_S), bf16),
        ((2, 8, 32, SLICE), f32), ((2, 8, 32, SLICE), f32), ((8, 512), f32),
        ((8, 3, 8, 128), f32), ((4, 3, 8, 128), f32), ((8, 3, 8, 128), f32),
        ((8,) + row8, f32), ((4,) + row8, f32), ((8,) + row8, f32),
        ((TOKENS, SLICE), bf16), ((256, SLICE), bf16), ((TOKENS, TOKENS), bf16), ((D_S, SLICE), bf16),
        ((4, 4, 4, 16, WIDE), bf16), ((4, 2, 2, 16, WIDE), bf16), ((4, 2, 4, 16, WIDE), bf16),
        ((4, 4, 16, WIDE), bf16), ((4, 3, 16, WIDE), bf16),
        ((8, 16, 512), f32), ((8, 16, 512), bf16), ((7, 16, 512), bf16), ((2, D_S), f32),
    ]
    loss, grad_head, grad_hidden, grad_gain = pl.pallas_call(
        kernel,
        out_shape=(
            jax.ShapeDtypeStruct((1, TOKENS), f32),
            jax.ShapeDtypeStruct((D_S, SLICE), bf16),
            jax.ShapeDtypeStruct((2, D_S), f32),
            jax.ShapeDtypeStruct((8, 512), f32),
        ),
        in_specs=[vmem, vmem, hbm, vmem, vmem, hbm, vmem],
        out_specs=(vmem, hbm, vmem, vmem),
        scratch_shapes=[pltpu.VMEM(shape, dtype) for shape, dtype in scratch]
        + [pltpu.SemaphoreType.DMA((N_SEMS,)), pltpu.SemaphoreType.DMA((N_SEMS,))],
        compiler_params=pltpu.CompilerParams(
            collective_id=0, has_side_effects=True, vmem_limit_bytes=56 * 1024 * 1024
        ),
        cost_estimate=pl.CostEstimate(
            flops=7_600_000_000, bytes_accessed=13_000_000, transcendentals=600_000
        ),
    )(
        teacher_hidden,
        teacher_gain,
        teacher_head,
        student_hidden,
        student_gain,
        student_head,
        token_ids.reshape(1, TOKENS),
    )
    loss, grad_hidden, grad_gain, grad_head = pl.pallas_call(
        finish,
        out_shape=(
            jax.ShapeDtypeStruct((1, TOKENS), f32),
            jax.ShapeDtypeStruct((2, D_S), bf16),
            jax.ShapeDtypeStruct((1, D_S), f32),
            jax.ShapeDtypeStruct((D_S, SLICE), bf16),
        ),
        grid=(2,),
        in_specs=[whole(1, TOKENS), whole(2, D_S), whole(8, 512), block],
        out_specs=(whole(1, TOKENS), whole(2, D_S), whole(1, D_S), block),
        compiler_params=pltpu.CompilerParams(vmem_limit_bytes=56 * 1024 * 1024),
    )(loss, grad_hidden, grad_gain, grad_head)
    return loss.reshape(TOKENS), grad_hidden, grad_gain.reshape(D_S), grad_head


def solution(mesh):
    in_specs = (
        P("tp", "dp"),
        P("dp"),
        P("dp", "tp"),
        P(("tp", "dp"), None),
        P(),
        P(None, ("tp", "dp")),
        P(),
    )
    out_specs = (P(), P(("tp", "dp"), None), P(), P(None, ("tp", "dp")))
    return jax.shard_map(shards, mesh=mesh, in_specs=in_specs, out_specs=out_specs, check_vma=False)
```

```python
import functools

import jax
import jax.numpy as jnp
from jax import lax
from jax.experimental import pallas as pl
from jax.experimental.pallas import tpu as pltpu
from jax.sharding import PartitionSpec as P

D_T = 16384
D_S = 4096
TOKENS = 512
SLICE = 256

epsilon = 1e-05
hard_weight = 0.5
loss_scale = 64.0

MESH = pl.DeviceIdType.MESH
f32 = jnp.float32
bf16 = jnp.bfloat16

CHUNK_ROWS = (32, 64, 64, 64, 32)
CHUNK_AT = (0, 32, 96, 160, 224)
ORDER = (0, 2, 1, 3)
WIDE = 1024


FRONT = (
    ("turn",), ("th", 0, 0), ("t0",), ("th", 1, 0), ("feat",), ("th", 0, 1), ("tchunk", 0),
    ("th", 1, 1), ("th", 2, 0), ("sstart",), ("tchunk", 1), ("th", 2, 1), ("b2", 0), ("a2", 0),
    ("tchunk", 2), ("b2", 1), ("sstep", 0, 0), ("th", 3, 0), ("tchunk", 3), ("th", 3, 1),
    ("sstep", 0, 1), ("b3", 0), ("a3", 0), ("b2", 2), ("a2", 1), ("sstep", 1, 0),
    ("tchunk", 4), ("sstep", 1, 1), ("b2", 3), ("a2", 2), ("sstep", 2, 0), ("b3", 1),
    ("a3", 1), ("a2", 3), ("sstep", 2, 1), ("b3", 2), ("fin", 0), ("b2", 4), ("slog", 0),
    ("a3", 2), ("a2", 4), ("a3", 3), ("sstep", 3, 0), ("b3", 3), ("b3", 4), ("sstep", 3, 1),
    ("sq",), ("fin", 1), ("a3", 4), ("slog", 1), ("fin", 2), ("fin", 3), ("slog", 2),
    ("fin", 4),
)
PIECES = ((0, 1), (2,), (3, 4))


class Sems:
    def __init__(self):
        self.count = 0

    def take(self, n):
        at = self.count
        self.count += n
        return at


def layout():
    s = Sems()
    base = {}
    for name, n in (
        ("load", 3),
        ("t_yh", 1), ("t_r", 8), ("t_l", 8), ("t_s", 8),
        ("s_yh", 1), ("s_r", 8), ("s_l", 8), ("s_s", 8),
        ("s0", 8), ("ex", 50), ("sq", 8),
        ("st_cx", 8), ("st_y", 4), ("st_z", 8),
        ("ga_cx", 8), ("ga_y", 4), ("ga_z", 8),
        ("wt", 1), ("gp", 1), ("q1", 8), ("q2", 8), ("q3", 8), ("rs2", 16), ("rs3", 8),
    ):
        base[name] = s.take(n)
    return base, s.count


BASE, N_SEMS = layout()


def kernel(
    th_ref, tg_ref, thead_hbm, sh_ref, sg_ref, shead_hbm, ids_ref,
    loss_ref, ghead_hbm, ghid_ref, ggain_ref,
    head, w, wt, h5, scaled, pa, pb, ya, xa1, xa2, xb1, xb2, yb, ssq, sqs, sqr,
    s0, s16, f5, t4, s4, cols,
    st_cx, st_y, st_z, ga_cx, ga_y, ga_z,
    gp, gr, perm, gh, rs, q1, q2, s2, r2, zf, zb, r3, unfolded,
    ssem, rsem,
):
    tp = lax.axis_index("tp")
    dp = lax.axis_index("dp")
    c = lax.rem(tp, 2)
    z = lax.rem(lax.div(tp, 2), 8)
    yh = lax.div(tp, 16)
    x = lax.div(dp, 2)
    yl = lax.rem(dp, 2)
    y = yh * 2 + yl

    def dev(xx, yy, zz, cc):
        return (lax.div(yy, 2) * 16 + zz * 2 + cc, xx * 2 + lax.rem(yy, 2))

    def zmod(v):
        return lax.rem(v + 16, 8)

    def peer(axis, j):
        if axis == "c":
            return dev(x, y, z, lax.rem(c + j, 2))
        if axis == "x":
            return dev(lax.rem(x + j, 4), y, z, c)
        if axis == "y":
            return dev(x, lax.rem(y + j, 4), z, c)
        if axis == "cx":
            at = lax.rem(x * 2 + c + j, 8)
            return dev(lax.div(at, 2), y, z, lax.rem(at, 2))
        return dev(x, y, lax.rem(z + j, 8), c)

    size = {"cx": 8, "y": 4, "z": 8}
    mine = {"cx": x * 2 + c, "y": y, "z": z}

    def rc(src, dst, name, i, device):
        at = BASE[name] + i
        return pltpu.make_async_remote_copy(
            src_ref=src, dst_ref=dst, send_sem=ssem.at[at], recv_sem=rsem.at[at],
            device_id=device, device_id_type=MESH,
        )

    def arrived(dst, name, i):
        rc(dst, dst, name, i, peer("c", 1)).wait_recv()

    load_head = pltpu.make_async_copy(thead_hbm, head, ssem.at[BASE["load"]])
    load_w = pltpu.make_async_copy(shead_hbm, w, ssem.at[BASE["load"] + 1])
    load_w.start()
    load_head.start()

    barrier = pltpu.get_barrier_semaphore()
    partners = [peer("c", 1)]
    partners += [dev((x + j) % 4, y, z, cc) for j in range(1, 4) for cc in range(2)]
    partners += [peer("y", j) for j in range(1, 4)]
    partners += [dev((x + j) % 4, yh * 2 + 1 - yl, z, c) for j in range(1, 4)]
    partners += [peer("z", j) for j in range(1, 8)]
    for device in partners:
        pl.semaphore_signal(barrier, inc=1, device_id=device, device_id_type=MESH)

    h5[yh, z, c] = th_ref[...]
    s0[dp] = sh_ref[...].astype(f32)

    p = lax.broadcasted_iota(jnp.int32, (TOKENS, TOKENS), 1)
    q = lax.broadcasted_iota(jnp.int32, (TOKENS, TOKENS), 0)
    source = (
        ((p >> 5) & 1) * 256
        + ((p >> 1) & 7) * 32
        + (p >> 8) * 16
        + ((p >> 6) & 3) * 4
        + ((p >> 4) & 1) * 2
        + (p & 1)
    )
    perm[...] = jnp.where(q == source, 1.0, 0.0).astype(bf16)

    pl.semaphore_wait(barrier, len(partners))

    yh_peer = dev(x, (y + 2) % 4, z, c)
    sibling = peer("c", 1)
    right = peer("z", 1)
    left = peer("z", 7)

    y_outer = dev(x, 3 - y, z, c)

    def yh_copy(buf, name):
        own_block = buf.at[yh, z, c]
        return rc(own_block, own_block, name + "_yh", 0, yh_peer if name == "t" else y_outer)

    def half_copies(buf, name, s, half):
        of = yh if half == 0 else 1 - yh
        r, l = buf.at[of, zmod(z - s), c], buf.at[of, zmod(z + s), c]
        copies = []
        if s < 3 or half == 0:
            copies.append(rc(r, r, name + "_r", 2 * s + half, right))
        if s < 3 or half == 1:
            copies.append(rc(l, l, name + "_l", 2 * s + half, left))
        return copies

    def half_arrived(buf, name, s, half):
        of = yh if half == 0 else 1 - yh
        if s < 3 or half == 0:
            arrived(buf.at[of, zmod(z - 1 - s), c], name + "_r", 2 * s + half)
        if s < 3 or half == 1:
            arrived(buf.at[of, zmod(z + 1 + s), c], name + "_l", 2 * s + half)

    def ring_send(buf, name, s, half):
        for cp in half_copies(buf, name, s, half):
            cp.start()

    def ring_step(buf, name, s, half):
        half_arrived(buf, name, s, half)
        if s < 3:
            ring_send(buf, name, s + 1, half)
        if half == 1:
            for cp in sib_copies(buf, name, s + 1):
                cp.start()

    def units(s):
        if s == 0:
            return [(0, z)]
        if s == 4:
            return [(7, zmod(z + 4))]
        return [(2 * s - 1, zmod(z - s)), (2 * s, zmod(z + s))]

    def sib_copies(buf, name, s):
        return [
            rc(buf.at[:, zz, c], buf.at[:, zz, c], name + "_s", k, sibling) for k, zz in units(s)
        ]

    def sib_arrived(buf, name, s):
        for k, zz in units(s):
            arrived(buf.at[:, zz, 1 - c], name + "_s", k)

    yh_copy(h5, "t").start()
    ring_send(h5, "t", 0, 0)

    def s0_copy(j):
        return rc(s0.at[dp], s0.at[dp], "s0", j, (tp, lax.rem(dp + j, 8)))

    for j in range(1, 8):
        s0_copy(j).start()

    def turn():
        load_w.wait()

        def tile(i, carry):
            at = pl.ds(pl.multiple_of(i * 512, 512), 512)
            wt[0:SLICE, at] = w[at, :].T
            return carry

        lax.fori_loop(0, 8, tile, 0)

    def t0():
        arrived(h5.at[1 - yh, z, c], "t_yh", 0)
        ring_send(h5, "t", 0, 1)
        for cp in sib_copies(h5, "t", 0):
            cp.start()

    gain_row = sg_ref[...].astype(f32).reshape(1, D_S)

    def feat():
        for j in range(1, 8):
            arrived(s0.at[lax.rem(dp + 8 - j, 8)], "s0", j)
        for d in range(8):
            s16[2 * d : 2 * d + 2, :] = s0[d]
        wide = s16[...]
        inv16 = lax.rsqrt(jnp.sum(wide * wide, -1, keepdims=True) / D_S + epsilon)
        f5[yh, z, c] = (wide * inv16 * gain_row).astype(bf16)
        yh_copy(f5, "s").start()

    tg = tg_ref[...].astype(f32).reshape(1, 2048)

    x_right = peer("x", 1)
    x_left = peer("x", 3)
    y_pair = dev(x, yh * 2 + 1 - yl, z, c)

    def span(k, part):
        at, n = CHUNK_AT[k], CHUNK_ROWS[k]
        return {"all": pl.ds(at, n), "r": pl.ds(at, n // 2), "l": pl.ds(at + n // 2, n // 2)}[part]

    def ex_copies(k, step, which="ab"):
        every, rows_r, rows_l = span(k, "all"), span(k, "r"), span(k, "l")
        a_y = (pa.at[:, 1, every], ya.at[:, every], 0, y_pair)
        a_x1r = (pa.at[2, 0, rows_r], xa1.at[0, rows_r], 1, x_right)
        a_x1l = (pa.at[2, 0, rows_l], xa1.at[1, rows_l], 2, x_left)
        a_x2r = (pa.at[1, 0, every], xa2.at[0, every], 3, x_right)
        a_x2l = (pa.at[3, 0, every], xa2.at[1, every], 4, x_left)
        b_x1r = (pb.at[2, :, rows_r], xb1.at[0, :, rows_r], 5, x_right)
        b_x1l = (pb.at[2, :, rows_l], xb1.at[1, :, rows_l], 6, x_left)
        b_x2r = (pb.at[1, :, every], xb2.at[0, :, every], 7, x_right)
        b_x2l = (pb.at[3, :, every], xb2.at[1, :, every], 8, x_left)
        b_y = (pb.at[0, 1, every], yb.at[every], 9, y_pair)
        steps = {
            "a": ((a_y,), (a_x1r, a_x1l), (a_x2r, a_x2l)),
            "b": ((b_x1r, b_x1l), (b_x2r, b_x2l), (b_y,)),
        }
        return [
            rc(src, dst, "ex", k * 10 + i, device)
            for part in which
            for src, dst, i, device in steps[part][step]
        ]

    def ex_arrived(k, step, which="ab"):
        for cp in ex_copies(k, step, which):
            cp.wait_recv()

    def ex_send(k, step, which):
        for cp in ex_copies(k, step, which):
            cp.start()

    def b2(k):
        rows_r, rows_l = span(k, "r"), span(k, "l")
        ex_arrived(k, 0, "b")
        pb[1, :, rows_r] += xb1[0, :, rows_r]
        pb[3, :, rows_l] += xb1[1, :, rows_l]
        ex_send(k, 1, "b")

    def a2(k):
        every = span(k, "all")
        ex_arrived(k, 0, "a")
        pa[:, 0, every] += ya[:, every]
        ex_send(k, 1, "a")

    def b3(k):
        every = span(k, "all")
        ex_arrived(k, 1, "b")
        pb[0, :, every] += xb2[0, :, every] + xb2[1, :, every]
        ex_send(k, 2, "b")

    def a3(k):
        rows_r, rows_l = span(k, "r"), span(k, "l")
        ex_arrived(k, 1, "a")
        pa[1, 0, rows_r] += xa1[0, rows_r]
        pa[3, 0, rows_l] += xa1[1, rows_l]
        ex_send(k, 2, "a")

    def fin(k):
        ex_arrived(k, 2)
        for i, (_, zz) in enumerate(units(k)):
            rows = pl.ds(CHUNK_AT[k] + 32 * i, 32)
            t4[0, zz] = pa[0, 0, rows] + xa2[0, rows] + xa2[1, rows]
            t4[1, zz] = pb[0, 0, rows] + yb[rows]

    def teacher_chunk(k):
        for i, (_, zz) in enumerate(units(k)):
            for half in range(2):
                block = h5[half, zz].reshape(32, 2048).astype(f32)
                squares = block * block
                total = squares[:, 0:128]
                for lane in range(128, 2048, 128):
                    total = total + squares[:, lane : lane + 128]
                ssq[half, zz] = total
                at = CHUNK_ROWS[k] * half + 32 * i
                scaled[at : at + 32, :] = (block * tg).astype(bf16)
        m = CHUNK_ROWS[k]

        def product(xo, yo):
            d = lax.rem(x + xo, 4) * 2 + lax.rem(yl + yo, 2)
            columns = pl.ds(pl.multiple_of(d * SLICE, SLICE), SLICE)
            both = jnp.dot(scaled[0 : 2 * m, :], head[:, columns], preferred_element_type=f32)
            pa[xo, yo, CHUNK_AT[k] : CHUNK_AT[k] + m, :] = both[0:m]
            pb[xo, yo, CHUNK_AT[k] : CHUNK_AT[k] + m, :] = both[m : 2 * m]

        def other_y(xo, carry):
            product(xo, 1)
            return carry

        lax.fori_loop(0, 4, other_y, 0)
        ex_send(k, 0, "a")
        product(2, 0)
        ex_send(k, 0, "b")
        for xo in (1, 3, 0):
            product(xo, 0)

    def tchunk(k):
        if k == 0:
            load_head.wait()
        sib_arrived(h5, "t", k)
        teacher_chunk(k)

    def sstart():
        arrived(f5.at[1 - yh, z, c], "s_yh", 0)
        ring_send(f5, "s", 0, 0)
        ring_send(f5, "s", 0, 1)
        for cp in sib_copies(f5, "s", 0):
            cp.start()

    def fold(*rows):
        pieces = [v[:, 128 * i : 128 * i + 128] for v in rows for i in range(4)]
        row = lax.broadcasted_iota(jnp.int32, (8, 128), 0)
        out = jnp.zeros((8, 128), f32)
        for i, piece in enumerate(pieces):
            out = jnp.where(row == i, piece, out)
        return out

    def unfold(tile, first):
        return jnp.concatenate([tile[first + i : first + i + 1, :] for i in range(4)], axis=1)

    def sq_copy(j):
        return rc(sqs, sqr.at[j - 1], "sq", j, (tp, lax.rem(dp + j, 8)))

    wt_copy = rc(wt.at[0:SLICE], wt.at[SLICE : 2 * SLICE], "wt", 0, sibling)

    def sq():
        sqs[...] = fold(jnp.sum(ssq[...].reshape(TOKENS, 128).T, 0, keepdims=True))
        for j in range(1, 8):
            sq_copy(j).start()
        wt_copy.start()

    def slog(piece):
        blocks = []
        for s in PIECES[piece]:
            sib_arrived(f5, "s", s)
            blocks += [zz for _, zz in units(s)]
        rows = jnp.concatenate([f5[:, zz].reshape(64, D_S) for zz in blocks], axis=0)
        product = jnp.dot(rows, w[...], preferred_element_type=f32)
        for i, zz in enumerate(blocks):
            s4[0, zz] = product[64 * i : 64 * i + 32]
            s4[1, zz] = product[64 * i + 32 : 64 * i + 64]

    steps = {
        "turn": turn, "t0": t0, "feat": feat, "tchunk": tchunk, "sstart": sstart,
        "th": functools.partial(ring_step, h5, "t"), "sstep": functools.partial(ring_step, f5, "s"),
        "b2": b2, "a2": a2, "b3": b3, "a3": a3, "sq": sq, "slog": slog, "fin": fin,
    }
    for step, *where in FRONT:
        steps[step](*where)

    first = (tp * 8 + dp) * SLICE
    target_mask = ids_ref[...] == first + lax.broadcasted_iota(jnp.int32, (SLICE, TOKENS), 0)
    student = s4[...].reshape(TOKENS, SLICE).T
    s_top = jnp.max(student, 0, keepdims=True)
    s_total = jnp.sum(jnp.exp(student - s_top), 0, keepdims=True)
    target = jnp.sum(jnp.where(target_mask, student, 0.0), 0, keepdims=True)

    for j in range(1, 8):
        arrived(sqr.at[j - 1], "sq", j)
    square_total = sqs[...]
    for j in range(7):
        square_total = square_total + sqr[j]
    t_inv = unfold(lax.rsqrt(square_total / D_T + epsilon), 0)
    teacher = t4[...].reshape(TOKENS, SLICE).T * t_inv

    t_top = jnp.max(teacher, 0, keepdims=True)
    t_exp = jnp.exp(teacher - t_top)
    t_total = jnp.sum(t_exp, 0, keepdims=True)
    cross = jnp.sum(t_exp * (teacher - student), 0, keepdims=True)
    stats = (fold(t_top, s_top), fold(t_total, s_total), fold(cross, target))

    def exchange(buf, name, axis, value):
        if isinstance(value, tuple):
            for i, v in enumerate(value):
                buf[mine[axis], i] = v
        else:
            buf[mine[axis]] = value
        for j in range(1, size[axis]):
            exchange_copy(buf, name, axis, j).start()

    def exchange_copy(buf, name, axis, j):
        slot = buf.at[mine[axis]]
        return rc(slot, slot, name + "_" + axis, j, peer(axis, j))

    def exchanged(buf, name, axis):
        n = size[axis]
        for j in range(1, n):
            arrived(buf.at[lax.rem(mine[axis] + n - j, n)], name + "_" + axis, j)
        return [buf[i] for i in range(n)]

    upper = lax.broadcasted_iota(jnp.int32, (8, 128), 0) < 4

    def merged(parts):
        top = functools.reduce(jnp.maximum, [p[0] for p in parts])
        total = other = 0.0
        for p in parts:
            factor = jnp.exp(p[0] - top)
            total = total + p[1] * factor
            other = other + p[2] * jnp.where(upper, factor, 1.0)
        return top, total, other

    def front_left():
        for buf, name in ((h5, "t"), (f5, "s")):
            yh_copy(buf, name).wait_send()
            for s in range(4):
                for cp in half_copies(buf, name, s, 0) + half_copies(buf, name, s, 1):
                    cp.wait_send()
            for s in range(5):
                for cp in sib_copies(buf, name, s):
                    cp.wait_send()
        wt_copy.wait_send()

    def exchange_left():
        for j in range(1, 8):
            s0_copy(j).wait_send()
            sq_copy(j).wait_send()
        for k in range(5):
            for step in range(3):
                for cp in ex_copies(k, step):
                    cp.wait_send()

    for axis, buf in (("cx", st_cx), ("y", st_y), ("z", st_z)):
        exchange(buf, "st", axis, stats)
        if axis == "cx":
            front_left()
        if axis == "z":
            exchange_left()
        stats = merged(exchanged(buf, "st", axis))

    top, total, other = stats
    lse = top + jnp.log(total)
    t_lse, s_lse = unfold(lse, 0), unfold(lse, 4)
    cross_mean, target = unfold(other / total, 0), unfold(other, 4)
    loss_ref[...] = cross_mean - t_lse + s_lse + hard_weight * (s_lse - target)
    t_prob = jnp.exp(teacher - t_lse)
    s_prob = jnp.exp(student - s_lse)
    onehot = target_mask.astype(f32)
    g = (loss_scale * (s_prob - t_prob + hard_weight * (s_prob - onehot))).astype(bf16)

    other_rows = pl.ds(pl.multiple_of((1 - c) * 256, 256), 256)
    own_rows = pl.ds(pl.multiple_of(c * 256, 256), 256)
    gp_copy = rc(gp.at[other_rows], gr, "gp", 0, sibling)
    gp[other_rows, :] = jnp.dot(g, perm[:, other_rows], preferred_element_type=f32).astype(bf16).T
    gp_copy.start()
    gp[own_rows, :] = jnp.dot(g, perm[:, own_rows], preferred_element_type=f32).astype(bf16).T
    first_own = [
        jnp.dot(gp[own_rows, :], wt[0:SLICE, at : at + 512], preferred_element_type=f32)
        for at in (ORDER[0] * WIDE, ORDER[0] * WIDE + 512)
    ]
    for axis, buf in (("cx", st_cx), ("y", st_y), ("z", st_z)):
        for j in range(1, size[axis]):
            exchange_copy(buf, "st", axis, j).wait_send()

    def shard(ch, o, part=slice(0, 4)):
        if ch < 2:
            return rs.at[ch, lax.rem(x + o, 4), part]
        return rs.at[ch, part, lax.rem(y + o, 4)]

    y_right = peer("y", 1)
    y_left = peer("y", 3)

    def q1_copies(ch):
        r, l = (x_right, x_left) if ch < 2 else (y_right, y_left)
        return (
            rc(shard(ch, 2, slice(0, 2)), q1.at[ch, 0], "q1", ch * 2, r),
            rc(shard(ch, 2, slice(2, 4)), q1.at[ch, 1], "q1", ch * 2 + 1, l),
        )

    def q2_copies(ch):
        r, l = (x_right, x_left) if ch < 2 else (y_right, y_left)
        low, high = slice(0, 2), slice(2, 4)
        return (
            rc(shard(ch, 1, low), q2.at[ch, 0, low], "q2", ch * 2, r),
            rc(shard(ch, 3, high), q2.at[ch, 1, high], "q2", ch * 2 + 1, l),
        )

    def q3_copies(ch):
        r, l = (x_right, x_left) if ch < 2 else (y_right, y_left)
        low, high = slice(0, 2), slice(2, 4)
        return (
            rc(shard(ch, 1, high), q2.at[ch, 0, high], "q3", ch * 2, r),
            rc(shard(ch, 3, low), q2.at[ch, 1, low], "q3", ch * 2 + 1, l),
        )

    arrived(wt.at[SLICE : 2 * SLICE], "wt", 0)
    arrived(gr, "gp", 0)
    both_slices = jnp.concatenate([gp[own_rows, :], gr[...]], axis=1)
    for ch in ORDER:
        for tile in range(2):
            at = ch * WIDE + tile * 512
            if ch == ORDER[0]:
                product = first_own[tile] + jnp.dot(
                    gr[...], wt[SLICE : 2 * SLICE, at : at + 512], preferred_element_type=f32
                )
            else:
                product = jnp.dot(both_slices, wt[:, at : at + 512], preferred_element_type=f32)
            rs[ch, :, :, :, tile * 512 : tile * 512 + 512] = product.astype(bf16).reshape(
                4, 4, 16, 512
            )
        for cp in q1_copies(ch):
            cp.start()
        for cp in q3_copies(ch):
            cp.start()
    def head_tile(i, carry):
        at = pl.ds(pl.multiple_of(i * 512, 512), 512)
        features = f5[:, :, :, :, at].reshape(TOKENS, 512)
        tile = jnp.dot(g, features, preferred_element_type=f32)
        cols[pl.ds(i, 1), :] = jnp.sum(tile * wt[0:SLICE, at].astype(f32), 0, keepdims=True)
        gh[at, :] = tile.astype(bf16).T
        return carry

    lax.fori_loop(0, 2, head_tile, 0)
    for ch in ORDER:
        for cp in q1_copies(ch):
            cp.wait_recv()
        for o, part, way in ((1, slice(0, 2), 0), (3, slice(2, 4), 1)):
            ref = shard(ch, o, part)
            ref[...] = (ref[...].astype(f32) + q1[ch, way].astype(f32)).astype(bf16)
        for cp in q2_copies(ch):
            cp.start()

    def rs2_copy(ch, j):
        if ch < 2:
            return rc(s2.at[ch, lax.rem(y + j, 4)], r2.at[ch, j - 1], "rs2", ch * 4 + j, peer("y", j))
        return rc(s2.at[ch, lax.rem(x + j, 4)], r2.at[ch, j - 1], "rs2", ch * 4 + j, peer("x", j))

    lax.fori_loop(2, 6, head_tile, 0)
    for ch in ORDER:
        if ch == ORDER[2]:
            lax.fori_loop(6, 8, head_tile, 0)
            store_head = pltpu.make_async_copy(gh, ghead_hbm, ssem.at[BASE["load"] + 2])
            store_head.start()
            exchange(ga_z, "ga", "z", cols[...])
        for cp in q2_copies(ch) + q3_copies(ch):
            cp.wait_recv()
        kept = shard(ch, 0)[...].astype(f32)
        total = kept + (q2[ch, 0].astype(f32) + q2[ch, 1].astype(f32))
        s2[ch] = total.astype(bf16)
        for j in range(1, 4):
            rs2_copy(ch, j).start()

    gain = functools.reduce(jnp.add, exchanged(ga_z, "ga", "z"))
    exchange(ga_cx, "ga", "cx", gain)

    for ch in ORDER:
        for j in range(1, 4):
            arrived(r2.at[ch, j - 1], "rs2", ch * 4 + j)
        kept = s2[ch, y] if ch < 2 else s2[ch, x]
        total = kept.astype(f32)
        for j in range(3):
            total = total + r2[ch, j].astype(f32)
        for zz in range(8):
            for half in range(2):
                at = 4 * ch + 2 * half
                zf[zz, at : at + 2, :] = total[2 * zz : 2 * zz + 2, 512 * half : 512 * half + 512]
    zb[...] = zf[...].astype(bf16)

    def rs3_copy(j):
        return rc(zb.at[lax.rem(z + j, 8)], r3.at[j - 1], "rs3", j, peer("z", j))

    for j in range(1, 8):
        rs3_copy(j).start()

    gain = functools.reduce(jnp.add, exchanged(ga_cx, "ga", "cx"))
    exchange(ga_y, "ga", "y", gain)

    def gains_left(*axes):
        for axis, buf in (("cx", ga_cx), ("y", ga_y), ("z", ga_z)):
            if axis in axes:
                for j in range(1, size[axis]):
                    exchange_copy(buf, "ga", axis, j).wait_send()

    gains_left("z", "cx")
    gp_copy.wait_send()
    for ch in range(4):
        for cp in q1_copies(ch) + q2_copies(ch) + q3_copies(ch):
            cp.wait_send()
        for j in range(1, 4):
            rs2_copy(ch, j).wait_send()

    own_wide = sh_ref[...].astype(f32)
    own_inv = lax.rsqrt(jnp.sum(own_wide * own_wide, -1, keepdims=True) / D_S + epsilon)
    own_normed = own_wide * own_inv
    for j in range(1, 8):
        arrived(r3.at[j - 1], "rs3", j)
    folded = zf[z]
    for j in range(7):
        folded = folded + r3[j].astype(f32)
    for i in range(8):
        unfolded[:, 512 * i : 512 * i + 512] = folded[2 * i : 2 * i + 2, :]
    grad_normed = unfolded[...] * gain_row
    inner = jnp.sum(grad_normed * own_normed, -1, keepdims=True) / D_S
    ghid_ref[...] = own_inv * (grad_normed - own_normed * inner)

    gain = functools.reduce(jnp.add, exchanged(ga_y, "ga", "y"))
    row = lax.broadcasted_iota(jnp.int32, (8, 512), 0)
    gain_rows = jnp.ones((8, 512), f32)
    for i in range(8):
        gain_rows = jnp.where(row == i, gain_row[:, 512 * i : 512 * i + 512], gain_rows)
    ggain_ref[...] = gain / gain_rows

    gains_left("y")
    for j in range(1, 8):
        rs3_copy(j).wait_send()
    store_head.wait()


def finish(loss_ref, hidden_ref, gain_ref, head_ref, loss_out, hidden_out, gain_out, head_out):
    head_out[...] = head_ref[...]

    @pl.when(pl.program_id(0) == 0)
    def _():
        loss_out[...] = loss_ref[...]
        hidden_out[...] = hidden_ref[...].astype(bf16)
        for i in range(8):
            gain_out[:, 512 * i : 512 * i + 512] = gain_ref[i : i + 1, :]


def shards(
    teacher_hidden,
    teacher_gain,
    teacher_head,
    student_hidden,
    student_gain,
    student_head,
    token_ids,
):
    vmem = pl.BlockSpec(memory_space=pltpu.VMEM)
    hbm = pl.BlockSpec(memory_space=pl.ANY)
    block = pl.BlockSpec((2048, SLICE), lambda i: (i, 0))

    def whole(*shape):
        return pl.BlockSpec(shape, lambda i: (0, 0))

    row8 = (8, TOKENS)
    scratch = [
        ((2048, 2048), bf16), ((D_S, SLICE), bf16), ((2 * SLICE, D_S), bf16), ((2, 8, 2, 16, 2048), bf16),
        ((128, 2048), bf16), ((4, 2, 256, SLICE), f32), ((4, 2, 256, SLICE), f32),
        ((4, 256, SLICE), f32), ((2, 256, SLICE), f32), ((2, 256, SLICE), f32),
        ((2, 2, 256, SLICE), f32), ((2, 2, 256, SLICE), f32), ((256, SLICE), f32),
        ((2, 8, 32, 128), f32), ((8, 128), f32), ((7, 8, 128), f32),
        ((8, 2, D_S), f32), ((16, D_S), f32), ((2, 8, 2, 16, D_S), bf16),
        ((2, 8, 32, SLICE), f32), ((2, 8, 32, SLICE), f32), ((8, 512), f32),
        ((8, 3, 8, 128), f32), ((4, 3, 8, 128), f32), ((8, 3, 8, 128), f32),
        ((8,) + row8, f32), ((4,) + row8, f32), ((8,) + row8, f32),
        ((TOKENS, SLICE), bf16), ((256, SLICE), bf16), ((TOKENS, TOKENS), bf16), ((D_S, SLICE), bf16),
        ((4, 4, 4, 16, WIDE), bf16), ((4, 2, 2, 16, WIDE), bf16), ((4, 2, 4, 16, WIDE), bf16),
        ((4, 4, 16, WIDE), bf16), ((4, 3, 16, WIDE), bf16),
        ((8, 16, 512), f32), ((8, 16, 512), bf16), ((7, 16, 512), bf16), ((2, D_S), f32),
    ]
    loss, grad_head, grad_hidden, grad_gain = pl.pallas_call(
        kernel,
        out_shape=(
            jax.ShapeDtypeStruct((1, TOKENS), f32),
            jax.ShapeDtypeStruct((D_S, SLICE), bf16),
            jax.ShapeDtypeStruct((2, D_S), f32),
            jax.ShapeDtypeStruct((8, 512), f32),
        ),
        in_specs=[vmem, vmem, hbm, vmem, vmem, hbm, vmem],
        out_specs=(vmem, hbm, vmem, vmem),
        scratch_shapes=[pltpu.VMEM(shape, dtype) for shape, dtype in scratch]
        + [pltpu.SemaphoreType.DMA((N_SEMS,)), pltpu.SemaphoreType.DMA((N_SEMS,))],
        compiler_params=pltpu.CompilerParams(
            collective_id=0, has_side_effects=True, vmem_limit_bytes=56 * 1024 * 1024
        ),
        cost_estimate=pl.CostEstimate(
            flops=7_600_000_000, bytes_accessed=13_000_000, transcendentals=600_000
        ),
    )(
        teacher_hidden,
        teacher_gain,
        teacher_head,
        student_hidden,
        student_gain,
        student_head,
        token_ids.reshape(1, TOKENS),
    )
    loss, grad_hidden, grad_gain, grad_head = pl.pallas_call(
        finish,
        out_shape=(
            jax.ShapeDtypeStruct((1, TOKENS), f32),
            jax.ShapeDtypeStruct((2, D_S), bf16),
            jax.ShapeDtypeStruct((1, D_S), f32),
            jax.ShapeDtypeStruct((D_S, SLICE), bf16),
        ),
        grid=(2,),
        in_specs=[whole(1, TOKENS), whole(2, D_S), whole(8, 512), block],
        out_specs=(whole(1, TOKENS), whole(2, D_S), whole(1, D_S), block),
        compiler_params=pltpu.CompilerParams(vmem_limit_bytes=56 * 1024 * 1024),
    )(loss, grad_hidden, grad_gain, grad_head)
    return loss.reshape(TOKENS), grad_hidden, grad_gain.reshape(D_S), grad_head


def solution(mesh):
    in_specs = (
        P("tp", "dp"),
        P("dp"),
        P("dp", "tp"),
        P(("tp", "dp"), None),
        P(),
        P(None, ("tp", "dp")),
        P(),
    )
    out_specs = (P(), P(("tp", "dp"), None), P(), P(None, ("tp", "dp")))
    return jax.shard_map(shards, mesh=mesh, in_specs=in_specs, out_specs=out_specs, check_vma=False)
```

```python
import functools

import jax
import jax.numpy as jnp
from jax import lax
from jax.experimental import pallas as pl
from jax.experimental.pallas import tpu as pltpu
from jax.sharding import PartitionSpec as P

D_T = 16384
D_S = 4096
TOKENS = 512
SLICE = 256

epsilon = 1e-05
hard_weight = 0.5
loss_scale = 64.0

MESH = pl.DeviceIdType.MESH
f32 = jnp.float32
bf16 = jnp.bfloat16

CHUNK_ROWS = (32, 64, 64, 64, 32)
CHUNK_AT = (0, 32, 96, 160, 224)
ORDER = (0, 2, 1, 3)
WIDE = 1024


FRONT = (
    ("turn",), ("th", 0, 0), ("t0",), ("th", 1, 0), ("feat",), ("th", 0, 1), ("tchunk", 0),
    ("th", 1, 1), ("th", 2, 0), ("sstart",), ("tchunk", 1), ("th", 2, 1), ("b2", 0), ("a2", 0),
    ("tchunk", 2), ("b2", 1), ("sstep", 0, 0), ("th", 3, 0), ("tchunk", 3), ("th", 3, 1),
    ("sstep", 0, 1), ("b3", 0), ("a3", 0), ("b2", 2), ("a2", 1), ("sstep", 1, 0),
    ("tchunk", 4), ("sstep", 1, 1), ("b2", 3), ("a2", 2), ("sstep", 2, 0), ("b3", 1),
    ("a3", 1), ("a2", 3), ("sstep", 2, 1), ("b3", 2), ("fin", 0), ("b2", 4), ("slog", 0),
    ("a3", 2), ("a2", 4), ("a3", 3), ("sstep", 3, 0), ("b3", 3), ("b3", 4), ("sstep", 3, 1),
    ("sq",), ("fin", 1), ("a3", 4), ("slog", 1), ("fin", 2), ("fin", 3), ("slog", 2),
    ("fin", 4),
)
PIECES = ((0, 1), (2,), (3, 4))


class Sems:
    def __init__(self):
        self.count = 0

    def take(self, n):
        at = self.count
        self.count += n
        return at


def layout():
    s = Sems()
    base = {}
    for name, n in (
        ("load", 3),
        ("t_yh", 1), ("t_r", 8), ("t_l", 8), ("t_s", 8),
        ("s_yh", 1), ("s_r", 8), ("s_l", 8), ("s_s", 8),
        ("s0", 8), ("ex", 50), ("sq", 8),
        ("st_cx", 8), ("st_y", 4), ("st_z", 8),
        ("ga_cx", 8), ("ga_y", 4), ("ga_z", 8),
        ("wt", 1), ("gp", 1), ("q1", 8), ("q2", 8), ("rs2", 16), ("rs3", 8),
    ):
        base[name] = s.take(n)
    return base, s.count


BASE, N_SEMS = layout()


def kernel(
    th_ref, tg_ref, thead_hbm, sh_ref, sg_ref, shead_hbm, ids_ref,
    loss_ref, ghead_hbm, ghid_ref, ggain_ref,
    head, w, wt, h5, scaled, pa, pb, ya, xa1, xa2, xb1, xb2, yb, ssq, sqs, sqr,
    s0, s16, f5, t4, s4, cols,
    st_cx, st_y, st_z, ga_cx, ga_y, ga_z,
    gp, gr, perm, gh, rs, q1, q2, s2, r2, zf, zb, r3, unfolded,
    ssem, rsem,
):
    tp = lax.axis_index("tp")
    dp = lax.axis_index("dp")
    c = lax.rem(tp, 2)
    z = lax.rem(lax.div(tp, 2), 8)
    yh = lax.div(tp, 16)
    x = lax.div(dp, 2)
    yl = lax.rem(dp, 2)
    y = yh * 2 + yl

    def dev(xx, yy, zz, cc):
        return (lax.div(yy, 2) * 16 + zz * 2 + cc, xx * 2 + lax.rem(yy, 2))

    def zmod(v):
        return lax.rem(v + 16, 8)

    def peer(axis, j):
        if axis == "c":
            return dev(x, y, z, lax.rem(c + j, 2))
        if axis == "x":
            return dev(lax.rem(x + j, 4), y, z, c)
        if axis == "y":
            return dev(x, lax.rem(y + j, 4), z, c)
        if axis == "cx":
            at = lax.rem(x * 2 + c + j, 8)
            return dev(lax.div(at, 2), y, z, lax.rem(at, 2))
        return dev(x, y, lax.rem(z + j, 8), c)

    size = {"cx": 8, "y": 4, "z": 8}
    mine = {"cx": x * 2 + c, "y": y, "z": z}

    def rc(src, dst, name, i, device):
        at = BASE[name] + i
        return pltpu.make_async_remote_copy(
            src_ref=src, dst_ref=dst, send_sem=ssem.at[at], recv_sem=rsem.at[at],
            device_id=device, device_id_type=MESH,
        )

    def arrived(dst, name, i):
        rc(dst, dst, name, i, peer("c", 1)).wait_recv()

    load_head = pltpu.make_async_copy(thead_hbm, head, ssem.at[BASE["load"]])
    load_w = pltpu.make_async_copy(shead_hbm, w, ssem.at[BASE["load"] + 1])
    load_w.start()
    load_head.start()

    barrier = pltpu.get_barrier_semaphore()
    partners = [peer("c", 1)]
    partners += [dev((x + j) % 4, y, z, cc) for j in range(1, 4) for cc in range(2)]
    partners += [peer("y", j) for j in range(1, 4)]
    partners += [dev((x + j) % 4, yh * 2 + 1 - yl, z, c) for j in range(1, 4)]
    partners += [peer("z", j) for j in range(1, 8)]
    for device in partners:
        pl.semaphore_signal(barrier, inc=1, device_id=device, device_id_type=MESH)

    h5[yh, z, c] = th_ref[...]
    s0[dp] = sh_ref[...].astype(f32)

    p = lax.broadcasted_iota(jnp.int32, (TOKENS, TOKENS), 1)
    q = lax.broadcasted_iota(jnp.int32, (TOKENS, TOKENS), 0)
    source = (
        ((p >> 5) & 1) * 256
        + ((p >> 1) & 7) * 32
        + (p >> 8) * 16
        + ((p >> 6) & 3) * 4
        + ((p >> 4) & 1) * 2
        + (p & 1)
    )
    perm[...] = jnp.where(q == source, 1.0, 0.0).astype(bf16)

    pl.semaphore_wait(barrier, len(partners))

    yh_peer = dev(x, (y + 2) % 4, z, c)
    sibling = peer("c", 1)
    right = peer("z", 1)
    left = peer("z", 7)

    y_outer = dev(x, 3 - y, z, c)

    def yh_copy(buf, name):
        own_block = buf.at[yh, z, c]
        return rc(own_block, own_block, name + "_yh", 0, yh_peer if name == "t" else y_outer)

    def half_copies(buf, name, s, half):
        of = yh if half == 0 else 1 - yh
        r, l = buf.at[of, zmod(z - s), c], buf.at[of, zmod(z + s), c]
        copies = []
        if s < 3 or half == 0:
            copies.append(rc(r, r, name + "_r", 2 * s + half, right))
        if s < 3 or half == 1:
            copies.append(rc(l, l, name + "_l", 2 * s + half, left))
        return copies

    def half_arrived(buf, name, s, half):
        of = yh if half == 0 else 1 - yh
        if s < 3 or half == 0:
            arrived(buf.at[of, zmod(z - 1 - s), c], name + "_r", 2 * s + half)
        if s < 3 or half == 1:
            arrived(buf.at[of, zmod(z + 1 + s), c], name + "_l", 2 * s + half)

    def ring_send(buf, name, s, half):
        for cp in half_copies(buf, name, s, half):
            cp.start()

    def ring_step(buf, name, s, half):
        half_arrived(buf, name, s, half)
        if s < 3:
            ring_send(buf, name, s + 1, half)
        if half == 1:
            for cp in sib_copies(buf, name, s + 1):
                cp.start()

    def units(s):
        if s == 0:
            return [(0, z)]
        if s == 4:
            return [(7, zmod(z + 4))]
        return [(2 * s - 1, zmod(z - s)), (2 * s, zmod(z + s))]

    def sib_copies(buf, name, s):
        return [
            rc(buf.at[:, zz, c], buf.at[:, zz, c], name + "_s", k, sibling) for k, zz in units(s)
        ]

    def sib_arrived(buf, name, s):
        for k, zz in units(s):
            arrived(buf.at[:, zz, 1 - c], name + "_s", k)

    yh_copy(h5, "t").start()
    ring_send(h5, "t", 0, 0)

    def s0_copy(j):
        return rc(s0.at[dp], s0.at[dp], "s0", j, (tp, lax.rem(dp + j, 8)))

    for j in range(1, 8):
        s0_copy(j).start()

    def turn():
        load_w.wait()

        def tile(i, carry):
            at = pl.ds(pl.multiple_of(i * 512, 512), 512)
            wt[0:SLICE, at] = w[at, :].T
            return carry

        lax.fori_loop(0, 8, tile, 0)

    def t0():
        arrived(h5.at[1 - yh, z, c], "t_yh", 0)
        ring_send(h5, "t", 0, 1)
        for cp in sib_copies(h5, "t", 0):
            cp.start()

    gain_row = sg_ref[...].astype(f32).reshape(1, D_S)

    def feat():
        for j in range(1, 8):
            arrived(s0.at[lax.rem(dp + 8 - j, 8)], "s0", j)
        for d in range(8):
            s16[2 * d : 2 * d + 2, :] = s0[d]
        wide = s16[...]
        inv16 = lax.rsqrt(jnp.sum(wide * wide, -1, keepdims=True) / D_S + epsilon)
        f5[yh, z, c] = (wide * inv16 * gain_row).astype(bf16)
        yh_copy(f5, "s").start()

    tg = tg_ref[...].astype(f32).reshape(1, 2048)

    x_right = peer("x", 1)
    x_left = peer("x", 3)
    y_pair = dev(x, yh * 2 + 1 - yl, z, c)

    def span(k, part):
        at, n = CHUNK_AT[k], CHUNK_ROWS[k]
        return {"all": pl.ds(at, n), "r": pl.ds(at, n // 2), "l": pl.ds(at + n // 2, n // 2)}[part]

    def ex_copies(k, step, which="ab"):
        every, rows_r, rows_l = span(k, "all"), span(k, "r"), span(k, "l")
        a_y = (pa.at[:, 1, every], ya.at[:, every], 0, y_pair)
        a_x1r = (pa.at[2, 0, rows_r], xa1.at[0, rows_r], 1, x_right)
        a_x1l = (pa.at[2, 0, rows_l], xa1.at[1, rows_l], 2, x_left)
        a_x2r = (pa.at[1, 0, every], xa2.at[0, every], 3, x_right)
        a_x2l = (pa.at[3, 0, every], xa2.at[1, every], 4, x_left)
        b_x1r = (pb.at[2, :, rows_r], xb1.at[0, :, rows_r], 5, x_right)
        b_x1l = (pb.at[2, :, rows_l], xb1.at[1, :, rows_l], 6, x_left)
        b_x2r = (pb.at[1, :, every], xb2.at[0, :, every], 7, x_right)
        b_x2l = (pb.at[3, :, every], xb2.at[1, :, every], 8, x_left)
        b_y = (pb.at[0, 1, every], yb.at[every], 9, y_pair)
        steps = {
            "a": ((a_y,), (a_x1r, a_x1l), (a_x2r, a_x2l)),
            "b": ((b_x1r, b_x1l), (b_x2r, b_x2l), (b_y,)),
        }
        return [
            rc(src, dst, "ex", k * 10 + i, device)
            for part in which
            for src, dst, i, device in steps[part][step]
        ]

    def ex_arrived(k, step, which="ab"):
        for cp in ex_copies(k, step, which):
            cp.wait_recv()

    def ex_send(k, step, which):
        for cp in ex_copies(k, step, which):
            cp.start()

    def b2(k):
        rows_r, rows_l = span(k, "r"), span(k, "l")
        ex_arrived(k, 0, "b")
        pb[1, :, rows_r] += xb1[0, :, rows_r]
        pb[3, :, rows_l] += xb1[1, :, rows_l]
        ex_send(k, 1, "b")

    def a2(k):
        every = span(k, "all")
        ex_arrived(k, 0, "a")
        pa[:, 0, every] += ya[:, every]
        ex_send(k, 1, "a")

    def b3(k):
        every = span(k, "all")
        ex_arrived(k, 1, "b")
        pb[0, :, every] += xb2[0, :, every] + xb2[1, :, every]
        ex_send(k, 2, "b")

    def a3(k):
        rows_r, rows_l = span(k, "r"), span(k, "l")
        ex_arrived(k, 1, "a")
        pa[1, 0, rows_r] += xa1[0, rows_r]
        pa[3, 0, rows_l] += xa1[1, rows_l]
        ex_send(k, 2, "a")

    def fin(k):
        ex_arrived(k, 2)
        for i, (_, zz) in enumerate(units(k)):
            rows = pl.ds(CHUNK_AT[k] + 32 * i, 32)
            t4[0, zz] = pa[0, 0, rows] + xa2[0, rows] + xa2[1, rows]
            t4[1, zz] = pb[0, 0, rows] + yb[rows]

    def teacher_chunk(k):
        for i, (_, zz) in enumerate(units(k)):
            for half in range(2):
                block = h5[half, zz].reshape(32, 2048).astype(f32)
                squares = block * block
                total = squares[:, 0:128]
                for lane in range(128, 2048, 128):
                    total = total + squares[:, lane : lane + 128]
                ssq[half, zz] = total
                at = CHUNK_ROWS[k] * half + 32 * i
                scaled[at : at + 32, :] = (block * tg).astype(bf16)
        m = CHUNK_ROWS[k]

        def product(xo, yo):
            d = lax.rem(x + xo, 4) * 2 + lax.rem(yl + yo, 2)
            columns = pl.ds(pl.multiple_of(d * SLICE, SLICE), SLICE)
            both = jnp.dot(scaled[0 : 2 * m, :], head[:, columns], preferred_element_type=f32)
            pa[xo, yo, CHUNK_AT[k] : CHUNK_AT[k] + m, :] = both[0:m]
            pb[xo, yo, CHUNK_AT[k] : CHUNK_AT[k] + m, :] = both[m : 2 * m]

        def other_y(xo, carry):
            product(xo, 1)
            return carry

        lax.fori_loop(0, 4, other_y, 0)
        ex_send(k, 0, "a")
        product(2, 0)
        ex_send(k, 0, "b")
        for xo in (1, 3, 0):
            product(xo, 0)

    def tchunk(k):
        if k == 0:
            load_head.wait()
        sib_arrived(h5, "t", k)
        teacher_chunk(k)

    def sstart():
        arrived(f5.at[1 - yh, z, c], "s_yh", 0)
        ring_send(f5, "s", 0, 0)
        ring_send(f5, "s", 0, 1)
        for cp in sib_copies(f5, "s", 0):
            cp.start()

    def fold(*rows):
        pieces = [v[:, 128 * i : 128 * i + 128] for v in rows for i in range(4)]
        row = lax.broadcasted_iota(jnp.int32, (8, 128), 0)
        out = jnp.zeros((8, 128), f32)
        for i, piece in enumerate(pieces):
            out = jnp.where(row == i, piece, out)
        return out

    def unfold(tile, first):
        return jnp.concatenate([tile[first + i : first + i + 1, :] for i in range(4)], axis=1)

    def sq_copy(j):
        return rc(sqs, sqr.at[j - 1], "sq", j, (tp, lax.rem(dp + j, 8)))

    wt_copy = rc(wt.at[0:SLICE], wt.at[SLICE : 2 * SLICE], "wt", 0, sibling)

    def sq():
        sqs[...] = fold(jnp.sum(ssq[...].reshape(TOKENS, 128).T, 0, keepdims=True))
        for j in range(1, 8):
            sq_copy(j).start()
        wt_copy.start()

    def slog(piece):
        blocks = []
        for s in PIECES[piece]:
            sib_arrived(f5, "s", s)
            blocks += [zz for _, zz in units(s)]
        rows = jnp.concatenate([f5[:, zz].reshape(64, D_S) for zz in blocks], axis=0)
        product = jnp.dot(rows, w[...], preferred_element_type=f32)
        for i, zz in enumerate(blocks):
            s4[0, zz] = product[64 * i : 64 * i + 32]
            s4[1, zz] = product[64 * i + 32 : 64 * i + 64]

    steps = {
        "turn": turn, "t0": t0, "feat": feat, "tchunk": tchunk, "sstart": sstart,
        "th": functools.partial(ring_step, h5, "t"), "sstep": functools.partial(ring_step, f5, "s"),
        "b2": b2, "a2": a2, "b3": b3, "a3": a3, "sq": sq, "slog": slog, "fin": fin,
    }
    for step, *where in FRONT:
        steps[step](*where)

    first = (tp * 8 + dp) * SLICE
    target_mask = ids_ref[...] == first + lax.broadcasted_iota(jnp.int32, (SLICE, TOKENS), 0)
    student = s4[...].reshape(TOKENS, SLICE).T
    s_top = jnp.max(student, 0, keepdims=True)
    s_total = jnp.sum(jnp.exp(student - s_top), 0, keepdims=True)
    target = jnp.sum(jnp.where(target_mask, student, 0.0), 0, keepdims=True)

    for j in range(1, 8):
        arrived(sqr.at[j - 1], "sq", j)
    square_total = sqs[...]
    for j in range(7):
        square_total = square_total + sqr[j]
    t_inv = unfold(lax.rsqrt(square_total / D_T + epsilon), 0)
    teacher = t4[...].reshape(TOKENS, SLICE).T * t_inv

    t_top = jnp.max(teacher, 0, keepdims=True)
    t_exp = jnp.exp(teacher - t_top)
    t_total = jnp.sum(t_exp, 0, keepdims=True)
    cross = jnp.sum(t_exp * (teacher - student), 0, keepdims=True)
    stats = (fold(t_top, s_top), fold(t_total, s_total), fold(cross, target))

    def exchange(buf, name, axis, value):
        if isinstance(value, tuple):
            for i, v in enumerate(value):
                buf[mine[axis], i] = v
        else:
            buf[mine[axis]] = value
        for j in range(1, size[axis]):
            exchange_copy(buf, name, axis, j).start()

    def exchange_copy(buf, name, axis, j):
        slot = buf.at[mine[axis]]
        return rc(slot, slot, name + "_" + axis, j, peer(axis, j))

    def exchanged(buf, name, axis):
        n = size[axis]
        for j in range(1, n):
            arrived(buf.at[lax.rem(mine[axis] + n - j, n)], name + "_" + axis, j)
        return [buf[i] for i in range(n)]

    upper = lax.broadcasted_iota(jnp.int32, (8, 128), 0) < 4

    def merged(parts):
        top = functools.reduce(jnp.maximum, [p[0] for p in parts])
        total = other = 0.0
        for p in parts:
            factor = jnp.exp(p[0] - top)
            total = total + p[1] * factor
            other = other + p[2] * jnp.where(upper, factor, 1.0)
        return top, total, other

    def front_left():
        for buf, name in ((h5, "t"), (f5, "s")):
            yh_copy(buf, name).wait_send()
            for s in range(4):
                for cp in half_copies(buf, name, s, 0) + half_copies(buf, name, s, 1):
                    cp.wait_send()
            for s in range(5):
                for cp in sib_copies(buf, name, s):
                    cp.wait_send()
        wt_copy.wait_send()

    def exchange_left():
        for j in range(1, 8):
            s0_copy(j).wait_send()
            sq_copy(j).wait_send()
        for k in range(5):
            for step in range(3):
                for cp in ex_copies(k, step):
                    cp.wait_send()

    for axis, buf in (("cx", st_cx), ("y", st_y), ("z", st_z)):
        exchange(buf, "st", axis, stats)
        if axis == "cx":
            front_left()
        if axis == "z":
            exchange_left()
        stats = merged(exchanged(buf, "st", axis))

    top, total, other = stats
    lse = top + jnp.log(total)
    t_lse, s_lse = unfold(lse, 0), unfold(lse, 4)
    cross_mean, target = unfold(other / total, 0), unfold(other, 4)
    loss_ref[...] = cross_mean - t_lse + s_lse + hard_weight * (s_lse - target)
    t_prob = jnp.exp(teacher - t_lse)
    s_prob = jnp.exp(student - s_lse)
    onehot = target_mask.astype(f32)
    g = (loss_scale * (s_prob - t_prob + hard_weight * (s_prob - onehot))).astype(bf16)

    gp[...] = jnp.dot(g, perm[...], preferred_element_type=f32).astype(bf16).T

    other_rows = pl.ds(pl.multiple_of((1 - c) * 256, 256), 256)
    own_rows = pl.ds(pl.multiple_of(c * 256, 256), 256)
    gp_copy = rc(gp.at[other_rows], gr, "gp", 0, sibling)
    gp_copy.start()
    first_own = [
        jnp.dot(gp[own_rows, :], wt[0:SLICE, at : at + 512], preferred_element_type=f32)
        for at in (ORDER[0] * WIDE, ORDER[0] * WIDE + 512)
    ]
    for axis, buf in (("cx", st_cx), ("y", st_y), ("z", st_z)):
        for j in range(1, size[axis]):
            exchange_copy(buf, "st", axis, j).wait_send()

    def shard(ch, o, part=slice(0, 4)):
        if ch < 2:
            return rs.at[ch, lax.rem(x + o, 4), part]
        return rs.at[ch, part, lax.rem(y + o, 4)]

    y_right = peer("y", 1)
    y_left = peer("y", 3)

    def q1_copies(ch):
        r, l = (x_right, x_left) if ch < 2 else (y_right, y_left)
        return (
            rc(shard(ch, 2, slice(0, 2)), q1.at[ch, 0], "q1", ch * 2, r),
            rc(shard(ch, 2, slice(2, 4)), q1.at[ch, 1], "q1", ch * 2 + 1, l),
        )

    def q2_copies(ch):
        r, l = (x_right, x_left) if ch < 2 else (y_right, y_left)
        return (
            rc(shard(ch, 1), q2.at[ch, 0], "q2", ch * 2, r),
            rc(shard(ch, 3), q2.at[ch, 1], "q2", ch * 2 + 1, l),
        )

    arrived(wt.at[SLICE : 2 * SLICE], "wt", 0)
    arrived(gr, "gp", 0)
    both_slices = jnp.concatenate([gp[own_rows, :], gr[...]], axis=1)
    for ch in ORDER:
        for tile in range(2):
            at = ch * WIDE + tile * 512
            if ch == ORDER[0]:
                product = first_own[tile] + jnp.dot(
                    gr[...], wt[SLICE : 2 * SLICE, at : at + 512], preferred_element_type=f32
                )
            else:
                product = jnp.dot(both_slices, wt[:, at : at + 512], preferred_element_type=f32)
            rs[ch, :, :, :, tile * 512 : tile * 512 + 512] = product.astype(bf16).reshape(
                4, 4, 16, 512
            )
        for cp in q1_copies(ch):
            cp.start()
    def head_tile(i, carry):
        at = pl.ds(pl.multiple_of(i * 512, 512), 512)
        features = f5[:, :, :, :, at].reshape(TOKENS, 512)
        tile = jnp.dot(g, features, preferred_element_type=f32)
        cols[pl.ds(i, 1), :] = jnp.sum(tile * wt[0:SLICE, at].astype(f32), 0, keepdims=True)
        gh[at, :] = tile.astype(bf16).T
        return carry

    lax.fori_loop(0, 4, head_tile, 0)
    for ch in ORDER:
        for cp in q1_copies(ch):
            cp.wait_recv()
        for o, part, way in ((1, slice(0, 2), 0), (3, slice(2, 4), 1)):
            ref = shard(ch, o, part)
            ref[...] = (ref[...].astype(f32) + q1[ch, way].astype(f32)).astype(bf16)
        for cp in q2_copies(ch):
            cp.start()

    def rs2_copy(ch, j):
        if ch < 2:
            return rc(s2.at[ch, lax.rem(y + j, 4)], r2.at[ch, j - 1], "rs2", ch * 4 + j, peer("y", j))
        return rc(s2.at[ch, lax.rem(x + j, 4)], r2.at[ch, j - 1], "rs2", ch * 4 + j, peer("x", j))

    lax.fori_loop(4, 8, head_tile, 0)
    store_head = pltpu.make_async_copy(gh, ghead_hbm, ssem.at[BASE["load"] + 2])
    store_head.start()
    exchange(ga_z, "ga", "z", cols[...])
    for ch in ORDER:
        for cp in q2_copies(ch):
            cp.wait_recv()
        kept = shard(ch, 0)[...].astype(f32)
        total = kept + (q2[ch, 0].astype(f32) + q2[ch, 1].astype(f32))
        s2[ch] = total.astype(bf16)
        for j in range(1, 4):
            rs2_copy(ch, j).start()

    gain = functools.reduce(jnp.add, exchanged(ga_z, "ga", "z"))
    exchange(ga_cx, "ga", "cx", gain)

    for ch in ORDER:
        for j in range(1, 4):
            arrived(r2.at[ch, j - 1], "rs2", ch * 4 + j)
        kept = s2[ch, y] if ch < 2 else s2[ch, x]
        total = kept.astype(f32)
        for j in range(3):
            total = total + r2[ch, j].astype(f32)
        for zz in range(8):
            for half in range(2):
                at = 4 * ch + 2 * half
                zf[zz, at : at + 2, :] = total[2 * zz : 2 * zz + 2, 512 * half : 512 * half + 512]
    zb[...] = zf[...].astype(bf16)

    def rs3_copy(j):
        return rc(zb.at[lax.rem(z + j, 8)], r3.at[j - 1], "rs3", j, peer("z", j))

    for j in range(1, 8):
        rs3_copy(j).start()

    gain = functools.reduce(jnp.add, exchanged(ga_cx, "ga", "cx"))
    exchange(ga_y, "ga", "y", gain)

    def gains_left(*axes):
        for axis, buf in (("cx", ga_cx), ("y", ga_y), ("z", ga_z)):
            if axis in axes:
                for j in range(1, size[axis]):
                    exchange_copy(buf, "ga", axis, j).wait_send()

    gains_left("z", "cx")
    gp_copy.wait_send()
    for ch in range(4):
        for cp in q1_copies(ch) + q2_copies(ch):
            cp.wait_send()
        for j in range(1, 4):
            rs2_copy(ch, j).wait_send()

    own_wide = sh_ref[...].astype(f32)
    own_inv = lax.rsqrt(jnp.sum(own_wide * own_wide, -1, keepdims=True) / D_S + epsilon)
    own_normed = own_wide * own_inv
    for j in range(1, 8):
        arrived(r3.at[j - 1], "rs3", j)
    folded = zf[z]
    for j in range(7):
        folded = folded + r3[j].astype(f32)
    for i in range(8):
        unfolded[:, 512 * i : 512 * i + 512] = folded[2 * i : 2 * i + 2, :]
    grad_normed = unfolded[...] * gain_row
    inner = jnp.sum(grad_normed * own_normed, -1, keepdims=True) / D_S
    ghid_ref[...] = own_inv * (grad_normed - own_normed * inner)

    gain = functools.reduce(jnp.add, exchanged(ga_y, "ga", "y"))
    row = lax.broadcasted_iota(jnp.int32, (8, 512), 0)
    gain_rows = jnp.ones((8, 512), f32)
    for i in range(8):
        gain_rows = jnp.where(row == i, gain_row[:, 512 * i : 512 * i + 512], gain_rows)
    ggain_ref[...] = gain / gain_rows

    gains_left("y")
    for j in range(1, 8):
        rs3_copy(j).wait_send()
    store_head.wait()


def finish(loss_ref, hidden_ref, gain_ref, head_ref, loss_out, hidden_out, gain_out, head_out):
    head_out[...] = head_ref[...]

    @pl.when(pl.program_id(0) == 0)
    def _():
        loss_out[...] = loss_ref[...]
        hidden_out[...] = hidden_ref[...].astype(bf16)
        for i in range(8):
            gain_out[:, 512 * i : 512 * i + 512] = gain_ref[i : i + 1, :]


def shards(
    teacher_hidden,
    teacher_gain,
    teacher_head,
    student_hidden,
    student_gain,
    student_head,
    token_ids,
):
    vmem = pl.BlockSpec(memory_space=pltpu.VMEM)
    hbm = pl.BlockSpec(memory_space=pl.ANY)
    block = pl.BlockSpec((2048, SLICE), lambda i: (i, 0))

    def whole(*shape):
        return pl.BlockSpec(shape, lambda i: (0, 0))

    row8 = (8, TOKENS)
    scratch = [
        ((2048, 2048), bf16), ((D_S, SLICE), bf16), ((2 * SLICE, D_S), bf16), ((2, 8, 2, 16, 2048), bf16),
        ((128, 2048), bf16), ((4, 2, 256, SLICE), f32), ((4, 2, 256, SLICE), f32),
        ((4, 256, SLICE), f32), ((2, 256, SLICE), f32), ((2, 256, SLICE), f32),
        ((2, 2, 256, SLICE), f32), ((2, 2, 256, SLICE), f32), ((256, SLICE), f32),
        ((2, 8, 32, 128), f32), ((8, 128), f32), ((7, 8, 128), f32),
        ((8, 2, D_S), f32), ((16, D_S), f32), ((2, 8, 2, 16, D_S), bf16),
        ((2, 8, 32, SLICE), f32), ((2, 8, 32, SLICE), f32), ((8, 512), f32),
        ((8, 3, 8, 128), f32), ((4, 3, 8, 128), f32), ((8, 3, 8, 128), f32),
        ((8,) + row8, f32), ((4,) + row8, f32), ((8,) + row8, f32),
        ((TOKENS, SLICE), bf16), ((256, SLICE), bf16), ((TOKENS, TOKENS), bf16), ((D_S, SLICE), bf16),
        ((4, 4, 4, 16, WIDE), bf16), ((4, 2, 2, 16, WIDE), bf16), ((4, 2, 4, 16, WIDE), bf16),
        ((4, 4, 16, WIDE), bf16), ((4, 3, 16, WIDE), bf16),
        ((8, 16, 512), f32), ((8, 16, 512), bf16), ((7, 16, 512), bf16), ((2, D_S), f32),
    ]
    loss, grad_head, grad_hidden, grad_gain = pl.pallas_call(
        kernel,
        out_shape=(
            jax.ShapeDtypeStruct((1, TOKENS), f32),
            jax.ShapeDtypeStruct((D_S, SLICE), bf16),
            jax.ShapeDtypeStruct((2, D_S), f32),
            jax.ShapeDtypeStruct((8, 512), f32),
        ),
        in_specs=[vmem, vmem, hbm, vmem, vmem, hbm, vmem],
        out_specs=(vmem, hbm, vmem, vmem),
        scratch_shapes=[pltpu.VMEM(shape, dtype) for shape, dtype in scratch]
        + [pltpu.SemaphoreType.DMA((N_SEMS,)), pltpu.SemaphoreType.DMA((N_SEMS,))],
        compiler_params=pltpu.CompilerParams(
            collective_id=0, has_side_effects=True, vmem_limit_bytes=56 * 1024 * 1024
        ),
        cost_estimate=pl.CostEstimate(
            flops=7_600_000_000, bytes_accessed=13_000_000, transcendentals=600_000
        ),
    )(
        teacher_hidden,
        teacher_gain,
        teacher_head,
        student_hidden,
        student_gain,
        student_head,
        token_ids.reshape(1, TOKENS),
    )
    loss, grad_hidden, grad_gain, grad_head = pl.pallas_call(
        finish,
        out_shape=(
            jax.ShapeDtypeStruct((1, TOKENS), f32),
            jax.ShapeDtypeStruct((2, D_S), bf16),
            jax.ShapeDtypeStruct((1, D_S), f32),
            jax.ShapeDtypeStruct((D_S, SLICE), bf16),
        ),
        grid=(2,),
        in_specs=[whole(1, TOKENS), whole(2, D_S), whole(8, 512), block],
        out_specs=(whole(1, TOKENS), whole(2, D_S), whole(1, D_S), block),
        compiler_params=pltpu.CompilerParams(vmem_limit_bytes=56 * 1024 * 1024),
    )(loss, grad_hidden, grad_gain, grad_head)
    return loss.reshape(TOKENS), grad_hidden, grad_gain.reshape(D_S), grad_head


def solution(mesh):
    in_specs = (
        P("tp", "dp"),
        P("dp"),
        P("dp", "tp"),
        P(("tp", "dp"), None),
        P(),
        P(None, ("tp", "dp")),
        P(),
    )
    out_specs = (P(), P(("tp", "dp"), None), P(), P(None, ("tp", "dp")))
    return jax.shard_map(shards, mesh=mesh, in_specs=in_specs, out_specs=out_specs, check_vma=False)
```
